32 devices in a mesh: dp: 8 (over z, x), tensor: 4 (over y, core).
Axes of the slice: x: 2, y: 2, z: 4, core: 2. Of those that a mesh axis runs over, the one named last changes fastest.
Arguments:
- tokens: bfloat16 [8, 1024, 768], P('dp', 'tensor'), may hold values from -6 to 6
- segment_ids: int32 [8, 1024], P('dp'), may hold values from 0 to 2, as said below
- mix_norm_gain: float32 [768], replicated, may hold values from 0.5 to 1.5
- mix_norm_bias: float32 [768], replicated, may hold values from -3 to 3
- in_weight: bfloat16 [768, 3, 768], P('dp', None, 'tensor'), may hold values from -0.21875 to 0.21875
- in_bias: float32 [3, 768], P(None, 'tensor'), may hold values from -3 to 3
- short_weight: float32 [3, 3, 768], P(None, None, 'tensor'), may hold values from -3.5 to 3.5
- short_bias: float32 [3, 768], P(None, 'tensor'), may hold values from -3 to 3
- filt_in_weight: float32 [33, 64], replicated, may hold values from -1 to 1
- filt_in_bias: float32 [64], replicated, may hold values from -4 to 4
- filt_mid_weight: float32 [64, 64], replicated, may hold values from -0.75 to 0.75
- filt_mid_bias: float32 [64], replicated, may hold values from -4 to 4
- filt_out_weight: float32 [64, 2, 768], P(None, None, 'tensor'), may hold values from -0.125 to 0.125
- decay_rates: float32 [2, 768], P(None, 'tensor'), may hold values from 0.0005 to 0.15
- long_bias: float32 [2, 768], P(None, 'tensor'), may hold values from -4 to 4
- out_weight: bfloat16 [768, 768], P('dp', 'tensor'), may hold values from -0.21875 to 0.21875
- out_bias: float32 [768], replicated, may hold values from -3 to 3
- mlp_norm_gain: float32 [768], replicated, may hold values from 0.5 to 1.5
- mlp_norm_bias: float32 [768], replicated, may hold values from -3 to 3
- up_weight: bfloat16 [768, 3072], P('dp', 'tensor'), may hold values from -0.21875 to 0.21875
- up_bias: float32 [3072], P('tensor'), may hold values from -3 to 3
- down_weight: bfloat16 [768, 3072], P('dp', 'tensor'), may hold values from -0.109375 to 0.109375
- down_bias: float32 [768], replicated, may hold values from -3 to 3
- cotangent: bfloat16 [8, 1024, 768], P('dp', 'tensor'), may hold values from -6 to 6
Outputs:
- output: bfloat16 [8, 1024, 768], P('dp', 'tensor')
- grad_tokens: bfloat16 [8, 1024, 768], P('dp', 'tensor')
- grad_mix_norm_gain: float32 [768], replicated
- grad_mix_norm_bias: float32 [768], replicated
- grad_in_weight: float32 [768, 3, 768], P('dp', None, 'tensor')
- grad_in_bias: float32 [3, 768], P(None, 'tensor')
- grad_short_weight: float32 [3, 3, 768], P(None, None, 'tensor')
- grad_short_bias: float32 [3, 768], P(None, 'tensor')
- grad_filt_in_weight: float32 [33, 64], replicated
- grad_filt_in_bias: float32 [64], replicated
- grad_filt_mid_weight: float32 [64, 64], replicated
- grad_filt_mid_bias: float32 [64], replicated
- grad_filt_out_weight: float32 [64, 2, 768], P(None, None, 'tensor')
- grad_long_bias: float32 [2, 768], P(None, 'tensor')
- grad_out_weight: float32 [768, 768], P('dp', 'tensor')
- grad_out_bias: float32 [768], replicated
- grad_mlp_norm_gain: float32 [768], replicated
- grad_mlp_norm_bias: float32 [768], replicated
- grad_up_weight: float32 [768, 3072], P('dp', 'tensor')
- grad_up_bias: float32 [3072], P('tensor')
- grad_down_weight: float32 [768, 3072], P('dp', 'tensor')
- grad_down_bias: float32 [768], replicated
The draws below stay inside these ranges and needn't reach their ends.
Inputs may be any that keep to these rules, and one draw needn't show every extreme that they name: `segment_ids`: ids never fall along a sequence and every sequence holds all 3 documents: document 0 covers the first 1 to 64 positions, document 2 the last 1 to 64, document 1 all positions between.
All inputs are finite; a program needn't handle non-finite values.
Results may differ from the reference program's by a relative error of at most 0.0055.
The reference program's roundings to bfloat16 on the way count: a program that leaves them out, or rounds other values in their place, can miss the bound.
Values may be sent and summed in bfloat16 or wider, within the bound.
A program may use at most 256 MiB of HBM per device.

```python
import math
import jax
import jax.numpy as jnp
from jax import lax

D = 768
F = 3072
EMB = 33
FH = 64
SHORT = 3
SEQ_LEN = 1024
DOCS = 3
SEQS = 8


def draw_segment_ids(key, part):
    first_key, second_key = jax.random.split(jax.random.fold_in(key, 7))
    edge_span = SEQ_LEN // 16
    first_start = jax.random.randint(first_key, (SEQS, 1), 1, edge_span + 1)
    last_start = jax.random.randint(second_key, (SEQS, 1), SEQ_LEN - edge_span, SEQ_LEN)
    places = jnp.arange(SEQ_LEN, dtype=jnp.int32)[None, :]
    return (places >= first_start).astype(jnp.int32) + (places >= last_start).astype(jnp.int32)


def spiked(entries, key, source, target, blocks, factor):
    def block_of(axis_at):
        return (jnp.arange(entries.shape[axis_at]) // (entries.shape[axis_at] // blocks)).reshape((-1,) + (1,) * (entries.ndim - 1 - axis_at))

    first = jax.random.permutation(key, blocks)[block_of(target)]
    other_side = (block_of(target) + blocks // 2) % blocks
    return jnp.where((block_of(source) == first) | (block_of(source) == other_side), factor * entries, entries)


def steps_of(rng, extent, cuts, low, largest):
    loudness, own = 1.0, jax.random.fold_in(rng, 6)
    for axis_at, blocks in cuts:
        heights = jnp.exp(jax.random.uniform(jax.random.fold_in(own, axis_at), (blocks,), jnp.float32, low / len(cuts), largest / len(cuts)))
        loudness = loudness * jnp.repeat(heights, extent[axis_at] // blocks).reshape([-1 if axis == axis_at else 1 for axis in range(len(extent))])
    return loudness


def noise(own_key, dims, scale, most, cuts=(), kind=jnp.bfloat16):
    values = scale * jax.random.normal(own_key, dims, jnp.float32)
    if cuts:
        values = values * steps_of(own_key, dims, cuts, -0.22, 0.18)
    return jnp.clip(values, -most, most).astype(kind)


def heavy_noise(rng, shape, scale, reach, cuts, heavy, kind=jnp.bfloat16):
    entries = scale * jax.random.normal(rng, shape, jnp.float32)
    if cuts:
        entries = entries * steps_of(rng, shape, cuts, -0.22, 0.18)
    return jnp.clip(spiked(entries, jax.random.fold_in(rng, 3), *heavy), -reach, reach).astype(kind)


def setup_inputs(seed: int = 0) -> dict:
    seeds = jax.random.split(jax.random.key(seed), 25)
    return {
        "tokens": noise(seeds[0], (SEQS, SEQ_LEN, D), 1.0, 6.0, ((0, 8), (1, 4))),
        "segment_ids": draw_segment_ids(jax.random.fold_in(seeds[24], 71), 0),
        "mix_norm_gain": jnp.clip(1.0 + 0.1 * jax.random.normal(seeds[2], (D,), jnp.float32), 0.5, 1.5),
        "mix_norm_bias": noise(seeds[3], (D,), 0.3, 3.0, (), jnp.float32),
        "in_weight": noise(seeds[4], (D, 3, D), D ** -0.5, 0.21875, ((0, 8), (2, 4))),
        "in_bias": noise(seeds[5], (3, D), 0.3, 3.0, ((1, 4),), jnp.float32),
        "short_weight": noise(seeds[6], (SHORT, 3, D), SHORT ** -0.5, 3.5, ((2, 4),), jnp.float32),
        "short_bias": noise(seeds[7], (3, D), 0.3, 3.0, ((1, 4),), jnp.float32),
        "filt_in_weight": noise(seeds[8], (EMB, FH), EMB ** -0.5, 1.0, (), jnp.float32),
        "filt_in_bias": noise(seeds[9], (FH,), 1.0, 4.0, (), jnp.float32),
        "filt_mid_weight": noise(seeds[10], (FH, FH), FH ** -0.5, 0.75, (), jnp.float32),
        "filt_mid_bias": noise(seeds[11], (FH,), 1.0, 4.0, (), jnp.float32),
        "filt_out_weight": noise(seeds[12], (FH, 2, D), (FH * SEQ_LEN // 32) ** -0.5, 0.125, ((2, 4),), jnp.float32),
        "decay_rates": jnp.clip(jnp.exp(math.log(0.15) - 5.7037825 * jax.random.uniform(seeds[13], (2, D), jnp.float32) ** steps_of(seeds[13], (2, D), ((1, 4),), -0.2, 0.2)), 0.0005, 0.15),
        "long_bias": noise(seeds[14], (2, D), 1.0, 4.0, ((1, 4),), jnp.float32),
        "out_weight": noise(seeds[15], (D, D), D ** -0.5, 0.21875, ((0, 8), (1, 4))),
        "out_bias": noise(seeds[16], (D,), 0.3, 3.0, (), jnp.float32),
        "mlp_norm_gain": jnp.clip(1.0 + 0.1 * jax.random.normal(seeds[17], (D,), jnp.float32), 0.5, 1.5),
        "mlp_norm_bias": noise(seeds[18], (D,), 0.3, 3.0, (), jnp.float32),
        "up_weight": noise(seeds[19], (D, F), D ** -0.5, 0.21875, ((0, 8), (1, 4))),
        "up_bias": noise(seeds[20], (F,), 0.3, 3.0, ((0, 4),), jnp.float32),
        "down_weight": noise(seeds[21], (D, F), F ** -0.5, 0.109375, ((0, 8), (1, 4))),
        "down_bias": noise(seeds[22], (D,), 0.3, 3.0, (), jnp.float32),
        "cotangent": heavy_noise(seeds[23], (SEQS, SEQ_LEN, D), 1.0, 6.0, ((0, 8), (1, 4)), (0, 2, 8, 2.0)),
    }


EPSILON = 1e-05
HIGHEST = lax.Precision.HIGHEST

@jax.custom_vjp
def low(v):
    return lax.optimization_barrier(v.astype(jnp.bfloat16)).astype(jnp.float32)

@jax.custom_vjp
def low_back(v):
    return v

def low_keep(v):
    return (low(v), None)

def low_pass(kept, grad):
    return (grad,)

def back_keep(v):
    return (v, None)

def back_low(kept, grad):
    return (low(grad),)
low.defvjp(low_keep, low_pass)
low_back.defvjp(back_keep, back_low)

def layer_norm(values, norm_gain, norm_shift):
    center = lax.optimization_barrier(jnp.mean(values, axis=-1, keepdims=True))
    centred = values - center
    spread = lax.optimization_barrier(jnp.mean(centred * centred, axis=-1, keepdims=True))
    return centred * lax.rsqrt(spread + EPSILON) * norm_gain + norm_shift

def position_table(length, emb_width):
    band_count = (emb_width - 1) // 2
    places = jnp.arange(length, dtype=jnp.float32)
    angles = 2.0 * math.pi * places / length
    frequency = jnp.linspace(0.0001, band_count - 1, band_count, dtype=jnp.float32)
    phases = angles[:, None] * frequency[None, :]
    return jnp.concatenate([(places / (length - 1))[:, None], jnp.cos(phases), -jnp.sin(phases)], axis=1)

def make_filter(table, first_weight, first_bias, middle_weight, middle_bias, last_weight, rates):
    hidden = jnp.sin(jnp.dot(table, first_weight, precision=HIGHEST) + first_bias)
    hidden = jnp.sin(jnp.dot(hidden, middle_weight, precision=HIGHEST) + middle_bias)
    raw_filter = jnp.einsum('tk,koc->toc', hidden, last_weight, precision=HIGHEST)
    places = jnp.arange(table.shape[0], dtype=jnp.float32)
    return raw_filter * jnp.exp(-places[:, None, None] * rates[None])

def short_conv(values, doc_ids, taps, tap_bias):
    running = tap_bias[None] + taps[0][None] * values
    for offset in range(1, taps.shape[0]):
        shifted = jnp.concatenate([jnp.zeros_like(values[:offset]), values[:-offset]], axis=0)
        same_doc = jnp.concatenate([jnp.zeros((offset,), jnp.float32), (doc_ids[offset:] == doc_ids[:-offset]).astype(jnp.float32)])
        running = running + taps[offset][None] * shifted * same_doc[:, None, None]
    return running

def long_conv(signal, filt_one, direct, doc_masks):
    length = signal.shape[0]
    size_all = 2 * length
    pieces = doc_masks[:, :, None] * signal[:, None, :]
    spectrum = jnp.fft.rfft(pieces, n=size_all, axis=0)
    filt_spec = jnp.fft.rfft(filt_one, n=size_all, axis=0)
    result = jnp.fft.irfft(spectrum * filt_spec[:, None, :], n=size_all, axis=0)[:length]
    return lax.optimization_barrier(jnp.sum(doc_masks[:, :, None] * result, axis=1)) + direct * signal

def reference(tokens, segment_ids, mix_norm_gain, mix_norm_bias, in_weight, in_bias, short_weight, short_bias, filt_in_weight, filt_in_bias, filt_mid_weight, filt_mid_bias, filt_out_weight, decay_rates, long_bias, out_weight, out_bias, mlp_norm_gain, mlp_norm_bias, up_weight, up_bias, down_weight, down_bias, cotangent):
    params = (mix_norm_gain, mix_norm_bias, in_weight.astype(jnp.float32), in_bias, short_weight, short_bias, filt_in_weight, filt_in_bias, filt_mid_weight, filt_mid_bias, filt_out_weight, long_bias, out_weight.astype(jnp.float32), out_bias, mlp_norm_gain, mlp_norm_bias, up_weight.astype(jnp.float32), up_bias, down_weight.astype(jnp.float32), down_bias)
    inputs = tokens.astype(jnp.float32)
    all_masks = (segment_ids[:, :, None] == jnp.arange(DOCS, dtype=jnp.int32)[None, None, :]).astype(jnp.float32)

    def forward(inputs, params):
        norm_gain1, norm_bias1, w_input, b_input, s_weight, s_bias, f_first, f_first_b, f_mid, f_mid_b, f_last, l_bias, w_output, b_output, norm_gain2, norm_bias2, w_upper, b_upper, w_lower, b_lower = params
        table = position_table(SEQ_LEN, EMB)
        filters = make_filter(table, f_first, f_first_b, f_mid, f_mid_b, f_last, decay_rates)

        def one_sequence(packed):
            seq_in, doc_masks, doc_ids = packed
            norm_one = low(layer_norm(seq_in, norm_gain1, norm_bias1))
            zpre = jnp.dot(norm_one, w_input.reshape(D, 3 * D), precision=HIGHEST).reshape(SEQ_LEN, 3, D)
            zpre = low_back(zpre + b_input)
            short = short_conv(zpre, doc_ids, s_weight, s_bias)
            first = short[:, 1] * long_conv(short[:, 0], filters[:, 0], l_bias[0], doc_masks)
            gated = low(short[:, 2] * long_conv(first, filters[:, 1], l_bias[1], doc_masks))
            mixed = low_back(jnp.dot(gated, w_output.T, precision=HIGHEST))
            mixed_sum = seq_in + mixed + b_output
            norm_two = low(layer_norm(mixed_sum, norm_gain2, norm_bias2))
            pre_act = low_back(jnp.dot(norm_two, w_upper, precision=HIGHEST) + b_upper)
            act = low(jax.nn.gelu(pre_act, approximate=True))
            return mixed_sum + jnp.dot(act, w_lower.T, precision=HIGHEST) + b_lower
        return lax.map(jax.checkpoint(one_sequence), (inputs, all_masks, segment_ids))
    result, backward = jax.vjp(forward, inputs, params)
    grad_inputs, grads = backward(cotangent.astype(jnp.float32))
    return (result.astype(jnp.bfloat16), grad_inputs.astype(jnp.bfloat16), grads[0], grads[1], grads[2], grads[3], grads[4], grads[5], grads[6], grads[7], grads[8], grads[9], grads[10], grads[11], grads[12], grads[13], grads[14], grads[15], grads[16], grads[17], grads[18], grads[19])
```

```python
import functools
import math

import jax
import jax.numpy as jnp
import numpy as np
from jax import lax
from jax.experimental import pallas as pl
from jax.experimental.pallas import tpu as pltpu
from jax.sharding import PartitionSpec as P

DOCS = 3
EPSILON = 1e-05
HIGHEST = lax.Precision.HIGHEST
ROW_CONTRACT = (((1,), (1,)), ((), ()))
COLUMN_CONTRACT = (((0,), (0,)), ((), ()))
F32, BF16 = jnp.float32, jnp.bfloat16
CHUNK = 64
VMEM_LIMIT = 58 * 2**20


def half_table(count, period):
    turns = ((2 * np.arange(count)[:, None] + 1) * np.arange(count)[None, :]) % (2 * period)
    angle = turns * (math.pi / period)
    return np.cos(angle), -np.sin(angle)


def three_pass(table):
    high = table.astype(np.float32).astype(jnp.bfloat16)
    low = (table.astype(np.float32) - high.astype(np.float32)).astype(jnp.bfloat16)
    return np.concatenate([high, high, low], axis=1)


def wave_tables(length):
    half, edge = length // 2, length // 32
    real, imag = half_table(half, length)
    whole = np.concatenate([real, imag], axis=0)
    e_real, e_imag = half_table(edge, 2 * edge)
    zero = np.zeros_like(e_real)
    both = np.block([[e_real, zero], [zero, e_real], [e_imag, zero], [zero, e_imag]])
    step = (2 * np.arange(half) + 1) * (math.pi / length)
    e_step = np.tile((2 * np.arange(edge) + 1) * (math.pi / (2 * edge)), 2)
    twist = np.stack([np.cos(step), -np.sin(step)], axis=1).astype(np.float32)
    e_twist = np.stack([np.cos(e_step), -np.sin(e_step)], axis=1).astype(np.float32)
    return (
        three_pass(whole), three_pass(whole.T), twist,
        three_pass(both), three_pass(both.T), e_twist,
    )


def position_table(length, emb_width):
    bands = (emb_width - 1) // 2
    places = np.arange(length, dtype=np.float32)
    angles = (2.0 * math.pi * places / length).astype(np.float32)
    frequency = np.linspace(0.0001, bands - 1, bands, dtype=np.float32)
    phases = (angles[:, None] * frequency[None, :]).astype(np.float64)
    table = np.concatenate([(places / (length - 1))[:, None], np.cos(phases), -np.sin(phases)], axis=1)
    return by_parity(table.astype(np.float32))


def by_parity(rows):
    return rows.reshape((rows.shape[0] // 2, 2) + rows.shape[1:]).swapaxes(0, 1)


def in_order(halves):
    return halves.swapaxes(0, 1).reshape((-1,) + halves.shape[2:])


def over_rows(rows, step, work):
    @pl.loop(0, rows // step)
    def _(i):
        work(pl.ds(pl.multiple_of(i * step, step), step))


def parts(x):
    high = x.astype(BF16)
    return high, (x - high.astype(F32)).astype(BF16)


def put_parts(rhs, at, base, block, x):
    high, low = parts(x)
    size = x.shape[0]
    start = at.start if isinstance(at, pl.Slice) else at
    for slot, piece in ((0, high), (1, low), (2, high)):
        rhs[pl.ds(pl.multiple_of(start + (base + slot * block), 16), size), :] = piece


def mul(ar, ai, br, bi):
    return ar * br - ai * bi, ar * bi + ai * br


def mul_conj(ar, ai, br, bi):
    return ar * br + ai * bi, ar * bi - ai * br


def blend(f, x, conj):
    (fe, fo, ft), (xe, xo) = f, x
    m = mul_conj if conj else mul
    if conj:
        a, b = m(*fe, *xe), m(*fo, *xo)
        c, d = m(*fe, *xo), m(*ft, *xe)
    else:
        a, b = m(*fe, *xe), m(*ft, *xo)
        c, d = m(*fe, *xo), m(*fo, *xe)
    return (a[0] + b[0], a[1] + b[1]), (c[0] + d[0], c[1] + d[1])


def dot(a, b):
    return jnp.dot(a, b, preferred_element_type=F32)


def fine_dot(a, b, dims=(((1,), (0,)), ((), ()))):
    return lax.dot_general(a, b, dims, precision=HIGHEST, preferred_element_type=F32)


def analyse(tabs, rhs, source, spec, edge_spec, masks):
    wave, _, _, e_wave, _, _ = tabs
    half, edge = wave.shape[1] // 3, e_wave.shape[1] // 6

    @pl.loop(0, 2)
    def _(par):
        def fill(at):
            put_parts(rhs, at, 0, half, source(par, at) * masks[par, at, 0:1])

        over_rows(half, CHUNK, fill)
        spec[par] = dot(wave[...], rhs[0 : 3 * half, :])
        first, last = pl.ds(0, edge), pl.ds(half - edge, edge)
        window = jnp.concatenate(
            [source(par, first) * masks[par, first, 1:2], source(par, last) * masks[par, last, 2:3]], axis=0
        )
        high, low = parts(window)
        edge_spec[par] = dot(e_wave[...], jnp.concatenate([high, low, high], axis=0))


def pair(ref, index, at, half):
    start = at.start
    return ref[index, at, :], ref[index, pl.ds(pl.multiple_of(start + half, 8), at.size), :]


def spectra_product(tabs, filt, e_filt, spec, e_spec, rhs_even, rhs_odd, conj, turn):
    _, wave_back, twist, _, e_back, e_twist = tabs
    half, edge2 = wave_back.shape[1] // 6, e_back.shape[1] // 6

    def get(f, tw, at, n):
        fe, fo = pair(f, 0, at, n), pair(f, 1, at, n)
        ft = mul(*fo, tw[at, 0:1], tw[at, 1:2]) if turn else pair(f, 2, at, n)
        return fe, fo, ft

    def work(at):
        even, odd = blend(get(filt, twist, at, half), (pair(spec, 0, at, half), pair(spec, 1, at, half)), conj)
        for rhs, (real, imag) in ((rhs_even, even), (rhs_odd, odd)):
            put_parts(rhs, at, 0, 2 * half, real)
            put_parts(rhs, at, half, 2 * half, imag)

    over_rows(half, CHUNK // 2, work)
    at = pl.ds(0, edge2)
    even, odd = blend(get(e_filt, e_twist, at, edge2), (pair(e_spec, 0, at, edge2), pair(e_spec, 1, at, edge2)), conj)
    out = []
    for real, imag in (even, odd):
        high, low = parts(jnp.concatenate([real, imag], axis=0))
        out.append(dot(e_back[...], jnp.concatenate([high, low, high], axis=0)))
    return out


def synthesise(tabs, rhs, out, par):
    out[par, 0 : tabs[1].shape[0], :] = dot(tabs[1][...], rhs[...])


def join(out, edges, direct, source, masks, half):
    for par in range(2):
        def work(at, par=par):
            out[par, at, :] = out[par, at, :] * masks[par, at, 0:1] + direct * source(par, at)

        over_rows(half, CHUNK, work)
        edge = edges[par].shape[0] // 2
        first, last = pl.ds(0, edge), pl.ds(half - edge, edge)
        out[par, first, :] += edges[par][:edge] * masks[par, first, 1:2]
        out[par, last, :] += edges[par][edge:] * masks[par, last, 2:3]


def hidden_layers(table, w1, b1, w2, b2):
    pre1 = fine_dot(table, w1) + b1
    h1 = jnp.sin(pre1)
    pre2 = fine_dot(h1, w2) + b2
    return pre1, h1, pre2


def decay_at(par, rows, start, rates):
    m = lax.broadcasted_iota(jnp.int32, (rows, rates.shape[1]), 0) + start
    return jnp.exp((2 * m + par).astype(F32) * -rates)


def make_filters(tabs, rhs, ptable, w1, b1, w2, b2, w3, rates, hidden, filt, filt_spec, e_filt_spec, par):
    wave, _, _, e_wave, _, _ = tabs
    half, edge = wave.shape[1] // 3, e_wave.shape[1] // 6
    _, _, pre2 = hidden_layers(ptable[par], w1[...], b1[...], w2[...], b2[...])
    hidden[par] = jnp.sin(pre2)

    @pl.loop(0, 2)
    def _(o):
        filt[...] = fine_dot(hidden[par], w3[o])

        def fill(at):
            put_parts(rhs, at, 0, half, filt[at, :] * decay_at(par, CHUNK, at.start, rates[pl.ds(o, 1), :]))

        over_rows(half, CHUNK, fill)
        filt_spec[o, par] = dot(wave[...], rhs[0 : 3 * half, :]) * (1.0 / half)
        window = filt[pl.ds(0, edge), :] * decay_at(par, edge, 0, rates[pl.ds(o, 1), :])
        high, low = parts(jnp.concatenate([window, window], axis=0))
        e_filt_spec[o, par] = dot(e_wave[...], jnp.concatenate([high, low, high], axis=0)) * (1.0 / edge)


def turn_filters(tabs, filt_spec, e_filt_spec):
    wave, _, twist, e_wave, _, e_twist = tabs
    half, edge = wave.shape[1] // 3, e_wave.shape[1] // 6
    for o in range(2):
        def turn(at, o=o):
            real, imag = mul(*pair(filt_spec.at[o], 1, at, half), twist[at, 0:1], twist[at, 1:2])
            filt_spec[o, 2, at, :] = real
            filt_spec[o, 2, pl.ds(pl.multiple_of(at.start + half, 8), at.size), :] = imag

        over_rows(half, CHUNK, turn)
        n = 2 * edge
        real, imag = mul(*pair(e_filt_spec.at[o], 1, pl.ds(0, n), n), e_twist[:, 0:1], e_twist[:, 1:2])
        e_filt_spec[o, 2] = jnp.concatenate([real, imag], axis=0)


PAD = 8


def short_rows(z, which, par, at, masks, taps, tap_bias):
    size, start = at.size, at.start
    here = z[which, par, pl.ds(pl.multiple_of(start + PAD, 8), size), :]
    wide = pl.ds(pl.multiple_of(start, 8), size + PAD)
    same_before = z[which, par, wide, :][PAD - 1 : PAD - 1 + size]
    if par == 0:
        other = z[which, 1, wide, :][PAD - 1 : PAD - 1 + size]
    else:
        other = z[which, 0, pl.ds(pl.multiple_of(start + PAD, 8), size), :]
    one, two = masks[par, at, 3:4] * other, masks[par, at, 4:5] * same_before
    tap = lambda j: taps[j, which : which + 1, :]
    return tap_bias[which : which + 1, :] + tap(0) * here + tap(1) * one + tap(2) * two, here, one, two


def put_zpre(z, normed, weights, in_bias, which, par, half):
    zero = jnp.zeros((PAD, z.shape[3]), F32)
    z[which, par, 0:PAD, :] = zero
    z[which, par, PAD + half : PAD + half + PAD, :] = zero
    z[which, par, PAD : PAD + half, :] = dot(normed, weights) + in_bias[which : which + 1, :]


def make_short(short, z, masks, taps, tap_bias, half):
    for par in range(2):
        def work(at, par=par):
            for which in range(3):
                short[which, par, at, :] = short_rows(z, which, par, at, masks, taps, tap_bias)[0]

        over_rows(half, CHUNK, work)


def layer_norm_parts(values):
    center = jnp.mean(values, axis=-1, keepdims=True)
    centred = values - center
    spread = jnp.mean(centred * centred, axis=-1, keepdims=True)
    scale = lax.rsqrt(spread + EPSILON)
    return centred * scale, scale


def parity_matrix(rows):
    half = rows // 2
    at = lax.broadcasted_iota(jnp.int32, (rows, rows), 0)
    wanted = jnp.where(at < half, 2 * at, 2 * (at - half) + 1)
    return (lax.broadcasted_iota(jnp.int32, (rows, rows), 1) == wanted).astype(F32).astype(BF16)


def make_masks(masks, segments, half):
    seg = segments[...].astype(F32)
    length = seg.shape[1]
    place = lax.broadcasted_iota(jnp.int32, (1, length), 1)
    one = lambda ok: jnp.where(ok, 1.0, 0.0)
    rows = [one(seg == 1.0), one(seg == 0.0), one(seg == 2.0)]
    for j in (1, 2):
        rows.append(jnp.where(place >= j, one(pltpu.roll(seg, j, 1) == seg), 0.0))
    marks = jnp.concatenate(rows + [jnp.zeros((3, length), F32)], axis=0).astype(BF16)
    at = lax.broadcasted_iota(jnp.int32, (half, length), 0)
    column = lax.broadcasted_iota(jnp.int32, (half, length), 1)
    for par in range(2):
        choose = jnp.where(column == 2 * at + par, 1.0, 0.0).astype(BF16)
        masks[par, 0:half, :] = lax.dot_general(choose, marks, ROW_CONTRACT, preferred_element_type=F32)
        masks[par, half : half + PAD, :] = jnp.zeros((PAD, 8), F32)


def front(
    dp, tensor,
    tokens, cotangent, segments, gain, shift, in_shard, out_shard, up_shard, down_shard,
    b_in, taps, tap_bias, ptable, w1, b1, w2, b2, w3, rates, direct,
    wave, wave_back, twist, e_wave, e_back, e_twist,
    in_all, out_full, up_all, down_all, cot_full, norm_out, gated_out, own_gated, masks_out,
    z_out, filt_out, e_filt_out, spec_out, e_spec_out, conv_out, hidden_out,
    in_land, w_in, cot_own, norm_full, gated, masks, z, filt_spec, e_filt_spec, spec, e_spec, conv, hidden,
    short, rhs, rhs_even, rhs_odd, filt, send, recv, local,
):
    tabs = (wave, wave_back, twist, e_wave, e_back, e_twist)
    half = wave.shape[1] // 3
    count = tokens.shape[0]
    own = count // 2
    place = Place(dp, tensor)
    sems, copies = Sems(send, recv), LocalCopies(local)
    barrier = place.greet()

    parity = parity_matrix(count)
    normal, _ = layer_norm_parts(dot(parity, tokens[...]))
    low = (normal * gain[...] + shift[...]).astype(BF16)
    for par in range(2):
        norm_full[par, place.t] = low[par * own : (par + 1) * own]
    shuffled = dot(parity, cotangent[...]).astype(BF16)
    for par in range(2):
        cot_own[par] = shuffled[par * own : (par + 1) * own]
    place.met(barrier)

    norms = [
        tensor_gather(place, sems, norm_full.at[par, place.t], lambda i, par=par: norm_full.at[par, i]) for par in range(2)
    ]
    ins = dp_gather(place, sems, in_shard, lambda i: in_land.at[i])
    outs = dp_gather(place, sems, out_shard, lambda i: out_full.at[place.t, i])
    ups = dp_gather(place, sems, up_shard, lambda i: up_all.at[i])
    downs = dp_gather(place, sems, down_shard, lambda i: down_all.at[i])
    cots = [tensor_gather(place, sems, cot_own.at[par], lambda i, par=par: cot_full.at[par, i]) for par in range(2)]
    for gather in [*norms, ins, outs, ups, downs, *cots]:
        gather.start()
    own_in = copies.start(in_shard, in_land.at[place.d])
    own_out = copies.start(out_shard, out_full.at[place.t, place.d])
    copies.start(up_shard, up_all.at[place.d])
    copies.start(down_shard, down_all.at[place.d])
    for par in range(2):
        copies.start(cot_own.at[par], cot_full.at[par, place.t])

    make_masks(masks, segments, half)
    copies.start(masks, masks_out)
    net = (ptable, w1, b1, w2, b2, w3, rates, hidden, filt, filt_spec, e_filt_spec)
    make_filters(tabs, rhs, *net, 0)
    for gather in norms:
        gather.forward(tensor_origins(place))
    ins.forward(dp_origins(place))
    make_filters(tabs, rhs, *net, 1)
    turn_filters(tabs, filt_spec, e_filt_spec)
    copies.start(filt_spec, filt_out)
    copies.start(e_filt_spec, e_filt_out)
    copies.start(hidden, hidden_out)
    for gather in norms:
        gather.arrived()
    ins.arrived()
    copies.take(own_in)
    for which in range(3):
        w_in[which] = jnp.concatenate([in_land[i, which].astype(F32) for i in range(dp)], axis=0).astype(BF16)
    copies.start(in_land, in_all)
    copies.start(norm_full, norm_out)
    for par in range(2):
        normed = norm_full[par].reshape(half, -1)
        for which in range(3):
            put_zpre(z, normed, w_in[which], b_in, which, par, half)
    copies.start(z, z_out)
    for gather in cots:
        gather.forward(tensor_origins(place))
    outs.forward(dp_origins(place))
    make_short(short, z, masks, taps, tap_bias, half)

    def convolve(o, source):
        analyse(tabs, rhs, source, spec.at[o], e_spec.at[o], masks)
        copies.start(spec.at[o], spec_out.at[o])
        copies.start(e_spec.at[o], e_spec_out.at[o])
        edges = spectra_product(
            tabs, filt_spec.at[o], e_filt_spec.at[o], spec.at[o], e_spec.at[o], rhs_even, rhs_odd, False, False
        )
        synthesise(tabs, rhs_even, conv.at[o], 0)
        synthesise(tabs, rhs_odd, conv.at[o], 1)
        join(conv.at[o], edges, direct[o : o + 1, :], source, masks, half)
        copies.start(conv.at[o], conv_out.at[o])

    convolve(0, lambda par, at: short[0, par, at, :])
    outs.arrived()
    copies.take(own_out)
    out_rows = tensor_gather(place, sems, out_full.at[place.t], lambda i: out_full.at[i])
    out_rows.start()
    ups.forward(dp_origins(place))
    convolve(1, lambda par, at: short[1, par, at, :] * conv[0, par, at, :])
    out_rows.forward(tensor_origins(place))
    for par in range(2):
        for block in range(tensor):
            values = short[2, par, block * own : (block + 1) * own, :] * conv[1, par, block * own : (block + 1) * own, :]
            gated[par, block] = values.astype(BF16)
    trades = []
    for i in range(1, tensor):
        to = place.t_at(i)
        for par in range(2):
            trades.append(sems.copy(gated.at[par, to], own_gated.at[place.t, par], {"tensor": to}))
    for copy in trades:
        copy.start()
    for par in range(2):
        copies.start(gated.at[par, place.t], own_gated.at[place.t, par])
    copies.start(gated, gated_out)
    downs.forward(dp_origins(place))
    for gather in (*cots, ups, downs, out_rows):
        gather.arrived()
    for copy in trades:
        copy.wait()
    for gather in (*norms, ins, outs, ups, downs, *cots, out_rows):
        gather.finish()
    copies.finish()


def mixer_backward(
    d_mix, w_out, taps, tap_bias, ptable, w1, b1, w2, b2, w3, rates, direct, masks,
    wave, wave_back, twist, e_wave, e_back, e_twist,
    z, filt_spec, e_filt_spec, spec, e_spec, conv, hidden,
    d_z, g_in_bias, g_taps, g_tap_bias, g_direct, g_w1, g_b1, g_w2, g_b2, g_w3,
    short, rhs, rhs_even, rhs_odd, g, g_spec, e_g_spec, d_short, d_filt, acc,
):
    tabs = (wave, wave_back, twist, e_wave, e_back, e_twist)
    half = wave.shape[1] // 3
    width = z.shape[3]

    make_short(short, z, masks, taps, tap_bias, half)
    for par in range(2):
        g[par] = dot(d_mix[par], w_out[...])

        def gate(at, par=par):
            grad = g[par, at, :]
            d_short[2, par, pl.ds(pl.multiple_of(at.start, 8), at.size), :] = grad * conv[1, par, at, :]
            g[par, at, :] = grad * short[2, par, at, :]

        over_rows(half, CHUNK, gate)

    def back(o, forward_in, out):
        analyse(tabs, rhs, lambda par, at: g[par, at, :], g_spec, e_g_spec, masks)
        edges = spectra_product(
            tabs, filt_spec.at[o], e_filt_spec.at[o], g_spec, e_g_spec, rhs_even, rhs_odd, True, False
        )
        synthesise(tabs, rhs_even, out, 0)
        synthesise(tabs, rhs_odd, out, 1)
        join(out, edges, direct[o : o + 1, :], lambda par, at: g[par, at, :], masks, half)
        edges = spectra_product(tabs, spec.at[o], e_spec.at[o], g_spec, e_g_spec, rhs_even, rhs_odd, True, True)
        synthesise(tabs, rhs_even, d_filt.at[o], 0)
        synthesise(tabs, rhs_odd, d_filt.at[o], 1)
        acc[...] = jnp.zeros_like(acc)
        for par in range(2):
            edge = edges[par].shape[0] // 2

            def scale(at, par=par):
                d_filt[o, par, at, :] *= 1.0 / half
                acc[0:8, :] += jnp.sum((g[par, at, :] * forward_in(par, at)).reshape(-1, 8, width), axis=0)

            over_rows(half, CHUNK, scale)
            d_filt[o, par, 0:edge, :] += (edges[par][:edge] + edges[par][edge:]) * (1.0 / edge)
        g_direct[o : o + 1, :] = jnp.sum(acc[0:8, :], axis=0, keepdims=True)

    back(1, lambda par, at: short[1, par, at, :] * conv[0, par, at, :], d_short.at[0])
    for par in range(2):
        def gate(at, par=par):
            grad = d_short[0, par, at, :]
            d_short[1, par, at, :] = grad * conv[0, par, at, :]
            g[par, at, :] = grad * short[1, par, at, :]

        over_rows(half, CHUNK, gate)
    back(0, lambda par, at: short[0, par, at, :], d_short.at[0])

    for which in range(3):
        acc[...] = jnp.zeros_like(acc)
        for par in range(2):
            d_short[which, par, half : half + PAD, :] = jnp.zeros((PAD, width), F32)
        for par in range(2):
            def short_back(at, par=par, which=which):
                size, start = at.size, at.start
                tap = lambda j: taps[j, which : which + 1, :]
                _, here, one, two = short_rows(z, which, par, at, masks, taps, tap_bias)
                grad = d_short[which, par, at, :]
                fold = lambda x: jnp.sum(x.reshape(-1, 8, width), axis=0)
                acc[0:8, :] += fold(grad)
                acc[8:16, :] += fold(grad * here)
                acc[16:24, :] += fold(grad * one)
                acc[24:32, :] += fold(grad * two)
                wide = pl.ds(pl.multiple_of(start, 8), size + PAD)
                same = (d_short[which, par, wide, :] * masks[par, wide, 4:5])[1 : size + 1]
                if par == 0:
                    other = d_short[which, 1, at, :] * masks[1, at, 3:4]
                else:
                    other = (d_short[which, 0, wide, :] * masks[0, wide, 3:4])[1 : size + 1]
                low = (tap(0) * grad + tap(1) * other + tap(2) * same).astype(BF16)
                d_z[which, par, at, :] = low
                acc[32:40, :] += fold(low.astype(F32))

            over_rows(half, CHUNK, short_back)
        total = lambda i: jnp.sum(acc[8 * i : 8 * i + 8, :], axis=0, keepdims=True)
        g_tap_bias[which : which + 1, :] = total(0)
        for j in range(3):
            g_taps[j, which : which + 1, :] = total(1 + j)
        g_in_bias[which : which + 1, :] = total(4)

    for o in range(2):
        for par in range(2):
            def undo(at, par=par, o=o):
                d_filt[o, par, at, :] *= decay_at(par, CHUNK, at.start, rates[o : o + 1, :])

            over_rows(half, CHUNK, undo)
        g_w3[o] = fine_dot(hidden[0], d_filt[o, 0], COLUMN_CONTRACT) + fine_dot(hidden[1], d_filt[o, 1], COLUMN_CONTRACT)
    sums = None
    for par in range(2):
        pre1, h1, pre2 = hidden_layers(ptable[par], w1[...], b1[...], w2[...], b2[...])
        d_h2 = fine_dot(d_filt[0, par], w3[0], ROW_CONTRACT) + fine_dot(d_filt[1, par], w3[1], ROW_CONTRACT)
        d_pre2 = d_h2 * jnp.cos(pre2)
        d_h1 = fine_dot(d_pre2, w2[...], ROW_CONTRACT)
        d_pre1 = d_h1 * jnp.cos(pre1)
        own = (
            fine_dot(ptable[par], d_pre1, COLUMN_CONTRACT),
            jnp.sum(d_pre1, axis=0, keepdims=True),
            fine_dot(h1, d_pre2, COLUMN_CONTRACT),
            jnp.sum(d_pre2, axis=0, keepdims=True),
        )
        sums = own if sums is None else tuple(a + b for a, b in zip(sums, own, strict=True))
    g_w1[...], g_b1[...], g_w2[...], g_b2[...] = sums


MESH = pl.DeviceIdType.MESH


class Place:
    def __init__(self, dp, tensor):
        self.dp, self.tensor = dp, tensor
        self.rows = 4 if dp % 4 == 0 else 1
        self.cols = dp // self.rows
        self.cores = 2 if tensor % 2 == 0 else 1
        self.ys = tensor // self.cores
        self.d, self.t = lax.axis_index("dp"), lax.axis_index("tensor")
        self.a, self.b = self.d // self.cols, lax.rem(self.d, self.cols)
        self.y, self.c = self.t // self.cores, lax.rem(self.t, self.cores)

    def a_at(self, i):
        return lax.rem(self.a + i + self.rows, self.rows) * self.cols + self.b

    def b_at(self, i):
        return self.a * self.cols + lax.rem(self.b + i + self.cols, self.cols)

    def y_at(self, i):
        return lax.rem(self.y + i + self.ys, self.ys) * self.cores + self.c

    def core_peer(self):
        return self.y * self.cores + 1 - self.c

    def t_at(self, i):
        return lax.rem(self.t + i + self.tensor, self.tensor)

    def greet(self, dp=True, all_tensor=True):
        peers = [{"tensor": self.t_at(i)} for i in range(1, self.tensor)]
        if dp:
            peers += [{"dp": self.a_at(i)} for i in range(1, self.rows)]
            peers += [{"dp": self.b_at(i)} for i in range(1, self.cols)]
        barrier = pltpu.get_barrier_semaphore()
        for peer in peers:
            pl.semaphore_signal(barrier, inc=1, device_id=peer, device_id_type=MESH)
        self.expected = len(peers)
        return barrier

    def met(self, barrier):
        pl.semaphore_wait(barrier, self.expected)


class Sems:
    def __init__(self, send, recv):
        self.send, self.recv, self.used = send, recv, 0

    def copy(self, src, dst, device):
        i = self.used
        self.used += 1
        return pltpu.make_async_remote_copy(
            src_ref=src, dst_ref=dst, send_sem=self.send.at[i], recv_sem=self.recv.at[i],
            device_id=device, device_id_type=MESH,
        )


class LocalCopies:
    def __init__(self, sems):
        self.sems, self.open, self.used = sems, [], 0

    def start(self, src, dst):
        copy = pltpu.make_async_copy(src, dst, self.sems.at[self.used])
        self.used += 1
        copy.start()
        self.open.append(copy)
        return copy

    def take(self, copy):
        copy.wait()
        self.open = [other for other in self.open if other is not copy]

    def finish(self):
        for copy in self.open:
            copy.wait()


class Gather:
    def __init__(self, sems, source, slot, own, far, near, device):
        self.first = [sems.copy(source, slot(own), device(i)) for i in far]
        self.near = [sems.copy(source, slot(own), device(i)) for i in near]
        self.sems, self.slot, self.device, self.near_ids = sems, slot, device, near
        self.second = []

    def start(self):
        for copy in self.first + self.near:
            copy.start()

    def forward(self, origins, which=None):
        for i, origin in enumerate(origins):
            if which is not None and i not in which:
                continue
            self.first[i].wait_recv()
            for peer in self.near_ids:
                copy = self.sems.copy(self.slot(origin), self.slot(origin), self.device(peer))
                copy.start()
                self.second.append(copy)

    def arrived(self):
        for copy in self.near + self.second:
            copy.wait_recv()

    def finish(self):
        for copy in self.first + self.near + self.second:
            copy.wait_send()


def tensor_gather(place, sems, source, slot):
    near = [place.core_peer()] if place.cores == 2 else []
    return Gather(
        sems, source, slot, place.t, [place.y_at(i) for i in range(1, place.ys)], near, lambda i: {"tensor": i}
    )


def dp_gather(place, sems, source, slot):
    return Gather(
        sems, source, slot, place.d, [place.a_at(i) for i in range(1, place.rows)],
        [place.b_at(i) for i in range(1, place.cols)], lambda i: {"dp": i},
    )


def tensor_origins(place):
    return [place.y_at(-i) for i in range(1, place.ys)]


def dp_origins(place):
    return [place.a_at(-i) for i in range(1, place.rows)]


def gather_counts(dp, tensor):
    cores = 2 if tensor % 2 == 0 else 1
    rows = 4 if dp % 4 == 0 else 1
    far_t, near_t, far_d, near_d = tensor // cores - 1, cores - 1, rows - 1, dp // rows - 1
    return far_t + near_t + far_t * near_t, far_d + near_d + far_d * near_d


def vmem_specs(n):
    return [pl.BlockSpec(memory_space=pltpu.VMEM)] * n


def mix_shapes(half, width, hidden_width):
    edge4 = half // 4
    return dict(
        z=((3, 2, half + 2 * PAD, width), F32),
        filt_spec=((2, 3, 2 * half, width), F32),
        e_filt_spec=((2, 3, edge4, width), F32),
        spec=((2, 2, 2 * half, width), F32),
        e_spec=((2, 2, edge4, width), F32),
        conv=((2, 2, half, width), F32),
        hidden=((2, half, hidden_width), F32),
    )


def layer_norm(values, norm_gain, norm_shift):
    center = jnp.mean(values, axis=-1, keepdims=True)
    centred = values - center
    spread = jnp.mean(centred * centred, axis=-1, keepdims=True)
    return centred * lax.rsqrt(spread + EPSILON) * norm_gain + norm_shift


def smooth_gelu(values):
    return jax.nn.gelu(values, approximate=True)


def front_call(dp, tensor, args, count, model, channels, units, rows, half, hidden_width):
    S = jax.ShapeDtypeStruct
    own = count // 2
    shapes = mix_shapes(half, channels, hidden_width)
    land = ((dp, 3, rows, channels), BF16)
    norm, gate, mask = ((2, tensor, own, model), BF16), ((2, tensor, own, channels), BF16), ((2, half + PAD, 8), F32)
    outs = [
        S(*land), S((tensor, dp, rows, channels), BF16), S((dp, rows, units), BF16), S((dp, rows, units), BF16),
        S(*norm), S(*norm), S(*gate), S((tensor, 2, own, channels), BF16), S(*mask),
    ] + [S(*v) for v in shapes.values()]
    per_t, per_d = gather_counts(dp, tensor)
    copies = 5 * per_t + 4 * per_d + 2 * (tensor - 1)
    return pl.pallas_call(
        functools.partial(front, dp, tensor),
        out_shape=outs,
        in_specs=vmem_specs(5) + [pl.BlockSpec(memory_space=pl.ANY)] * 4 + vmem_specs(len(args) - 9),
        out_specs=[pl.BlockSpec(memory_space=pl.ANY)] * len(outs),
        scratch_shapes=[
            pltpu.VMEM(*land), pltpu.VMEM((3, model, channels), BF16), pltpu.VMEM((2, own, model), BF16),
            pltpu.VMEM(*norm), pltpu.VMEM(*gate), pltpu.VMEM(*mask),
        ] + [pltpu.VMEM(*v) for v in shapes.values()] + [
            pltpu.VMEM((3, 2, half, channels), F32),
            pltpu.VMEM((3 * half, channels), BF16),
            pltpu.VMEM((6 * half, channels), BF16),
            pltpu.VMEM((6 * half, channels), BF16),
            pltpu.VMEM((half, channels), F32),
            pltpu.SemaphoreType.DMA((copies,)),
            pltpu.SemaphoreType.DMA((copies,)),
            pltpu.SemaphoreType.DMA((24,)),
        ],
        compiler_params=pltpu.CompilerParams(collective_id=0, has_side_effects=True, vmem_limit_bytes=VMEM_LIMIT),
        name="front",
    )(*args)


def backward_call(args, half, width, emb, hidden_width):
    S = jax.ShapeDtypeStruct
    outs = [
        S((3, 2, half, width), BF16), S((3, width), F32), S((3, 3, width), F32), S((3, width), F32), S((2, width), F32),
        S((emb, hidden_width), F32), S((1, hidden_width), F32), S((hidden_width, hidden_width), F32), S((1, hidden_width), F32),
        S((2, hidden_width, width), F32),
    ]
    return pl.pallas_call(
        mixer_backward,
        out_shape=outs,
        in_specs=vmem_specs(len(args)),
        out_specs=vmem_specs(len(outs)),
        scratch_shapes=[
            pltpu.VMEM((3, 2, half, width), F32),
            pltpu.VMEM((3 * half, width), BF16),
            pltpu.VMEM((6 * half, width), BF16),
            pltpu.VMEM((6 * half, width), BF16),
            pltpu.VMEM((2, half, width), F32),
            pltpu.VMEM((2, 2 * half, width), F32),
            pltpu.VMEM((2, half // 4, width), F32),
            pltpu.VMEM((3, 2, half + PAD, width), F32),
            pltpu.VMEM((2, 2, half, width), F32),
            pltpu.VMEM((40, width), F32),
        ],
        compiler_params=pltpu.CompilerParams(vmem_limit_bytes=VMEM_LIMIT),
        name="mixer_backward",
    )(*args)


def smooth_gelu(values):
    return jax.nn.gelu(values, approximate=True)


def body(
    tokens,
    segment_ids,
    mix_norm_gain,
    mix_norm_bias,
    in_weight,
    in_bias,
    short_weight,
    short_bias,
    filt_in_weight,
    filt_in_bias,
    filt_mid_weight,
    filt_mid_bias,
    filt_out_weight,
    decay_rates,
    long_bias,
    out_weight,
    out_bias,
    mlp_norm_gain,
    mlp_norm_bias,
    up_weight,
    up_bias,
    down_weight,
    down_bias,
    cotangent,
):
    residual = tokens[0].astype(jnp.float32)
    doc_ids = segment_ids[0]
    model_width = residual.shape[1]
    length = doc_ids.shape[0]
    dp, tensor = lax.axis_size("dp"), lax.axis_size("tensor")
    rows, channels, units, count = in_weight.shape[0], in_weight.shape[2], up_weight.shape[1], tokens.shape[1]
    half, hidden_width = length // 2, filt_mid_bias.shape[0]

    def take_rows(weight_flat, incoming):
        product = jnp.dot(incoming, weight_flat, preferred_element_type=jnp.float32)
        return (product, incoming)

    def back_rows(weight_all, kept_low, incoming):
        product = jnp.dot(incoming, weight_all, preferred_element_type=jnp.float32)
        weight_grad = lax.dot_general(
            incoming, kept_low, COLUMN_CONTRACT, preferred_element_type=jnp.float32
        )
        return (product, weight_grad)

    def sum_terms(left_low, weight_all):
        return lax.dot_general(
            left_low, weight_all, ROW_CONTRACT, preferred_element_type=jnp.float32
        )

    normed, first_norm_back = jax.vjp(layer_norm, residual, mix_norm_gain, mix_norm_bias)
    normed_low = normed.astype(jnp.bfloat16)
    tables = tuple(jnp.asarray(t) for t in wave_tables(length))
    ptable = jnp.asarray(position_table(length, filt_in_weight.shape[0]))
    net = (
        short_weight, short_bias, ptable, filt_in_weight, filt_in_bias[None], filt_mid_weight,
        filt_mid_bias[None], jnp.swapaxes(filt_out_weight, 0, 1), decay_rates, long_bias,
    )
    in_par, out_par, up_par, down_par, cot_par, norm_par, gated_par, own_gated, masks, *kept = front_call(
        dp, tensor,
        (tokens[0], cotangent[0], segment_ids, mix_norm_gain[None], mix_norm_bias[None], jnp.swapaxes(in_weight, 0, 1), out_weight,
         up_weight, down_weight, in_bias) + net + tables,
        count, model_width, channels, units, rows, half, hidden_width,
    )
    in_flat = jnp.swapaxes(in_par, 1, 2).reshape(model_width, 3 * channels)
    out_full = jnp.moveaxis(out_par.reshape(tensor, model_width, channels), 0, 1).reshape(model_width, model_width)
    out_all = lax.dynamic_index_in_dim(out_par, lax.axis_index("tensor"), 0, False).reshape(model_width, channels)
    up_all, down_all = up_par.reshape(model_width, units), down_par.reshape(model_width, units)
    normed_full = in_order(norm_par.reshape(2, half, model_width))
    cot_full = in_order(cot_par.reshape(2, half, model_width))
    gated_low = in_order(gated_par.reshape(2, half, channels))
    own_gated = in_order(jnp.moveaxis(own_gated, 0, 2).reshape(2, count // 2, model_width))
    mixed = lax.dot_general(own_gated, out_full, ROW_CONTRACT, preferred_element_type=jnp.float32)
    mixed_sum = residual + mixed + out_bias
    normed_two, second_norm_back = jax.vjp(layer_norm, mixed_sum, mlp_norm_gain, mlp_norm_bias)
    normed_two_low = normed_two.astype(jnp.bfloat16)
    up_raw, normed_two_full = take_rows(
        up_all, lax.all_gather(normed_two_low, "tensor", axis=0, tiled=True)
    )
    pre_act = up_raw + up_bias
    activated, gelu_back = jax.vjp(smooth_gelu, pre_act)
    act_low = activated.astype(jnp.bfloat16)
    mlp_sum = lax.psum_scatter(
        sum_terms(act_low, down_all), "tensor", scatter_dimension=0, tiled=True
    )
    output = (mixed_sum + mlp_sum + down_bias).astype(jnp.bfloat16)
    grad_low = cotangent[0]
    grad_out = grad_low.astype(jnp.float32)
    grad_down_bias = jnp.sum(grad_out, axis=0)
    d_act, grad_down = back_rows(
        down_all, act_low, cot_full
    )
    d_pre_low = gelu_back(d_act)[0].astype(jnp.bfloat16)
    grad_up_bias = jnp.sum(d_pre_low, axis=0, dtype=jnp.float32)
    grad_up = lax.dot_general(
        normed_two_full, d_pre_low, COLUMN_CONTRACT, preferred_element_type=jnp.float32
    )
    d_normed_two = lax.psum_scatter(
        sum_terms(d_pre_low, up_all), "tensor", scatter_dimension=0, tiled=True
    )
    d_mixed_norm, grad_mlp_gain, grad_mlp_shift = second_norm_back(d_normed_two)
    d_mixed = grad_out + d_mixed_norm
    grad_out_bias = jnp.sum(d_mixed, axis=0)
    d_mix_low = d_mixed.astype(jnp.bfloat16)
    d_mix_full = lax.all_gather(d_mix_low, "tensor", axis=0, tiled=True)
    grad_out_w = lax.dot_general(d_mix_full, gated_low, COLUMN_CONTRACT, preferred_element_type=jnp.float32)
    (
        d_z_par, grad_in_bias, grad_taps, grad_tap_bias, grad_direct, grad_first_w, grad_first_b, grad_middle_w, grad_middle_b,
        grad_last_w,
    ) = backward_call((by_parity(d_mix_full), out_all) + net + (masks,) + tables + tuple(kept), half, channels, filt_in_weight.shape[0], hidden_width)
    grad_first_b, grad_middle_b = grad_first_b[0], grad_middle_b[0]
    grad_last_w = jnp.swapaxes(grad_last_w, 0, 1)
    d_z_low = in_order(jnp.moveaxis(d_z_par, 0, 2)).reshape(length, 3 * channels)
    grad_in = lax.dot_general(
        normed_full, d_z_low, COLUMN_CONTRACT, preferred_element_type=jnp.float32
    ).reshape(model_width, 3, channels)
    d_normed = lax.psum_scatter(
        sum_terms(d_z_low, in_flat), "tensor", scatter_dimension=0, tiled=True
    )
    d_input_norm, grad_mix_gain, grad_mix_shift = first_norm_back(d_normed)
    grad_tokens = (d_mixed + d_input_norm).astype(jnp.bfloat16)[None]
    grad_in, grad_out_w, grad_up, grad_down = (
        lax.psum_scatter(grad_in, "dp", scatter_dimension=0, tiled=True),
        lax.psum_scatter(grad_out_w, "dp", scatter_dimension=0, tiled=True),
        lax.psum_scatter(grad_up, "dp", scatter_dimension=0, tiled=True),
        lax.psum_scatter(grad_down, "dp", scatter_dimension=0, tiled=True),
    )
    grad_in_bias, grad_taps, grad_tap_bias, grad_last_w, grad_direct, grad_up_bias = lax.psum(
        (grad_in_bias, grad_taps, grad_tap_bias, grad_last_w, grad_direct, grad_up_bias), "dp"
    )
    (
        grad_mix_gain,
        grad_mix_shift,
        grad_first_w,
        grad_first_b,
        grad_middle_w,
        grad_middle_b,
        grad_out_bias,
        grad_mlp_gain,
        grad_mlp_shift,
        grad_down_bias,
    ) = lax.psum(
        (
            grad_mix_gain,
            grad_mix_shift,
            grad_first_w,
            grad_first_b,
            grad_middle_w,
            grad_middle_b,
            grad_out_bias,
            grad_mlp_gain,
            grad_mlp_shift,
            grad_down_bias,
        ),
        ("dp", "tensor"),
    )
    return (
        output[None],
        grad_tokens,
        grad_mix_gain,
        grad_mix_shift,
        grad_in,
        grad_in_bias,
        grad_taps,
        grad_tap_bias,
        grad_first_w,
        grad_first_b,
        grad_middle_w,
        grad_middle_b,
        grad_last_w,
        grad_direct,
        grad_out_w,
        grad_out_bias,
        grad_mlp_gain,
        grad_mlp_shift,
        grad_up,
        grad_up_bias,
        grad_down,
        grad_down_bias,
    )


def solution(mesh):
    placed = (
        P("dp", "tensor", None),
        P("dp", None),
        P(),
        P(),
        P("dp", None, "tensor"),
        P(None, "tensor"),
        P(None, None, "tensor"),
        P(None, "tensor"),
        P(),
        P(),
        P(),
        P(),
        P(None, None, "tensor"),
        P(None, "tensor"),
        P(None, "tensor"),
        P("dp", "tensor"),
        P(),
        P(),
        P(),
        P("dp", "tensor"),
        P("tensor"),
        P("dp", "tensor"),
        P(),
        P("dp", "tensor", None),
    )
    return jax.shard_map(
        body,
        mesh=mesh,
        in_specs=placed,
        out_specs=(
            P("dp", "tensor", None),
            P("dp", "tensor", None),
            P(),
            P(),
            P("dp", None, "tensor"),
            P(None, "tensor"),
            P(None, None, "tensor"),
            P(None, "tensor"),
            P(),
            P(),
            P(),
            P(),
            P(None, None, "tensor"),
            P(None, "tensor"),
            P("dp", "tensor"),
            P(),
            P(),
            P(),
            P("dp", "tensor"),
            P("tensor"),
            P("dp", "tensor"),
            P(),
        ),
        check_vma=False,
    )
```

```python
import functools
import math

import jax
import jax.numpy as jnp
import numpy as np
from jax import lax
from jax.experimental import pallas as pl
from jax.experimental.pallas import tpu as pltpu
from jax.sharding import PartitionSpec as P

DOCS = 3
EPSILON = 1e-05
HIGHEST = lax.Precision.HIGHEST
ROW_CONTRACT = (((1,), (1,)), ((), ()))
COLUMN_CONTRACT = (((0,), (0,)), ((), ()))
F32, BF16 = jnp.float32, jnp.bfloat16
CHUNK = 64
VMEM_LIMIT = 58 * 2**20


def half_table(count, period):
    turns = ((2 * np.arange(count)[:, None] + 1) * np.arange(count)[None, :]) % (2 * period)
    angle = turns * (math.pi / period)
    return np.cos(angle), -np.sin(angle)


def three_pass(table):
    high = table.astype(np.float32).astype(jnp.bfloat16)
    low = (table.astype(np.float32) - high.astype(np.float32)).astype(jnp.bfloat16)
    return np.concatenate([high, high, low], axis=1)


def wave_tables(length):
    half, edge = length // 2, length // 32
    real, imag = half_table(half, length)
    whole = np.concatenate([real, imag], axis=0)
    e_real, e_imag = half_table(edge, 2 * edge)
    zero = np.zeros_like(e_real)
    both = np.block([[e_real, zero], [zero, e_real], [e_imag, zero], [zero, e_imag]])
    step = (2 * np.arange(half) + 1) * (math.pi / length)
    e_step = np.tile((2 * np.arange(edge) + 1) * (math.pi / (2 * edge)), 2)
    twist = np.stack([np.cos(step), -np.sin(step)], axis=1).astype(np.float32)
    e_twist = np.stack([np.cos(e_step), -np.sin(e_step)], axis=1).astype(np.float32)
    return (
        three_pass(whole), three_pass(whole.T), twist,
        three_pass(both), three_pass(both.T), e_twist,
    )


def position_table(length, emb_width):
    bands = (emb_width - 1) // 2
    places = np.arange(length, dtype=np.float32)
    angles = (2.0 * math.pi * places / length).astype(np.float32)
    frequency = np.linspace(0.0001, bands - 1, bands, dtype=np.float32)
    phases = (angles[:, None] * frequency[None, :]).astype(np.float64)
    table = np.concatenate([(places / (length - 1))[:, None], np.cos(phases), -np.sin(phases)], axis=1)
    return by_parity(table.astype(np.float32))


def by_parity(rows):
    return rows.reshape((rows.shape[0] // 2, 2) + rows.shape[1:]).swapaxes(0, 1)


def in_order(halves):
    return halves.swapaxes(0, 1).reshape((-1,) + halves.shape[2:])


def over_rows(rows, step, work):
    @pl.loop(0, rows // step)
    def _(i):
        work(pl.ds(pl.multiple_of(i * step, step), step))


def parts(x):
    high = x.astype(BF16)
    return high, (x - high.astype(F32)).astype(BF16)


def put_parts(rhs, at, base, block, x):
    high, low = parts(x)
    size = x.shape[0]
    start = at.start if isinstance(at, pl.Slice) else at
    for slot, piece in ((0, high), (1, low), (2, high)):
        rhs[pl.ds(pl.multiple_of(start + (base + slot * block), 16), size), :] = piece


def mul(ar, ai, br, bi):
    return ar * br - ai * bi, ar * bi + ai * br


def mul_conj(ar, ai, br, bi):
    return ar * br + ai * bi, ar * bi - ai * br


def blend(f, x, conj):
    (fe, fo, ft), (xe, xo) = f, x
    m = mul_conj if conj else mul
    if conj:
        a, b = m(*fe, *xe), m(*fo, *xo)
        c, d = m(*fe, *xo), m(*ft, *xe)
    else:
        a, b = m(*fe, *xe), m(*ft, *xo)
        c, d = m(*fe, *xo), m(*fo, *xe)
    return (a[0] + b[0], a[1] + b[1]), (c[0] + d[0], c[1] + d[1])


def dot(a, b):
    return jnp.dot(a, b, preferred_element_type=F32)


def fine_dot(a, b, dims=(((1,), (0,)), ((), ()))):
    return lax.dot_general(a, b, dims, precision=HIGHEST, preferred_element_type=F32)


def analyse(tabs, rhs, source, spec, edge_spec, masks):
    wave, _, _, e_wave, _, _ = tabs
    half, edge = wave.shape[1] // 3, e_wave.shape[1] // 6

    @pl.loop(0, 2)
    def _(par):
        def fill(at):
            put_parts(rhs, at, 0, half, source(par, at) * masks[par, at, 0:1])

        over_rows(half, CHUNK, fill)
        spec[par] = dot(wave[...], rhs[0 : 3 * half, :])
        first, last = pl.ds(0, edge), pl.ds(half - edge, edge)
        window = jnp.concatenate(
            [source(par, first) * masks[par, first, 1:2], source(par, last) * masks[par, last, 2:3]], axis=0
        )
        high, low = parts(window)
        edge_spec[par] = dot(e_wave[...], jnp.concatenate([high, low, high], axis=0))


def pair(ref, index, at, half):
    start = at.start
    return ref[index, at, :], ref[index, pl.ds(pl.multiple_of(start + half, 8), at.size), :]


def spectra_product(tabs, filt, e_filt, spec, e_spec, rhs_even, rhs_odd, conj, turn):
    _, wave_back, twist, _, e_back, e_twist = tabs
    half, edge2 = wave_back.shape[1] // 6, e_back.shape[1] // 6

    def get(f, tw, at, n):
        fe, fo = pair(f, 0, at, n), pair(f, 1, at, n)
        ft = mul(*fo, tw[at, 0:1], tw[at, 1:2]) if turn else pair(f, 2, at, n)
        return fe, fo, ft

    def work(at):
        even, odd = blend(get(filt, twist, at, half), (pair(spec, 0, at, half), pair(spec, 1, at, half)), conj)
        for rhs, (real, imag) in ((rhs_even, even), (rhs_odd, odd)):
            put_parts(rhs, at, 0, 2 * half, real)
            put_parts(rhs, at, half, 2 * half, imag)

    over_rows(half, CHUNK // 2, work)
    at = pl.ds(0, edge2)
    even, odd = blend(get(e_filt, e_twist, at, edge2), (pair(e_spec, 0, at, edge2), pair(e_spec, 1, at, edge2)), conj)
    out = []
    for real, imag in (even, odd):
        high, low = parts(jnp.concatenate([real, imag], axis=0))
        out.append(dot(e_back[...], jnp.concatenate([high, low, high], axis=0)))
    return out


def synthesise(tabs, rhs, out, par):
    out[par, 0 : tabs[1].shape[0], :] = dot(tabs[1][...], rhs[...])


def join(out, edges, direct, source, masks, half):
    for par in range(2):
        def work(at, par=par):
            out[par, at, :] = out[par, at, :] * masks[par, at, 0:1] + direct * source(par, at)

        over_rows(half, CHUNK, work)
        edge = edges[par].shape[0] // 2
        first, last = pl.ds(0, edge), pl.ds(half - edge, edge)
        out[par, first, :] += edges[par][:edge] * masks[par, first, 1:2]
        out[par, last, :] += edges[par][edge:] * masks[par, last, 2:3]


def hidden_layers(table, w1, b1, w2, b2):
    pre1 = fine_dot(table, w1) + b1
    h1 = jnp.sin(pre1)
    pre2 = fine_dot(h1, w2) + b2
    return pre1, h1, pre2


def decay_at(par, rows, start, rates):
    m = lax.broadcasted_iota(jnp.int32, (rows, rates.shape[1]), 0) + start
    return jnp.exp((2 * m + par).astype(F32) * -rates)


def make_filters(tabs, rhs, ptable, w1, b1, w2, b2, w3, rates, hidden, filt, filt_spec, e_filt_spec, par):
    wave, _, _, e_wave, _, _ = tabs
    half, edge = wave.shape[1] // 3, e_wave.shape[1] // 6
    _, _, pre2 = hidden_layers(ptable[par], w1[...], b1[...], w2[...], b2[...])
    hidden[par] = jnp.sin(pre2)

    @pl.loop(0, 2)
    def _(o):
        filt[...] = fine_dot(hidden[par], w3[o])

        def fill(at):
            put_parts(rhs, at, 0, half, filt[at, :] * decay_at(par, CHUNK, at.start, rates[pl.ds(o, 1), :]))

        over_rows(half, CHUNK, fill)
        filt_spec[o, par] = dot(wave[...], rhs[0 : 3 * half, :]) * (1.0 / half)
        window = filt[pl.ds(0, edge), :] * decay_at(par, edge, 0, rates[pl.ds(o, 1), :])
        high, low = parts(jnp.concatenate([window, window], axis=0))
        e_filt_spec[o, par] = dot(e_wave[...], jnp.concatenate([high, low, high], axis=0)) * (1.0 / edge)


def turn_filters(tabs, filt_spec, e_filt_spec):
    wave, _, twist, e_wave, _, e_twist = tabs
    half, edge = wave.shape[1] // 3, e_wave.shape[1] // 6
    for o in range(2):
        def turn(at, o=o):
            real, imag = mul(*pair(filt_spec.at[o], 1, at, half), twist[at, 0:1], twist[at, 1:2])
            filt_spec[o, 2, at, :] = real
            filt_spec[o, 2, pl.ds(pl.multiple_of(at.start + half, 8), at.size), :] = imag

        over_rows(half, CHUNK, turn)
        n = 2 * edge
        real, imag = mul(*pair(e_filt_spec.at[o], 1, pl.ds(0, n), n), e_twist[:, 0:1], e_twist[:, 1:2])
        e_filt_spec[o, 2] = jnp.concatenate([real, imag], axis=0)


PAD = 8


def short_rows(z, which, par, at, masks, taps, tap_bias):
    size, start = at.size, at.start
    here = z[which, par, pl.ds(pl.multiple_of(start + PAD, 8), size), :]
    wide = pl.ds(pl.multiple_of(start, 8), size + PAD)
    same_before = z[which, par, wide, :][PAD - 1 : PAD - 1 + size]
    if par == 0:
        other = z[which, 1, wide, :][PAD - 1 : PAD - 1 + size]
    else:
        other = z[which, 0, pl.ds(pl.multiple_of(start + PAD, 8), size), :]
    one, two = masks[par, at, 3:4] * other, masks[par, at, 4:5] * same_before
    tap = lambda j: taps[j, which : which + 1, :]
    return tap_bias[which : which + 1, :] + tap(0) * here + tap(1) * one + tap(2) * two, here, one, two


def put_zpre(z, normed, weights, in_bias, which, par, half):
    zero = jnp.zeros((PAD, z.shape[3]), F32)
    z[which, par, 0:PAD, :] = zero
    z[which, par, PAD + half : PAD + half + PAD, :] = zero
    z[which, par, PAD : PAD + half, :] = dot(normed, weights) + in_bias[which : which + 1, :]


def make_short(short, z, masks, taps, tap_bias, half):
    for par in range(2):
        def work(at, par=par):
            for which in range(3):
                short[which, par, at, :] = short_rows(z, which, par, at, masks, taps, tap_bias)[0]

        over_rows(half, CHUNK, work)


def layer_norm_parts(values):
    center = jnp.mean(values, axis=-1, keepdims=True)
    centred = values - center
    spread = jnp.mean(centred * centred, axis=-1, keepdims=True)
    scale = lax.rsqrt(spread + EPSILON)
    return centred * scale, scale


def parity_matrix(rows):
    half = rows // 2
    at = lax.broadcasted_iota(jnp.int32, (rows, rows), 0)
    wanted = jnp.where(at < half, 2 * at, 2 * (at - half) + 1)
    return (lax.broadcasted_iota(jnp.int32, (rows, rows), 1) == wanted).astype(F32).astype(BF16)


def make_masks(masks, segments, half):
    seg = segments[...].astype(F32)
    length = seg.shape[1]
    place = lax.broadcasted_iota(jnp.int32, (1, length), 1)
    one = lambda ok: jnp.where(ok, 1.0, 0.0)
    rows = [one(seg == 1.0), one(seg == 0.0), one(seg == 2.0)]
    for j in (1, 2):
        rows.append(jnp.where(place >= j, one(pltpu.roll(seg, j, 1) == seg), 0.0))
    marks = jnp.concatenate(rows + [jnp.zeros((3, length), F32)], axis=0).astype(BF16)
    at = lax.broadcasted_iota(jnp.int32, (half, length), 0)
    column = lax.broadcasted_iota(jnp.int32, (half, length), 1)
    for par in range(2):
        choose = jnp.where(column == 2 * at + par, 1.0, 0.0).astype(BF16)
        masks[par, 0:half, :] = lax.dot_general(choose, marks, ROW_CONTRACT, preferred_element_type=F32)
        masks[par, half : half + PAD, :] = jnp.zeros((PAD, 8), F32)


def front(
    dp, tensor,
    tokens, cotangent, segments, gain, shift, in_shard, out_shard, up_shard, down_shard,
    b_in, taps, tap_bias, ptable, w1, b1, w2, b2, w3, rates, direct,
    wave, wave_back, twist, e_wave, e_back, e_twist,
    w_in_out, out_full, up_all, down_all, cot_full, norm_out, gated_out, own_gated, masks_out,
    z_out, filt_out, e_filt_out, spec_out, e_spec_out, conv_out, hidden_out,
    in_land, w_in, cot_own, norm_full, gated, masks, z, filt_spec, e_filt_spec, spec, e_spec, conv, hidden,
    short, rhs, rhs_even, rhs_odd, filt, send, recv, local,
):
    tabs = (wave, wave_back, twist, e_wave, e_back, e_twist)
    half = wave.shape[1] // 3
    count = tokens.shape[0]
    own = count // 2
    place = Place(dp, tensor)
    sems, copies = Sems(send, recv), LocalCopies(local)
    barrier = place.greet()

    parity = parity_matrix(count)
    normal, _ = layer_norm_parts(dot(parity, tokens[...]))
    low = (normal * gain[...] + shift[...]).astype(BF16)
    for par in range(2):
        norm_full[par, place.t] = low[par * own : (par + 1) * own]
    shuffled = dot(parity, cotangent[...]).astype(BF16)
    for par in range(2):
        cot_own[par] = shuffled[par * own : (par + 1) * own]
    place.met(barrier)

    norms = [
        tensor_gather(place, sems, norm_full.at[par, place.t], lambda i, par=par: norm_full.at[par, i]) for par in range(2)
    ]
    ins = dp_gather(place, sems, in_shard, lambda i: in_land.at[i])
    outs = dp_gather(place, sems, out_shard, lambda i: out_full.at[place.t, i])
    ups = dp_gather(place, sems, up_shard, lambda i: up_all.at[i])
    downs = dp_gather(place, sems, down_shard, lambda i: down_all.at[i])
    cots = [tensor_gather(place, sems, cot_own.at[par], lambda i, par=par: cot_full.at[par, i]) for par in range(2)]
    for gather in [*norms, ins, outs, ups, downs, *cots]:
        gather.start()
    own_in = copies.start(in_shard, in_land.at[place.d])
    own_out = copies.start(out_shard, out_full.at[place.t, place.d])
    copies.start(up_shard, up_all.at[place.d])
    copies.start(down_shard, down_all.at[place.d])
    for par in range(2):
        copies.start(cot_own.at[par], cot_full.at[par, place.t])

    make_masks(masks, segments, half)
    copies.start(masks, masks_out)
    net = (ptable, w1, b1, w2, b2, w3, rates, hidden, filt, filt_spec, e_filt_spec)
    make_filters(tabs, rhs, *net, 0)
    for gather in norms:
        gather.forward(tensor_origins(place))
    ins.forward(dp_origins(place))
    make_filters(tabs, rhs, *net, 1)
    turn_filters(tabs, filt_spec, e_filt_spec)
    copies.start(filt_spec, filt_out)
    copies.start(e_filt_spec, e_filt_out)
    copies.start(hidden, hidden_out)
    for gather in norms:
        gather.arrived()
    ins.arrived()
    copies.take(own_in)
    for which in range(3):
        w_in[which] = jnp.concatenate([in_land[i, which].astype(F32) for i in range(dp)], axis=0).astype(BF16)
    copies.start(w_in, w_in_out)
    copies.start(norm_full, norm_out)
    for par in range(2):
        normed = norm_full[par].reshape(half, -1)
        for which in range(3):
            put_zpre(z, normed, w_in[which], b_in, which, par, half)
    copies.start(z, z_out)
    for gather in cots:
        gather.forward(tensor_origins(place))
    outs.forward(dp_origins(place))
    make_short(short, z, masks, taps, tap_bias, half)

    def convolve(o, source):
        analyse(tabs, rhs, source, spec.at[o], e_spec.at[o], masks)
        copies.start(spec.at[o], spec_out.at[o])
        copies.start(e_spec.at[o], e_spec_out.at[o])
        edges = spectra_product(
            tabs, filt_spec.at[o], e_filt_spec.at[o], spec.at[o], e_spec.at[o], rhs_even, rhs_odd, False, False
        )
        synthesise(tabs, rhs_even, conv.at[o], 0)
        synthesise(tabs, rhs_odd, conv.at[o], 1)
        join(conv.at[o], edges, direct[o : o + 1, :], source, masks, half)
        copies.start(conv.at[o], conv_out.at[o])

    convolve(0, lambda par, at: short[0, par, at, :])
    outs.arrived()
    copies.take(own_out)
    out_rows = tensor_gather(place, sems, out_full.at[place.t], lambda i: out_full.at[i])
    out_rows.start()
    ups.forward(dp_origins(place))
    convolve(1, lambda par, at: short[1, par, at, :] * conv[0, par, at, :])
    out_rows.forward(tensor_origins(place))
    for par in range(2):
        for block in range(tensor):
            values = short[2, par, block * own : (block + 1) * own, :] * conv[1, par, block * own : (block + 1) * own, :]
            gated[par, block] = values.astype(BF16)
    trades = []
    for i in range(1, tensor):
        to = place.t_at(i)
        for par in range(2):
            trades.append(sems.copy(gated.at[par, to], own_gated.at[place.t, par], {"tensor": to}))
    for copy in trades:
        copy.start()
    for par in range(2):
        copies.start(gated.at[par, place.t], own_gated.at[place.t, par])
    copies.start(gated, gated_out)
    downs.forward(dp_origins(place))
    for gather in (*cots, ups, downs, out_rows):
        gather.arrived()
    for copy in trades:
        copy.wait()
    for gather in (*norms, ins, outs, ups, downs, *cots, out_rows):
        gather.finish()
    copies.finish()


MESH = pl.DeviceIdType.MESH


class Place:
    def __init__(self, dp, tensor):
        self.dp, self.tensor = dp, tensor
        self.rows = 4 if dp % 4 == 0 else 1
        self.cols = dp // self.rows
        self.cores = 2 if tensor % 2 == 0 else 1
        self.ys = tensor // self.cores
        self.d, self.t = lax.axis_index("dp"), lax.axis_index("tensor")
        self.a, self.b = self.d // self.cols, lax.rem(self.d, self.cols)
        self.y, self.c = self.t // self.cores, lax.rem(self.t, self.cores)

    def a_at(self, i):
        return lax.rem(self.a + i + self.rows, self.rows) * self.cols + self.b

    def b_at(self, i):
        return self.a * self.cols + lax.rem(self.b + i + self.cols, self.cols)

    def y_at(self, i):
        return lax.rem(self.y + i + self.ys, self.ys) * self.cores + self.c

    def core_peer(self):
        return self.y * self.cores + 1 - self.c

    def t_at(self, i):
        return lax.rem(self.t + i + self.tensor, self.tensor)

    def d_at(self, i):
        return lax.rem(self.d + i + self.dp, self.dp)

    def greet(self, dp=True, all_dp=False):
        peers = [{"tensor": self.t_at(i)} for i in range(1, self.tensor)]
        if all_dp:
            peers += [{"dp": self.d_at(i)} for i in range(1, self.dp)]
        elif dp:
            peers += [{"dp": self.a_at(i)} for i in range(1, self.rows)]
            peers += [{"dp": self.b_at(i)} for i in range(1, self.cols)]
        barrier = pltpu.get_barrier_semaphore()
        for peer in peers:
            pl.semaphore_signal(barrier, inc=1, device_id=peer, device_id_type=MESH)
        self.expected = len(peers)
        return barrier

    def met(self, barrier):
        pl.semaphore_wait(barrier, self.expected)


class Sems:
    def __init__(self, send, recv):
        self.send, self.recv, self.used = send, recv, 0

    def copy(self, src, dst, device):
        i = self.used
        self.used += 1
        return pltpu.make_async_remote_copy(
            src_ref=src, dst_ref=dst, send_sem=self.send.at[i], recv_sem=self.recv.at[i],
            device_id=device, device_id_type=MESH,
        )


class LocalCopies:
    def __init__(self, sems):
        self.sems, self.open, self.used = sems, [], 0

    def start(self, src, dst):
        copy = pltpu.make_async_copy(src, dst, self.sems.at[self.used])
        self.used += 1
        copy.start()
        self.open.append(copy)
        return copy

    def take(self, copy):
        copy.wait()
        self.open = [other for other in self.open if other is not copy]

    def finish(self):
        for copy in self.open:
            copy.wait()


class Gather:
    def __init__(self, sems, source, slot, own, far, near, device):
        self.first = [sems.copy(source, slot(own), device(i)) for i in far]
        self.near = [sems.copy(source, slot(own), device(i)) for i in near]
        self.sems, self.slot, self.device, self.near_ids = sems, slot, device, near
        self.second = []

    def start(self):
        for copy in self.first + self.near:
            copy.start()

    def forward(self, origins, which=None):
        for i, origin in enumerate(origins):
            if which is not None and i not in which:
                continue
            self.first[i].wait_recv()
            for peer in self.near_ids:
                copy = self.sems.copy(self.slot(origin), self.slot(origin), self.device(peer))
                copy.start()
                self.second.append(copy)

    def arrived(self):
        for copy in self.near + self.second:
            copy.wait_recv()

    def finish(self):
        for copy in self.first + self.near + self.second:
            copy.wait_send()


def tensor_gather(place, sems, source, slot):
    near = [place.core_peer()] if place.cores == 2 else []
    return Gather(
        sems, source, slot, place.t, [place.y_at(i) for i in range(1, place.ys)], near, lambda i: {"tensor": i}
    )


def dp_gather(place, sems, source, slot):
    return Gather(
        sems, source, slot, place.d, [place.a_at(i) for i in range(1, place.rows)],
        [place.b_at(i) for i in range(1, place.cols)], lambda i: {"dp": i},
    )


def tensor_origins(place):
    return [place.y_at(-i) for i in range(1, place.ys)]


def dp_origins(place):
    return [place.a_at(-i) for i in range(1, place.rows)]


def gather_counts(dp, tensor):
    cores = 2 if tensor % 2 == 0 else 1
    rows = 4 if dp % 4 == 0 else 1
    far_t, near_t, far_d, near_d = tensor // cores - 1, cores - 1, rows - 1, dp // rows - 1
    return far_t + near_t + far_t * near_t, far_d + near_d + far_d * near_d


def vmem_specs(n):
    return [pl.BlockSpec(memory_space=pltpu.VMEM)] * n


def mix_shapes(half, width, hidden_width, filter_parts=3):
    edge4 = half // 4
    return dict(
        z=((3, 2, half + 2 * PAD, width), F32),
        filt_spec=((2, filter_parts, 2 * half, width), F32),
        e_filt_spec=((2, filter_parts, edge4, width), F32),
        spec=((2, 2, 2 * half, width), F32),
        e_spec=((2, 2, edge4, width), F32),
        conv=((2, 2, half, width), F32),
        hidden=((2, half, hidden_width), F32),
    )


def front_call(dp, tensor, args, count, model, channels, units, rows, half, hidden_width):
    S = jax.ShapeDtypeStruct
    own = count // 2
    shapes = mix_shapes(half, channels, hidden_width)
    land = ((dp, 3, rows, channels), BF16)
    norm, gate, mask = ((2, tensor, own, model), BF16), ((2, tensor, own, channels), BF16), ((2, half + PAD, 8), F32)
    outs = [
        S((3, model, channels), BF16), S((tensor, dp, rows, channels), BF16), S((dp, rows, units), BF16), S((dp, rows, units), BF16),
        S(*norm), S(*norm), S(*gate), S((tensor, 2, own, channels), BF16), S(*mask),
    ] + [S(*v) for v in shapes.values()]
    per_t, per_d = gather_counts(dp, tensor)
    copies = 5 * per_t + 4 * per_d + 2 * (tensor - 1)
    return pl.pallas_call(
        functools.partial(front, dp, tensor),
        out_shape=outs,
        in_specs=vmem_specs(5) + [pl.BlockSpec(memory_space=pl.ANY)] * 4 + vmem_specs(len(args) - 9),
        out_specs=[pl.BlockSpec(memory_space=pl.ANY)] * len(outs),
        scratch_shapes=[
            pltpu.VMEM(*land), pltpu.VMEM((3, model, channels), BF16), pltpu.VMEM((2, own, model), BF16),
            pltpu.VMEM(*norm), pltpu.VMEM(*gate), pltpu.VMEM(*mask),
        ] + [pltpu.VMEM(*v) for v in shapes.values()] + [
            pltpu.VMEM((3, 2, half, channels), F32),
            pltpu.VMEM((3 * half, channels), BF16),
            pltpu.VMEM((6 * half, channels), BF16),
            pltpu.VMEM((6 * half, channels), BF16),
            pltpu.VMEM((half, channels), F32),
            pltpu.SemaphoreType.DMA((copies,)),
            pltpu.SemaphoreType.DMA((copies,)),
            pltpu.SemaphoreType.DMA((24,)),
        ],
        compiler_params=pltpu.CompilerParams(collective_id=0, has_side_effects=True, vmem_limit_bytes=VMEM_LIMIT),
        name="front",
    )(*args)


class Reduce:
    def __init__(self, place, sems, near_out, near_in, far_out, far_in):
        self.place, self.near_in, self.near_out, self.far_in, self.far_out = place, near_in, near_out, far_in, far_out
        peer = {"tensor": place.core_peer()}
        self.near = [sems.copy(near_out.at[i], near_in.at[i], peer) for i in range(place.ys)] if place.cores == 2 else []
        self.far = []
        if far_in is not None:
            self.far = [
                sems.copy(far_out.at[i - 1], far_in.at[i - 1], {"tensor": place.y_at(i)}) for i in range(1, place.ys)
            ]

    def order(self):
        place = self.place
        blocks = []
        for i in [0] + list(range(place.ys - 1, 0, -1)):
            for other in range(place.cores):
                owner = place.y_at(i)
                blocks.append((i, other, owner + (1 - 2 * place.c) if other else owner))
        return blocks

    def combine(self, keep, rows, send=True):
        for i in list(range(1, self.place.ys)) + [0]:
            if self.near:
                self.near[i].wait_recv()

            def work(at, i=i):
                total = keep[i, at, :]
                if self.near:
                    total = total + self.near_in[i, at, :].astype(F32)
                if i:
                    self.far_out[i - 1, at, :] = total.astype(BF16)
                else:
                    keep[0, at, :] = total

            over_rows(rows, 32, work)
            if i and send:
                self.far[i - 1].start()

    def total(self, keep, at):
        out = keep[0, at, :]
        for i in range(self.place.ys - 1):
            out = out + self.far_in[i, at, :].astype(F32)
        return out

    def arrived(self):
        for copy in self.far:
            copy.wait_recv()

    def finish(self):
        for copy in self.near + self.far:
            copy.wait_send()


GELU_SCALE = math.sqrt(2.0 / math.pi)


def gelu_and_slope(x):
    square = x * x
    bent = jnp.tanh(GELU_SCALE * (x + 0.044715 * (x * square)))
    slope = 0.5 * (1.0 + bent) + 0.5 * x * (1.0 - bent * bent) * (GELU_SCALE + (3.0 * 0.044715 * GELU_SCALE) * square)
    return 0.5 * x * (1.0 + bent), slope


def fold8(x):
    return jnp.sum(x.reshape(-1, 8, x.shape[1]), axis=0)


def norm_back(grad, normal, scale, gain):
    k = grad * gain
    return scale * (k - jnp.mean(k, axis=-1, keepdims=True) - normal * jnp.mean(k * normal, axis=-1, keepdims=True))


def put_weight_grad(place, grad, left, right, low):
    rows = low.shape[2]

    @pl.loop(0, 2)
    def _(par):
        flat = lambda ref: ref[par].reshape(-1, ref.shape[-1])
        part = lax.dot_general(flat(left), flat(right), COLUMN_CONTRACT, preferred_element_type=F32)

        @pl.when(par == 0)
        def _():
            grad[...] = part

        @pl.when(par != 0)
        def _():
            grad[...] += part

    for a in range(place.rows):
        for b in range(place.cols):
            start = (a * place.cols + b) * rows
            low[b, a] = grad[start : start + rows, :].astype(BF16)


def middle(
    dp, tensor,
    tokens, cotangent, own_gated, out_full, out_bias, gain, shift, up_all, up_bias, down_all, cot_full,
    down_bias,
    d_mixed_out, d_mix_low, mlp_own, mlp_far, g_down, g_up, row_sums, up_sums,
    mixed, normal, scales, norm_full, d_act, pre, acts, d_pres, keep, near_out, near_in, far_out, far_in, keep_mlp, near_out_mlp, near_in_mlp,
    far_mlp, cot_rows, grad, low_down, low_up, acc, up_acc,
    send, recv, local,
):
    count, model = tokens.shape
    own, units = count // 2, up_all.shape[1]
    place = Place(dp, tensor)
    sems, copies = Sems(send, recv), LocalCopies(local)
    barrier = place.greet(dp=False)
    parity = parity_matrix(count)
    residual = dot(parity, tokens[...])
    total = residual + out_bias[...]
    for block in range(tensor):
        rows = jnp.concatenate([own_gated[block, 0], own_gated[block, 1]], axis=0)
        total += lax.dot_general(rows, out_full[block], ROW_CONTRACT, preferred_element_type=F32)
    mixed[...] = total
    xhat, scale = layer_norm_parts(total)
    normal[...] = xhat
    scales[...] = jnp.broadcast_to(scale, scales.shape)
    low = (xhat * gain[...] + shift[...]).astype(BF16)
    for par in range(2):
        norm_full[par, place.t] = low[par * own : (par + 1) * own]
    place.met(barrier)
    gathers = [
        tensor_gather(place, sems, norm_full.at[par, place.t], lambda i, par=par: norm_full.at[par, i]) for par in range(2)
    ]
    for gather in gathers:
        gather.start()
    reduce = Reduce(place, sems, near_out, near_in, far_out, far_in)
    up_acc[...] = jnp.zeros_like(up_acc)

    def block_rows(ref, owner):
        return jnp.concatenate([ref[0, owner], ref[1, owner]], axis=0)

    @pl.loop(0, tensor)
    def _(block):
        d_act[block] = dot(jnp.concatenate([cot_full[0, block], cot_full[1, block]], axis=0), down_all[...])

    def work_block(step, other, owner):
        pre[...] = dot(block_rows(norm_full, owner), up_all[...]) + up_bias[...]

        for par in range(2):
            def work(at, par=par):
                rows = pl.ds(pl.multiple_of(par * own + at.start, 16), at.size)
                act, slope = gelu_and_slope(pre[rows, :])
                acts[par, owner, at, :] = act.astype(BF16)
                d_pre = (d_act[owner, rows, :] * slope).astype(BF16)
                d_pres[par, owner, at, :] = d_pre
                up_acc[...] += fold8(d_pre.astype(F32))

            over_rows(own, 16, work)
        part = lax.dot_general(block_rows(d_pres, owner), up_all[...], ROW_CONTRACT, preferred_element_type=F32)
        if other:
            near_out[step] = part.astype(BF16)
            reduce.near[step].start()
        else:
            keep[step] = part

    blocks = reduce.order()
    forwarded = False
    for step, other, owner in blocks:
        if step == 0 and other:
            for gather in gathers:
                for copy in gather.near:
                    copy.wait_recv()
        if step and not forwarded:
            for gather in gathers:
                gather.forward(tensor_origins(place))
            forwarded = True
        if step and other:
            for gather in gathers:
                gather.second[place.ys - 1 - step].wait_recv()
        work_block(step, other, owner)
    reduce.combine(keep, count)
    sums = Reduce(place, sems, near_out_mlp, near_in_mlp, far_mlp, None)
    for step, other, owner in blocks[::-1]:
        part = lax.dot_general(block_rows(acts, owner), down_all[...], ROW_CONTRACT, preferred_element_type=F32)
        if other:
            near_out_mlp[step] = part.astype(BF16)
            sums.near[step].start()
        else:
            keep_mlp[step] = part
    put_weight_grad(place, grad, cot_full, acts, low_down)
    copies.start(low_down, g_down)
    put_weight_grad(place, grad, norm_full, d_pres, low_up)
    copies.start(low_up, g_up)
    sums.combine(keep_mlp, count, send=False)
    if place.ys > 1:
        copies.start(far_mlp, mlp_far)

    def own_rows(at):
        mlp_own[at, :] = keep_mlp[0, at, :] + mixed[at, :] + down_bias[...]

    over_rows(count, 32, own_rows)
    up_sums[...] = jnp.sum(up_acc[...], axis=0, keepdims=True)
    for gather in gathers:
        gather.finish()
    acc[...] = jnp.zeros_like(acc)
    cot_rows[...] = dot(parity, cotangent[...])
    reduce.arrived()

    def back(at):
        grad = reduce.total(keep, at)
        xhat = normal[at, :]
        out_grad = cot_rows[at, :]
        d_mixed = out_grad + norm_back(grad, xhat, scales[at, 0:1], gain[...])
        mixed[at, :] = d_mixed
        d_mix_low[at, :] = d_mixed.astype(BF16)
        acc[0:8, :] += fold8(grad * xhat)
        acc[8:16, :] += fold8(grad)
        acc[16:24, :] += fold8(d_mixed)
        acc[24:32, :] += fold8(out_grad)

    over_rows(count, 16, back)
    copies.start(mixed, d_mixed_out)
    for i in range(4):
        row_sums[i : i + 1, :] = jnp.sum(acc[8 * i : 8 * i + 8, :], axis=0, keepdims=True)
    reduce.finish()
    sums.finish()
    copies.finish()


def middle_call(dp, tensor, args):
    S = jax.ShapeDtypeStruct
    count, model = args[0].shape
    units = args[7].shape[1]
    own, cores, rows_d = count // 2, 2 if tensor % 2 == 0 else 1, 4 if dp % 4 == 0 else 1
    ys, farther = tensor // cores, max(tensor // cores - 1, 1)
    rows, low_rows = ((count, model), F32), ((ys, count, model), BF16)
    blocks, norms = ((2, tensor, own, units), BF16), ((2, tensor, own, model), BF16)
    low_grad = ((dp // rows_d, rows_d, model // dp, units), BF16)
    far = ((farther, count, model), BF16)
    per_t, _ = gather_counts(dp, tensor)
    total = 2 * per_t + 3 * ys
    hbm, vmem = pl.BlockSpec(memory_space=pl.ANY), pl.BlockSpec(memory_space=pltpu.VMEM)
    return pl.pallas_call(
        functools.partial(middle, dp, tensor),
        out_shape=[
            S(*rows), S((count, model), BF16), S(*rows), S(*far), S(*low_grad), S(*low_grad), S((4, model), F32), S((1, units), F32),
        ],
        in_specs=vmem_specs(len(args)),
        out_specs=[hbm, vmem, vmem, hbm, hbm, hbm, vmem, vmem],
        scratch_shapes=[
            pltpu.VMEM(*rows), pltpu.VMEM(*rows), pltpu.VMEM((count, 128), F32), pltpu.VMEM(*norms),
            pltpu.VMEM((tensor, count, units), F32), pltpu.VMEM((count, units), F32),
            pltpu.VMEM(*blocks), pltpu.VMEM(*blocks), pltpu.VMEM((ys, count, model), F32),
            pltpu.VMEM(*low_rows), pltpu.VMEM(*low_rows), pltpu.VMEM(*far), pltpu.VMEM(*far),
            pltpu.VMEM((ys, count, model), F32), pltpu.VMEM(*low_rows), pltpu.VMEM(*low_rows), pltpu.VMEM(*far),
            pltpu.VMEM(*rows), pltpu.VMEM((model, units), F32), pltpu.VMEM(*low_grad), pltpu.VMEM(*low_grad),
            pltpu.VMEM((32, model), F32), pltpu.VMEM((8, units), F32),
            pltpu.SemaphoreType.DMA((total,)), pltpu.SemaphoreType.DMA((total,)), pltpu.SemaphoreType.DMA((8,)),
        ],
        compiler_params=pltpu.CompilerParams(collective_id=1, has_side_effects=True, vmem_limit_bytes=VMEM_LIMIT),
        name="middle",
    )(*args)


class WeightReduce:
    def __init__(self, place, sems, low, near_in, keep, far_out, far_in):
        self.place, self.low, self.near_in, self.keep, self.far_out, self.far_in = place, low, near_in, keep, far_out, far_in
        own = lambda i: lax.rem(place.b + i, place.cols)
        self.near = [
            sems.copy(low.at[own(i)], near_in.at[i - 1], {"dp": place.b_at(i)}) for i in range(1, place.cols)
        ]
        self.far = [sems.copy(far_out.at[i - 1], far_in.at[i - 1], {"dp": place.a_at(i)}) for i in range(1, place.rows)]

    def start(self):
        for copy in self.near:
            copy.start()

    def combine(self, own_blocks=None):
        place = self.place
        for copy in self.near:
            copy.wait_recv()
        for i in list(range(1, place.rows)) + [0]:
            a = lax.rem(place.a + i, place.rows)
            total = (self.low[place.b, a] if own_blocks is None else own_blocks[a]).astype(F32)
            for j in range(place.cols - 1):
                total = total + self.near_in[j, a].astype(F32)
            if i:
                self.far_out[i - 1] = total.astype(BF16)
                self.far[i - 1].start()
            else:
                self.keep[...] = total

    def total(self):
        for copy in self.far:
            copy.wait_recv()
        out = self.keep[...]
        for i in range(self.place.rows - 1):
            out = out + self.far_in[i].astype(F32)
        return out

    def finish(self):
        for copy in self.near + self.far:
            copy.wait_send()


def order_matrix(rows):
    half = rows // 2
    at = lax.broadcasted_iota(jnp.int32, (rows, rows), 0)
    wanted = lax.rem(at, 2) * half + at // 2
    return (lax.broadcasted_iota(jnp.int32, (rows, rows), 1) == wanted).astype(F32).astype(BF16)


MISC, TAPS, FIRST, SECOND, BIASES = 0, 8, 24, 64, 128


def rear(
    dp, tensor,
    tokens, d_mix_low, row_sums, up_sums, gain, taps, tap_bias, ptable, w1, b1, w2, b2, w3, rates, direct,
    d_mixed_in, mlp_own, mlp_far, g_down, g_up, norm_in, gated_in, w_in_in, out_in, masks_in,
    wave_in, wave_back_in, twist, e_wave, e_back, e_twist,
    z_in, filt_in, e_filt_in, spec_in, e_spec_in, conv_in, hidden_in,
    output, grad_tokens, o_down, o_up, o_in, o_out, o_small, o_first, o_rows,
    wave, wave_back, masks, z, filt_spec, e_filt_spec, spec, e_spec, conv, hidden,
    d_mixed, norm_full, gated, w_in, w_out, d_mix_full, mlp_in, own_down, own_up,
    short, rhs_even, rhs_odd, g, g_spec, e_g_spec, d_short, d_z, acc, normal, scales,
    down_near, down_keep, down_far, down_land, up_near, up_keep, up_far, up_land,
    in_low, in_near, in_keep, in_far, in_land, out_low, out_near, out_keep, out_far, out_land,
    keep, near_out, near_in, far_out, far_in,
    small, small_in, small_own, small_all, first, first_in, sums, sums_in, wide, wide_in,
    send, recv, local,
):
    tabs = (wave, wave_back, twist, e_wave, e_back, e_twist)
    half, width = z.shape[2] - 2 * PAD, z.shape[3]
    count, model = tokens.shape
    own = count // 2
    d_filt, rhs = conv, rhs_even
    place = Place(dp, tensor)
    sems, copies = Sems(send, recv), LocalCopies(local)
    barrier = place.greet(all_dp=True)
    loads = {}
    for name, src, dst in (
        ("z", z_in, z), ("masks", masks_in, masks), ("out", out_in.at[place.t], w_out), ("conv", conv_in, conv),
        ("gated", gated_in, gated), ("wave", wave_in, wave), ("norm", norm_in, norm_full), ("filt", filt_in.at[:, 0:2], filt_spec),
        ("e_filt", e_filt_in.at[:, 0:2], e_filt_spec), ("wave_back", wave_back_in, wave_back), ("down", g_down.at[place.b], own_down),
        ("up", g_up.at[place.b], own_up), ("spec", spec_in, spec), ("e_spec", e_spec_in, e_spec), ("w_in", w_in_in, w_in),
        ("mixed", d_mixed_in, d_mixed), ("hidden", hidden_in, hidden),
    ):
        loads[name] = copies.start(src, dst)

    def loaded(*names):
        for name in names:
            copies.take(loads[name])

    for par in range(2):
        d_mix_full[par, place.t] = d_mix_low[par * own : (par + 1) * own, :]
    place.met(barrier)
    gathers = [
        tensor_gather(place, sems, d_mix_full.at[par, place.t], lambda i, par=par: d_mix_full.at[par, i]) for par in range(2)
    ]
    for gather in gathers:
        gather.start()
    downs = WeightReduce(place, sems, g_down, down_near, down_keep, down_far, down_land)
    ups = WeightReduce(place, sems, g_up, up_near, up_keep, up_far, up_land)
    ins = [
        WeightReduce(place, sems, in_low.at[p], in_near.at[p], in_keep.at[p], in_far.at[p], in_land.at[p]) for p in range(3)
    ]
    outs = WeightReduce(place, sems, out_low, out_near, out_keep, out_far, out_land)
    downs.start()
    ups.start()
    mlp = [sems.copy(mlp_far.at[i - 1], mlp_in.at[i - 1], {"tensor": place.y_at(i)}) for i in range(1, place.ys)]
    for copy in mlp:
        copy.start()

    xhat, scale = layer_norm_parts(dot(parity_matrix(count), tokens[...]))
    normal[...] = xhat
    scales[...] = jnp.broadcast_to(scale, scales.shape)
    loaded("z", "masks")
    make_short(short, z, masks, taps, tap_bias, half)
    loaded("out", "conv")
    for gather in gathers:
        gather.forward(tensor_origins(place))
    for gather in gathers:
        gather.arrived()
    for par in range(2):
        g[par] = dot(d_mix_full[par].reshape(half, model), w_out[...])

        def gate(at, par=par):
            grad = g[par, at, :]
            d_short[2, par, at, :] = grad * conv[1, par, at, :]
            g[par, at, :] = grad * short[2, par, at, :]

        over_rows(half, CHUNK, gate)

    rows = model // dp

    def weight_blocks(low, total):
        for a in range(place.rows):
            for b in range(place.cols):
                start = (a * place.cols + b) * rows
                low[b, a] = total[start : start + rows, :].astype(BF16)

    def in_grad(p):
        total = None
        for par in range(2):
            part = lax.dot_general(
                norm_full[par].reshape(half, model), d_z[p, par], COLUMN_CONTRACT, preferred_element_type=F32
            )
            total = part if total is None else total + part
        weight_blocks(in_low.at[p], total)
        ins[p].start()

    base = 2 * w3.shape[1]

    def short_back_all(which):
        acc[...] = jnp.zeros_like(acc)
        for par in range(2):
            d_short[which, par, half : half + PAD, :] = jnp.zeros((PAD, width), F32)
        for par in range(2):
            def work(at, par=par):
                size, start = at.size, at.start
                tap = lambda j: taps[j, which : which + 1, :]
                _, here, one, two = short_rows(z, which, par, at, masks, taps, tap_bias)
                grad = d_short[which, par, at, :]
                acc[0:8, :] += fold8(grad)
                acc[8:16, :] += fold8(grad * here)
                acc[16:24, :] += fold8(grad * one)
                acc[24:32, :] += fold8(grad * two)
                rows_on = pl.ds(pl.multiple_of(start, 8), size + PAD)
                same = (d_short[which, par, rows_on, :] * masks[par, rows_on, 4:5])[1 : size + 1]
                if par == 0:
                    other = d_short[which, 1, at, :] * masks[1, at, 3:4]
                else:
                    other = (d_short[which, 0, rows_on, :] * masks[0, rows_on, 3:4])[1 : size + 1]
                low = (tap(0) * grad + tap(1) * other + tap(2) * same).astype(BF16)
                d_z[which, par, at, :] = low
                acc[32:40, :] += fold8(low.astype(F32))

            over_rows(half, CHUNK, work)
        total = lambda i: jnp.sum(acc[8 * i : 8 * i + 8, :], axis=0, keepdims=True)
        small[pl.ds(base + MISC + which, 1), :] = total(4)
        small[pl.ds(base + MISC + 3 + which, 1), :] = total(0)
        for j in range(3):
            small[pl.ds(base + TAPS + 3 * j + which, 1), :] = total(1 + j)

    small[...] = jnp.zeros_like(small)
    loaded("gated")
    total = None
    for par in range(2):
        part = lax.dot_general(
            d_mix_full[par].reshape(half, model), gated[par].reshape(half, width), COLUMN_CONTRACT, preferred_element_type=F32
        )
        total = part if total is None else total + part
    weight_blocks(out_low, total)
    outs.start()
    loaded("wave")

    def spread_back(o, out):
        analyse(tabs, rhs, lambda par, at: g[par, at, :], g_spec, e_g_spec, masks)
        if o:
            loaded("filt", "e_filt", "wave_back")
        edges = spectra_product(
            tabs, filt_spec.at[o], e_filt_spec.at[o], g_spec, e_g_spec, rhs_even, rhs_odd, True, True
        )
        synthesise(tabs, rhs_even, out, 0)
        synthesise(tabs, rhs_odd, out, 1)
        join(out, edges, direct[o : o + 1, :], lambda par, at: g[par, at, :], masks, half)

    def filter_back(o, forward_in):
        edges = spectra_product(tabs, spec.at[o], e_spec.at[o], g_spec, e_g_spec, rhs_even, rhs_odd, True, True)
        synthesise(tabs, rhs_even, d_filt.at[o], 0)
        synthesise(tabs, rhs_odd, d_filt.at[o], 1)
        acc[...] = jnp.zeros_like(acc)
        for par in range(2):
            edge = edges[par].shape[0] // 2
            d_filt[o, par, 0:edge, :] += (edges[par][:edge] + edges[par][edge:]) * (half / edge)

            def work(at, par=par):
                decay = decay_at(par, CHUNK, at.start, rates[o : o + 1, :])
                d_filt[o, par, at, :] = d_filt[o, par, at, :] * (decay * (1.0 / half))
                acc[0:8, :] += fold8(g[par, at, :] * forward_in(par, at))

            over_rows(half, CHUNK, work)
        small[pl.ds(base + MISC + 6 + o, 1), :] = jnp.sum(acc[0:8, :], axis=0, keepdims=True)

    spread_back(1, d_short.at[0])
    short_back_all(2)
    loaded("norm")
    in_grad(2)
    loaded("down")
    downs.combine(own_down)
    loaded("spec", "e_spec")
    filter_back(1, lambda par, at: short[1, par, at, :] * conv[0, par, at, :])
    for par in range(2):
        def gate_again(at, par=par):
            grad = d_short[0, par, at, :]
            d_short[1, par, at, :] = grad * conv[0, par, at, :]
            g[par, at, :] = grad * short[1, par, at, :]

        over_rows(half, CHUNK, gate_again)
    loaded("up")
    ups.combine(own_up)
    spread_back(0, d_short.at[0])
    short_back_all(1)
    in_grad(1)
    outs.combine()
    ins[2].combine()
    short_back_all(0)
    loaded("w_in")
    reduce = Reduce(place, sems, near_out, near_in, far_out, far_in)
    for step, other, owner in reduce.order()[::-1]:
        at = pl.ds(pl.multiple_of(owner * own, 16), own)
        part = None
        for p in range(3):
            rows_p = jnp.concatenate([d_z[p, 0, at, :], d_z[p, 1, at, :]], axis=0)
            term = lax.dot_general(rows_p, w_in[p], ROW_CONTRACT, preferred_element_type=F32)
            part = term if part is None else part + term
        if other:
            near_out[step] = part.astype(BF16)
            reduce.near[step].start()
        else:
            keep[step] = part
    in_grad(0)
    reduce.combine(keep, count)
    ins[1].combine()

    filter_back(0, lambda par, at: short[0, par, at, :])
    loaded("hidden")
    hidden_width = w3.shape[1]
    for o in range(2):
        small[o * hidden_width : (o + 1) * hidden_width, :] = fine_dot(
            hidden[0], d_filt[o, 0], COLUMN_CONTRACT
        ) + fine_dot(hidden[1], d_filt[o, 1], COLUMN_CONTRACT)
    first[...] = jnp.zeros_like(first)
    emb = w1.shape[0]
    f_second, f_bias = 40, 40 + hidden_width
    for par in range(2):
        pre1, h1, pre2 = hidden_layers(ptable[par], w1[...], b1[...], w2[...], b2[...])
        d_h2 = fine_dot(d_filt[0, par], w3[0], ROW_CONTRACT) + fine_dot(d_filt[1, par], w3[1], ROW_CONTRACT)
        d_pre2 = d_h2 * jnp.cos(pre2)
        d_h1 = fine_dot(d_pre2, w2[...], ROW_CONTRACT)
        d_pre1 = d_h1 * jnp.cos(pre1)
        first[0:emb, :] += fine_dot(ptable[par], d_pre1, COLUMN_CONTRACT)
        first[f_second:f_bias, :] += fine_dot(h1, d_pre2, COLUMN_CONTRACT)
        first[f_bias : f_bias + 1, :] += jnp.sum(d_pre1, axis=0, keepdims=True)
        first[f_bias + 1 : f_bias + 2, :] += jnp.sum(d_pre2, axis=0, keepdims=True)
    trades = [sems.copy(first, first_in.at[i - 1], {"tensor": place.t_at(i)}) for i in range(1, tensor)]
    for copy in trades:
        copy.start()
    ins[0].combine()

    sums[...] = jnp.zeros_like(sums)
    loaded("mixed")
    wide[...] = jnp.zeros_like(wide)
    reduce.arrived()

    def back(at):
        grad = reduce.total(keep, at)
        hat = normal[at, :]
        d_input = norm_back(grad, hat, scales[at, 0:1], gain[...])
        near_out[0, at, :] = (d_mixed[at, :] + d_input).astype(BF16)
        wide[0:8, 0:model] += fold8(grad * hat)
        wide[8:16, 0:model] += fold8(grad)

    reduce.finish()
    over_rows(count, 16, back)
    mlp_sum = d_mixed
    mlp_loaded = copies.start(mlp_own, mlp_sum)
    sums[0:1, :] = jnp.sum(wide[0:8, 0:model], axis=0, keepdims=True)
    sums[1:2, :] = jnp.sum(wide[8:16, 0:model], axis=0, keepdims=True)
    sums[2:6, :] = row_sums[...]
    row_trades = [sems.copy(sums, sums_in.at[i - 1], {"tensor": place.t_at(i)}) for i in range(1, tensor)]
    for copy in row_trades:
        copy.start()

    for copy in trades:
        copy.wait_recv()
    total = first[...]
    for i in range(tensor - 1):
        total = total + first_in[i]
    small[base + FIRST : base + FIRST + emb, 0:hidden_width] = total[0:emb]
    small[base + SECOND : base + SECOND + hidden_width, 0:hidden_width] = total[f_second:f_bias]
    small[base + BIASES : base + BIASES + 8, 0:hidden_width] = total[f_bias : f_bias + 8]
    chunk = small_own.shape[0]
    part_of = lambda d: pl.ds(pl.multiple_of(d * chunk, 8), chunk)
    spread = [
        sems.copy(small.at[part_of(place.d_at(i)), :], small_in.at[i - 1], {"dp": place.d_at(i)}) for i in range(1, dp)
    ]
    for copy in spread:
        copy.start()

    for copy in row_trades:
        copy.wait_recv()
    total = sums[...]
    for i in range(tensor - 1):
        total = total + sums_in[i]
    wide[...] = jnp.zeros_like(wide)
    wide[0:8, 0:model] = total
    wide[8:9, 0 : up_sums.shape[1]] = up_sums[...]
    wide_trades = [sems.copy(wide, wide_in.at[i - 1], {"dp": place.d_at(i)}) for i in range(1, dp)]
    for copy in wide_trades:
        copy.start()
    order = order_matrix(count)
    grad_tokens[...] = dot(order, near_out[0]).astype(BF16)
    for copy in spread:
        copy.wait_recv()
    total = small[part_of(place.d), :]
    for i in range(dp - 1):
        total = total + small_in[i]
    small_own[...] = total
    small_all[part_of(place.d), :] = total
    joined = [sems.copy(small_own, small_all.at[part_of(place.d), :], {"dp": place.d_at(i)}) for i in range(1, dp)]
    for copy in joined:
        copy.start()
    for copy in mlp:
        copy.wait_recv()
    copies.take(mlp_loaded)
    total = mlp_sum[...]
    for i in range(place.ys - 1):
        total = total + mlp_in[i].astype(F32)
    output[...] = dot(order, total.astype(BF16)).astype(BF16)
    o_down[...] = downs.total()
    o_up[...] = ups.total()
    o_out[...] = outs.total()
    for p in (2, 1, 0):
        o_in[p] = ins[p].total()
    for copy in wide_trades:
        copy.wait_recv()
    total = wide[...]
    for i in range(dp - 1):
        total = total + wide_in[i]
    o_rows[...] = total
    for copy in joined:
        copy.wait_recv()
    o_small[...] = small_all[0 : base + FIRST, :]
    o_first[...] = small_all[base + FIRST : base + BIASES + 8, 0:hidden_width]
    for group in (trades, row_trades, spread, wide_trades, joined, mlp):
        for copy in group:
            copy.wait_send()
    for group in (*gathers, downs, ups, outs, *ins):
        group.finish()
    copies.finish()


def rear_call(dp, tensor, args, half):
    S = jax.ShapeDtypeStruct
    count, model = args[0].shape
    hidden_width, channels = args[12].shape[1], args[12].shape[2]
    units = args[3].shape[1]
    own, cores, rows_d = count // 2, 2 if tensor % 2 == 0 else 1, 4 if dp % 4 == 0 else 1
    cols_d, ys, rows = dp // rows_d, tensor // cores, model // dp
    farther = max(ys - 1, 1)
    base = 2 * hidden_width
    chunk = -(-(base + BIASES + 8) // (8 * dp)) * 8
    widest = max(model, units)
    shapes = mix_shapes(half, channels, hidden_width, 2)
    V = pltpu.VMEM
    rows_f = ((count, model), F32)
    norm = ((2, tensor, own, model), BF16)
    far = ((farther, count, model), BF16)

    def buffers(lead, last, low):
        first = [V((*lead, cols_d, rows_d, rows, last), BF16)] if low else []
        return first + [
            V((*lead, max(cols_d - 1, 1), rows_d, rows, last), BF16), V((*lead, rows, last), F32),
            V((*lead, max(rows_d - 1, 1), rows, last), BF16), V((*lead, max(rows_d - 1, 1), rows, last), BF16),
        ]

    per_t, _ = gather_counts(dp, tensor)
    copies = 2 * per_t + 6 * (rows_d + cols_d) + 4 * ys + 2 * tensor + 3 * dp
    hbm = pl.BlockSpec(memory_space=pl.ANY)
    n_vmem, n_hbm_first = 15, 12
    specs = vmem_specs(n_vmem) + [hbm] * n_hbm_first + vmem_specs(4) + [hbm] * 7
    wave, wave_back = args[25], args[26]
    return pl.pallas_call(
        functools.partial(rear, dp, tensor),
        out_shape=[
            S((count, model), BF16), S((count, model), BF16), S((rows, units), F32), S((rows, units), F32),
            S((3, rows, channels), F32), S((rows, channels), F32), S((base + FIRST, channels), F32),
            S((BIASES + 8 - FIRST, hidden_width), F32), S((16, widest), F32),
        ],
        in_specs=specs,
        out_specs=vmem_specs(9),
        scratch_shapes=[V(wave.shape, BF16), V(wave_back.shape, BF16), V((2, half + PAD, 8), F32)]
        + [V(*v) for v in shapes.values()]
        + [
            V(*rows_f), V(*norm), V((2, tensor, own, channels), BF16), V((3, model, channels), BF16), V((model, channels), BF16),
            V(*norm), V(*far), V((rows_d, rows, units), BF16), V((rows_d, rows, units), BF16),
            V((3, 2, half, channels), F32), V((6 * half, channels), BF16), V((6 * half, channels), BF16),
            V((2, half, channels), F32), V((2, 2 * half, channels), F32),
            V((2, half // 4, channels), F32), V((3, 2, half + PAD, channels), F32),
            V((3, 2, half, channels), BF16), V((40, channels), F32), V(*rows_f), V((count, 128), F32),
        ]
        + buffers((), units, False) + buffers((), units, False) + buffers((3,), channels, True) + buffers((), channels, True)
        + [V((ys, count, model), F32), V((ys, count, model), BF16), V((ys, count, model), BF16), V(*far), V(*far)]
        + [
            V((dp * chunk, channels), F32), V((dp - 1, chunk, channels), F32), V((chunk, channels), F32),
            V((dp * chunk, channels), F32), V((48 + hidden_width, hidden_width), F32),
            V((tensor - 1, 48 + hidden_width, hidden_width), F32), V((8, model), F32), V((tensor - 1, 8, model), F32),
            V((16, widest), F32), V((dp - 1, 16, widest), F32),
            pltpu.SemaphoreType.DMA((copies,)), pltpu.SemaphoreType.DMA((copies,)), pltpu.SemaphoreType.DMA((20,)),
        ],
        compiler_params=pltpu.CompilerParams(collective_id=2, has_side_effects=True, vmem_limit_bytes=63 * 2**20),
        name="rear",
    )(*args)


def body(
    tokens,
    segment_ids,
    mix_norm_gain,
    mix_norm_bias,
    in_weight,
    in_bias,
    short_weight,
    short_bias,
    filt_in_weight,
    filt_in_bias,
    filt_mid_weight,
    filt_mid_bias,
    filt_out_weight,
    decay_rates,
    long_bias,
    out_weight,
    out_bias,
    mlp_norm_gain,
    mlp_norm_bias,
    up_weight,
    up_bias,
    down_weight,
    down_bias,
    cotangent,
):
    dp, tensor = lax.axis_size("dp"), lax.axis_size("tensor")
    rows, channels, units = in_weight.shape[0], in_weight.shape[2], up_weight.shape[1]
    count, model = tokens.shape[1:]
    length, emb, hidden_width = segment_ids.shape[1], filt_in_weight.shape[0], filt_mid_bias.shape[0]
    half = length // 2
    wave, wave_back, *fixed = (jnp.asarray(t) for t in wave_tables(length))
    net = (
        short_weight, short_bias, jnp.asarray(position_table(length, emb)), filt_in_weight, filt_in_bias[None],
        filt_mid_weight, filt_mid_bias[None], jnp.swapaxes(filt_out_weight, 0, 1), decay_rates, long_bias,
    )
    w_in, out_par, up_par, down_par, cot_par, norm_par, gated_par, own_gated, masks, *kept = front_call(
        dp, tensor,
        (tokens[0], cotangent[0], segment_ids, mix_norm_gain[None], mix_norm_bias[None], jnp.swapaxes(in_weight, 0, 1),
         out_weight, up_weight, down_weight, in_bias) + net + (wave, wave_back, *fixed),
        count, model, channels, units, rows, half, hidden_width,
    )
    out_full = out_par.reshape(tensor, model, channels)
    d_mixed, d_mix_low, mlp_own, mlp_far, g_down, g_up, row_sums, up_sums = middle_call(
        dp, tensor,
        (tokens[0], cotangent[0], own_gated, out_full, out_bias[None], mlp_norm_gain[None], mlp_norm_bias[None],
         up_par.reshape(model, units), up_bias[None], down_par.reshape(model, units), cot_par, down_bias[None]),
    )
    output, grad_tokens, g_down, g_up, g_in, g_out, small, first, wide = rear_call(
        dp, tensor,
        (tokens[0], d_mix_low, row_sums, up_sums, mix_norm_gain[None]) + net
        + (d_mixed, mlp_own, mlp_far, g_down, g_up, norm_par, gated_par, w_in, out_full, masks, wave, wave_back, *fixed, *kept),
        half,
    )
    base = 2 * hidden_width
    misc = small[base : base + 8]
    return (
        output[None],
        grad_tokens[None],
        wide[0, :model],
        wide[1, :model],
        jnp.swapaxes(g_in, 0, 1),
        misc[0:3],
        small[base + TAPS : base + TAPS + 9].reshape(3, 3, channels),
        misc[3:6],
        first[0:emb],
        first[BIASES - FIRST],
        first[SECOND - FIRST : SECOND - FIRST + hidden_width],
        first[BIASES - FIRST + 1],
        jnp.swapaxes(small[0:base].reshape(2, hidden_width, channels), 0, 1),
        misc[6:8],
        g_out,
        wide[4, :model],
        wide[2, :model],
        wide[3, :model],
        g_up,
        wide[8, :units],
        g_down,
        wide[5, :model],
    )


def solution(mesh):
    placed = (
        P("dp", "tensor", None),
        P("dp", None),
        P(),
        P(),
        P("dp", None, "tensor"),
        P(None, "tensor"),
        P(None, None, "tensor"),
        P(None, "tensor"),
        P(),
        P(),
        P(),
        P(),
        P(None, None, "tensor"),
        P(None, "tensor"),
        P(None, "tensor"),
        P("dp", "tensor"),
        P(),
        P(),
        P(),
        P("dp", "tensor"),
        P("tensor"),
        P("dp", "tensor"),
        P(),
        P("dp", "tensor", None),
    )
    return jax.shard_map(
        body,
        mesh=mesh,
        in_specs=placed,
        out_specs=(
            P("dp", "tensor", None),
            P("dp", "tensor", None),
            P(),
            P(),
            P("dp", None, "tensor"),
            P(None, "tensor"),
            P(None, None, "tensor"),
            P(None, "tensor"),
            P(),
            P(),
            P(),
            P(),
            P(None, None, "tensor"),
            P(None, "tensor"),
            P("dp", "tensor"),
            P(),
            P(),
            P(),
            P("dp", "tensor"),
            P("tensor"),
            P("dp", "tensor"),
            P(),
        ),
        check_vma=False,
    )
```

```python
import functools
import math

import jax
import jax.numpy as jnp
import numpy as np
from jax import lax
from jax.experimental import pallas as pl
from jax.experimental.pallas import tpu as pltpu
from jax.sharding import PartitionSpec as P

DOCS = 3
EPSILON = 1e-05
ROW_CONTRACT = (((1,), (1,)), ((), ()))
COLUMN_CONTRACT = (((0,), (0,)), ((), ()))
F32, BF16 = jnp.float32, jnp.bfloat16
CHUNK = 64
VMEM_LIMIT = 58 * 2**20


def half_table(count, period):
    turns = ((2 * np.arange(count)[:, None] + 1) * np.arange(count)[None, :]) % (2 * period)
    angle = turns * (math.pi / period)
    return np.cos(angle), -np.sin(angle)


def three_pass(table):
    high = table.astype(np.float32).astype(jnp.bfloat16)
    low = (table.astype(np.float32) - high.astype(np.float32)).astype(jnp.bfloat16)
    return np.concatenate([high, high, low], axis=1)


def wave_tables(length):
    half, edge = length // 2, length // 32
    real, imag = half_table(half, length)
    whole = np.concatenate([real, imag], axis=0)
    e_real, e_imag = half_table(edge, 2 * edge)
    zero = np.zeros_like(e_real)
    both = np.block([[e_real, zero], [zero, e_real], [e_imag, zero], [zero, e_imag]])
    step = (2 * np.arange(half) + 1) * (math.pi / length)
    e_step = np.tile((2 * np.arange(edge) + 1) * (math.pi / (2 * edge)), 2)
    lanes = lambda turn: np.repeat(np.stack([np.cos(turn), -np.sin(turn)])[:, :, None], 128, axis=2).astype(np.float32)
    twist, e_twist = lanes(step), lanes(e_step)
    return (
        three_pass(whole), three_pass(whole.T), twist,
        three_pass(both), three_pass(both.T), e_twist,
    )


def position_table(length, emb_width):
    bands = (emb_width - 1) // 2
    places = np.arange(length, dtype=np.float32)
    angles = (2.0 * math.pi * places / length).astype(np.float32)
    frequency = np.linspace(0.0001, bands - 1, bands, dtype=np.float32)
    phases = (angles[:, None] * frequency[None, :]).astype(np.float64)
    table = np.concatenate([(places / (length - 1))[:, None], np.cos(phases), -np.sin(phases)], axis=1).astype(np.float32)
    room = np.zeros((length, -(-emb_width // 8) * 8 - emb_width), np.float32)
    table = np.concatenate([table, room], axis=1)
    return np.concatenate([table[0::2], table[1::2]], axis=1)


def over_rows(rows, step, work):
    @pl.loop(0, rows // step)
    def _(i):
        work(pl.ds(pl.multiple_of(i * step, step), step))


def over_rows_marked(rows, step, work):
    work(pl.ds(0, step), True)

    @pl.loop(1, rows // step - 1)
    def _(i):
        work(pl.ds(pl.multiple_of(i * step, step), step), False)

    work(pl.ds(rows - step, step), True)


def parts(x):
    high = x.astype(BF16)
    return high, (x - high.astype(F32)).astype(BF16)


def put_parts(rhs, at, base, block, x):
    high, low = parts(x)
    size = x.shape[0]
    start = at.start if isinstance(at, pl.Slice) else at
    for slot, piece in ((0, high), (1, low), (2, high)):
        rhs[pl.ds(pl.multiple_of(start + (base + slot * block), 16), size), :] = piece


def widen(rows, width):
    whole, rest = divmod(width, 128)
    return jnp.concatenate([rows] * whole + ([rows[:, :rest]] if rest else []), axis=1)


def turned(pair_of, twist, at):
    width = pair_of[0].shape[1]
    return mul(*pair_of, widen(twist[0, at, :], width), widen(twist[1, at, :], width))


def mul(ar, ai, br, bi):
    return ar * br - ai * bi, ar * bi + ai * br


def mul_conj(ar, ai, br, bi):
    return ar * br + ai * bi, ar * bi - ai * br


def blend(f, x, conj):
    (fe, fo, ft), (xe, xo) = f, x
    m = mul_conj if conj else mul
    if conj:
        a, b = m(*fe, *xe), m(*fo, *xo)
        c, d = m(*fe, *xo), m(*ft, *xe)
    else:
        a, b = m(*fe, *xe), m(*ft, *xo)
        c, d = m(*fe, *xo), m(*fo, *xe)
    return (a[0] + b[0], a[1] + b[1]), (c[0] + d[0], c[1] + d[1])


def dot(a, b):
    return jnp.dot(a, b, preferred_element_type=F32)


def analyse(tabs, rhs, source, spec, edge_spec, masks):
    wave, _, _, e_wave, _, _ = tabs
    half, edge = wave.shape[1] // 3, e_wave.shape[1] // 6

    @pl.loop(0, 2)
    def _(par):
        def fill(at, marked):
            rows = source(par, at)
            put_parts(rhs, at, 0, half, rows * masks[par, at, 0:1] if marked else rows)

        over_rows_marked(half, CHUNK, fill)
        spec[par] = dot(wave[...], rhs[0 : 3 * half, :])
        first, last = pl.ds(0, edge), pl.ds(half - edge, edge)
        window = jnp.concatenate(
            [source(par, first) * masks[par, first, 1:2], source(par, last) * masks[par, last, 2:3]], axis=0
        )
        high, low = parts(window)
        edge_spec[par] = dot(e_wave[...], jnp.concatenate([high, low, high], axis=0))


def pair(ref, index, at, half):
    start = at.start
    return ref[index, at, :], ref[index, pl.ds(pl.multiple_of(start + half, 8), at.size), :]


def spectra_product(tabs, filt, e_filt, spec, e_spec, rhs_even, rhs_odd, conj, turn):
    _, wave_back, twist, _, e_back, e_twist = tabs
    half, edge2 = wave_back.shape[1] // 6, e_back.shape[1] // 6

    def get(f, tw, at, n):
        fe, fo = pair(f, 0, at, n), pair(f, 1, at, n)
        ft = turned(fo, tw, at) if turn else pair(f, 2, at, n)
        return fe, fo, ft

    def work(at):
        even, odd = blend(get(filt, twist, at, half), (pair(spec, 0, at, half), pair(spec, 1, at, half)), conj)
        for rhs, (real, imag) in ((rhs_even, even), (rhs_odd, odd)):
            put_parts(rhs, at, 0, 2 * half, real)
            put_parts(rhs, at, half, 2 * half, imag)

    over_rows(half, CHUNK // 2, work)
    at = pl.ds(0, edge2)
    even, odd = blend(get(e_filt, e_twist, at, edge2), (pair(e_spec, 0, at, edge2), pair(e_spec, 1, at, edge2)), conj)
    out = []
    for real, imag in (even, odd):
        high, low = parts(jnp.concatenate([real, imag], axis=0))
        out.append(dot(e_back[...], jnp.concatenate([high, low, high], axis=0)))
    return out


def synthesise(tabs, rhs, out, par):
    out[par, 0 : tabs[1].shape[0], :] = dot(tabs[1][...], rhs[...])


def join(out, edges, direct, source, masks, half):
    for par in range(2):
        def work(at, marked, par=par):
            rows = out[par, at, :]
            out[par, at, :] = (rows * masks[par, at, 0:1] if marked else rows) + direct * source(par, at)

        over_rows_marked(half, CHUNK, work)
        edge = edges[par].shape[0] // 2
        first, last = pl.ds(0, edge), pl.ds(half - edge, edge)
        out[par, first, :] += edges[par][:edge] * masks[par, first, 1:2]
        out[par, last, :] += edges[par][edge:] * masks[par, last, 2:3]


INVERSE_PI = 1.0 / math.pi
PI_HIGH, PI_MID = 3.140625, math.pi - 3.140625
SINE = [(-1.0) ** i / math.factorial(2 * i + 1) for i in range(6)]
COSINE = [(-1.0) ** i / math.factorial(2 * i) for i in range(7)]


def reduced(x):
    turns = jnp.floor(x * INVERSE_PI + 0.5)
    sign = 1.0 - 2.0 * (turns - 2.0 * jnp.floor(0.5 * turns))
    return (x - turns * PI_HIGH) - turns * PI_MID, sign


def poly(square, terms):
    total = terms[-1]
    for term in terms[-2::-1]:
        total = total * square + term
    return total


def sine(x):
    left, sign = reduced(x)
    return sign * left * poly(left * left, SINE)


def sine_cosine(x):
    left, sign = reduced(x)
    square = left * left
    return sign * left * poly(square, SINE), sign * poly(square, COSINE)


def fine_dot(a, b, dims=(((1,), (0,)), ((), ()))):
    (ah, al), (bh, bl) = parts(a), parts(b)
    one = lambda x, y: lax.dot_general(x, y, dims, preferred_element_type=F32)
    return one(ah, bh) + (one(al, bh) + one(ah, bl))


def row_of(ref):
    return ref[...].reshape(1, ref.shape[0])


def flat_rows(land):
    n, rows, width = land.shape
    if rows % 16 == 0:
        return land[...].reshape(n * rows, width)
    return jnp.concatenate([land[i].astype(F32) for i in range(n)], axis=0).astype(BF16)


def twice(rows):
    return jnp.concatenate([rows, rows], axis=1)


def blocks_of(matrix, rows):
    height, width = matrix.shape
    padded = matrix if rows == height else jnp.concatenate([matrix, jnp.zeros((rows - height, width), F32)], axis=0)
    none = jnp.zeros_like(padded)
    return jnp.concatenate(
        [jnp.concatenate([padded, none], axis=1), jnp.concatenate([none, padded], axis=1)], axis=0
    )


def of_parity(rows, par):
    lane = lax.broadcasted_iota(jnp.int32, rows.shape, 1)
    return jnp.where((lane >= rows.shape[1] // 2) == (par == 1), rows, 0.0)


def hidden_layers(ptable, w1, b1, w2, b2):
    pre1 = fine_dot(ptable[...], blocks_of(w1[...], ptable.shape[1] // 2)) + twice(row_of(b1))
    h1, c1 = sine_cosine(pre1)
    pre2 = fine_dot(h1, blocks_of(w2[...], w2.shape[0])) + twice(row_of(b2))
    return h1, c1, pre2


def decay_at(par, rows, start, rates):
    m = lax.broadcasted_iota(jnp.int32, (rows, rates.shape[1]), 0) + start
    return jnp.exp((2 * m + par).astype(F32) * -rates)


def make_filter(tabs, rhs, w3, rates, hidden, filt, filt_spec, e_filt_spec, par, o):
    wave, _, _, e_wave, _, _ = tabs
    half, edge = wave.shape[1] // 3, e_wave.shape[1] // 6
    last = w3[:, o, :]
    filt[...] = fine_dot(of_parity(hidden[...], par), jnp.concatenate([last, last], axis=0))

    def fill(at):
        filt[at, :] = filt[at, :] * decay_at(par, CHUNK, at.start, rates[o : o + 1, :])
        put_parts(rhs, at, 0, half, filt[at, :])

    over_rows(half, CHUNK, fill)
    filt_spec[o, par] = dot(wave[...], rhs[0 : 3 * half, :]) * (1.0 / half)
    window = filt[pl.ds(0, edge), :]
    high, low = parts(jnp.concatenate([window, window], axis=0))
    e_filt_spec[o, par] = dot(e_wave[...], jnp.concatenate([high, low, high], axis=0)) * (1.0 / edge)


def turn_filters(tabs, filt_spec, e_filt_spec):
    wave, _, twist, e_wave, _, e_twist = tabs
    half, edge = wave.shape[1] // 3, e_wave.shape[1] // 6
    for o in range(2):
        def turn(at, o=o):
            real, imag = turned(pair(filt_spec.at[o], 1, at, half), twist, at)
            filt_spec[o, 2, at, :] = real
            filt_spec[o, 2, pl.ds(pl.multiple_of(at.start + half, 8), at.size), :] = imag

        over_rows(half, CHUNK, turn)
        n = 2 * edge
        real, imag = turned(pair(e_filt_spec.at[o], 1, pl.ds(0, n), n), e_twist, pl.ds(0, n))
        e_filt_spec[o, 2] = jnp.concatenate([real, imag], axis=0)


PAD = 8


def short_rows(z, which, par, at, marked, masks, taps, tap_bias):
    size, start = at.size, at.start
    here = z[which, par, pl.ds(pl.multiple_of(start + PAD, 8), size), :]
    wide = pl.ds(pl.multiple_of(start, 8), size + PAD)
    same_before = z[which, par, wide, :][PAD - 1 : PAD - 1 + size]
    if par == 0:
        other = z[which, 1, wide, :][PAD - 1 : PAD - 1 + size]
    else:
        other = z[which, 0, pl.ds(pl.multiple_of(start + PAD, 8), size), :]
    one, two = other, same_before
    if marked:
        one, two = masks[par, at, 3:4] * one, masks[par, at, 4:5] * two
    tap = lambda j: taps[j, which : which + 1, :]
    return tap_bias[which : which + 1, :] + tap(0) * here + tap(1) * one + tap(2) * two, here, one, two


def put_zpre(z, normed, weights, in_bias, which, par, half):
    zero = jnp.zeros((PAD, z.shape[3]), F32)
    z[which, par, 0:PAD, :] = zero
    z[which, par, PAD + half : PAD + half + PAD, :] = zero
    z[which, par, PAD : PAD + half, :] = dot(normed, weights) + in_bias[which : which + 1, :]


def make_short(short, z, masks, taps, tap_bias, half, which):
    for par in range(2):
        def work(at, marked, par=par):
            short[which, par, at, :] = short_rows(z, which, par, at, marked, masks, taps, tap_bias)[0]

        over_rows_marked(half, CHUNK, work)


def layer_norm_parts(values):
    center = jnp.mean(values, axis=-1, keepdims=True)
    centred = values - center
    spread = jnp.mean(centred * centred, axis=-1, keepdims=True)
    scale = lax.rsqrt(spread + EPSILON)
    return centred * scale, scale


def parity_matrix(rows):
    half = rows // 2
    at = lax.broadcasted_iota(jnp.int32, (rows, rows), 0)
    wanted = jnp.where(at < half, 2 * at, 2 * (at - half) + 1)
    return (lax.broadcasted_iota(jnp.int32, (rows, rows), 1) == wanted).astype(F32).astype(BF16)


def make_masks(masks, segments, half):
    seg = segments[...].astype(F32)
    length = seg.shape[1]
    place = lax.broadcasted_iota(jnp.int32, (1, length), 1)
    one = lambda ok: jnp.where(ok, 1.0, 0.0)
    rows = [one(seg == 1.0), one(seg == 0.0), one(seg == 2.0)]
    for j in (1, 2):
        rows.append(jnp.where(place >= j, one(pltpu.roll(seg, j, 1) == seg), 0.0))
    marks = jnp.concatenate(rows + [jnp.zeros((3, length), F32)], axis=0).astype(BF16)
    at = lax.broadcasted_iota(jnp.int32, (half, length), 0)
    column = lax.broadcasted_iota(jnp.int32, (half, length), 1)
    for par in range(2):
        choose = jnp.where(column == 2 * at + par, 1.0, 0.0).astype(BF16)
        masks[par, 0:half, :] = lax.dot_general(choose, marks, ROW_CONTRACT, preferred_element_type=F32)
        masks[par, half : half + PAD, :] = jnp.zeros((PAD, 8), F32)


def front(
    dp, tensor,
    tokens, cotangent, segments, gain, shift, in_shard, b_in, taps, tap_bias, ptable, w1, b1, w2, b2, w3, rates, direct,
    twist, e_wave, e_back, e_twist, out_shard, up_shard, wave_in, wave_back_in,
    w_in_out, out_full, up_all, cot_full, norm_out, gated_out, own_gated, masks_out,
    z_out, filt_out, e_filt_out, spec_out, e_spec_out, conv_out, hidden_out,
    wave, wave_back, in_own, in_land, w_in, cot_own, norm_full, gated, masks, z, filt_spec, e_filt_spec, spec, e_spec, conv, hidden,
    short, rhs, rhs_even, rhs_odd, filt, send, recv, local,
):
    tabs = (wave, wave_back, twist, e_wave, e_back, e_twist)
    half = wave.shape[1] // 3
    count = tokens.shape[1]
    own = count // 2
    place = Place(dp, tensor)
    sems, copies = Sems(send, recv), LocalCopies(local)
    barrier = place.greet()
    wave_loaded, back_loaded = copies.start(wave_in, wave), copies.start(wave_back_in, wave_back)
    origins, t_origins = dp_origins(place), tensor_origins(place)

    for which in range(3):
        in_own[which] = in_shard[:, which, :]
    parity = parity_matrix(count)
    normal, _ = layer_norm_parts(dot(parity, tokens[0]))
    low = (normal * row_of(gain) + row_of(shift)).astype(BF16)
    for par in range(2):
        norm_full[par, place.t] = low[par * own : (par + 1) * own]
    place.met(barrier)

    norms = [
        tensor_gather(place, sems, norm_full.at[par, place.t], lambda i, par=par: norm_full.at[par, i]) for par in range(2)
    ]
    ins = [dp_gather(place, sems, in_own.at[p], lambda i, p=p: in_land.at[p, i]) for p in range(3)]
    outs = dp_gather(place, sems, out_shard, lambda i: out_full.at[place.t, i])
    ups = [
        dp_gather(place, sems, up_shard.at[at], lambda i, at=at: up_all.at[i, at]) for at in row_pieces(up_shard.shape[0])
    ]
    cots = [tensor_gather(place, sems, cot_own.at[par], lambda i, par=par: cot_full.at[par, i]) for par in range(2)]
    for gather in (ins[0], *norms):
        gather.start()
    own_ins = [copies.start(in_own.at[p], in_land.at[p, place.d]) for p in range(3)]
    own_out = copies.start(out_shard, out_full.at[place.t, place.d])
    copies.start(up_shard, up_all.at[place.d])

    shuffled = dot(parity, cotangent[0]).astype(BF16)
    for par in range(2):
        cot_own[par] = shuffled[par * own : (par + 1) * own]
        copies.start(cot_own.at[par], cot_full.at[par, place.t])
    make_masks(masks, segments, half)
    copies.start(masks, masks_out)
    hidden[...] = sine(hidden_layers(ptable, w1, b1, w2, b2)[2])
    copies.start(hidden, hidden_out)
    net = (w3, rates, hidden, filt, filt_spec, e_filt_spec)
    copies.take(wave_loaded)
    make_filter(tabs, rhs, *net, 0, 0)
    ins[0].forward(origins)
    ins[1].start()
    outs.start()
    make_filter(tabs, rhs, *net, 0, 1)
    for gather in norms:
        gather.forward(t_origins)
    make_filter(tabs, rhs, *net, 1, 0)
    ins[1].forward(origins)
    ins[2].start()
    make_filter(tabs, rhs, *net, 1, 1)
    turn_filters(tabs, filt_spec, e_filt_spec)
    copies.start(filt_spec, filt_out)
    copies.start(e_filt_spec, e_filt_out)
    for gather in norms:
        gather.arrived()
    copies.start(norm_full, norm_out)

    def project(which):
        ins[which].arrived()
        copies.take(own_ins[which])
        w_in[which] = flat_rows(in_land.at[which])
        for par in range(2):
            put_zpre(z, norm_full[par].reshape(half, -1), w_in[which], b_in, which, par, half)
        make_short(short, z, masks, taps, tap_bias, half, which)

    def convolve(o, source, between):
        analyse(tabs, rhs, source, spec.at[o], e_spec.at[o], masks)
        copies.start(spec.at[o], spec_out.at[o])
        copies.start(e_spec.at[o], e_spec_out.at[o])
        between()
        edges = spectra_product(
            tabs, filt_spec.at[o], e_filt_spec.at[o], spec.at[o], e_spec.at[o], rhs_even, rhs_odd, False, False
        )
        synthesise(tabs, rhs_even, conv.at[o], 0)
        synthesise(tabs, rhs_odd, conv.at[o], 1)
        join(conv.at[o], edges, direct[o : o + 1, :], source, masks, half)
        copies.start(conv.at[o], conv_out.at[o])

    def early():
        outs.forward(origins)
        ins[2].forward(origins)
        for gather in (*ups, *cots):
            gather.start()

    project(0)
    copies.take(back_loaded)
    convolve(0, lambda par, at: short[0, par, at, :], early)
    project(1)
    outs.arrived()
    copies.take(own_out)
    out_rows = tensor_gather(place, sems, out_full.at[place.t], lambda i: out_full.at[i])
    out_rows.start()

    def more():
        for gather in ups[:-1]:
            gather.forward(origins)
        for gather in cots:
            gather.forward(t_origins)

    convolve(1, lambda par, at: short[1, par, at, :] * conv[0, par, at, :], more)
    project(2)
    copies.start(w_in, w_in_out)
    copies.start(z, z_out)
    for par in range(2):
        for block in range(tensor):
            values = short[2, par, block * own : (block + 1) * own, :] * conv[1, par, block * own : (block + 1) * own, :]
            gated[par, block] = values.astype(BF16)
    trades = []
    for i in range(1, tensor):
        to = place.t_at(i)
        for par in range(2):
            trades.append(sems.copy(gated.at[par, to], own_gated.at[place.t, par], {"tensor": to}))
    for copy in trades:
        copy.start()
    out_rows.forward(t_origins)
    ups[-1].forward(origins)
    for par in range(2):
        copies.start(gated.at[par, place.t], own_gated.at[place.t, par])
    copies.start(gated, gated_out)
    for gather in (*cots, *ups, out_rows):
        gather.arrived()
    for copy in trades:
        copy.wait()
    for gather in (*norms, *ins, outs, *ups, *cots, out_rows):
        gather.finish()
    copies.finish()


MESH = pl.DeviceIdType.MESH


class Place:
    def __init__(self, dp, tensor):
        self.dp, self.tensor = dp, tensor
        self.rows = 4 if dp % 4 == 0 else 1
        self.cols = dp // self.rows
        self.cores = 2 if tensor % 2 == 0 else 1
        self.ys = tensor // self.cores
        self.d, self.t = lax.axis_index("dp"), lax.axis_index("tensor")
        self.a, self.b = self.d // self.cols, lax.rem(self.d, self.cols)
        self.y, self.c = self.t // self.cores, lax.rem(self.t, self.cores)

    def a_at(self, i):
        return lax.rem(self.a + i + self.rows, self.rows) * self.cols + self.b

    def b_at(self, i):
        return self.a * self.cols + lax.rem(self.b + i + self.cols, self.cols)

    def y_at(self, i):
        return lax.rem(self.y + i + self.ys, self.ys) * self.cores + self.c

    def core_peer(self):
        return self.y * self.cores + 1 - self.c

    def t_at(self, i):
        return lax.rem(self.t + i + self.tensor, self.tensor)

    def d_at(self, i):
        return lax.rem(self.d + i + self.dp, self.dp)

    def greet(self, dp=True, all_dp=False):
        peers = [{"tensor": self.t_at(i)} for i in range(1, self.tensor)]
        if all_dp:
            peers += [{"dp": self.d_at(i)} for i in range(1, self.dp)]
        elif dp:
            peers += [{"dp": self.a_at(i)} for i in range(1, self.rows)]
            peers += [{"dp": self.b_at(i)} for i in range(1, self.cols)]
        barrier = pltpu.get_barrier_semaphore()
        for peer in peers:
            pl.semaphore_signal(barrier, inc=1, device_id=peer, device_id_type=MESH)
        self.expected = len(peers)
        return barrier

    def met(self, barrier):
        pl.semaphore_wait(barrier, self.expected)


class Sems:
    def __init__(self, send, recv):
        self.send, self.recv, self.used = send, recv, 0

    def copy(self, src, dst, device):
        i = self.used
        self.used += 1
        return pltpu.make_async_remote_copy(
            src_ref=src, dst_ref=dst, send_sem=self.send.at[i], recv_sem=self.recv.at[i],
            device_id=device, device_id_type=MESH,
        )


class LocalCopies:
    def __init__(self, sems):
        self.sems, self.open, self.used = sems, [], 0

    def start(self, src, dst):
        copy = pltpu.make_async_copy(src, dst, self.sems.at[self.used])
        self.used += 1
        copy.start()
        self.open.append(copy)
        return copy

    def take(self, copy):
        copy.wait()
        self.open = [other for other in self.open if other is not copy]

    def finish(self):
        for copy in self.open:
            copy.wait()


class Gather:
    def __init__(self, sems, source, slot, own, far, near, device):
        self.first = [sems.copy(source, slot(own), device(i)) for i in far]
        self.near = [sems.copy(source, slot(own), device(i)) for i in near]
        self.sems, self.slot, self.device, self.near_ids = sems, slot, device, near
        self.second = []

    def start(self):
        for copy in self.first + self.near:
            copy.start()

    def forward(self, origins, which=None):
        for i, origin in enumerate(origins):
            if which is not None and i not in which:
                continue
            self.first[i].wait_recv()
            for peer in self.near_ids:
                copy = self.sems.copy(self.slot(origin), self.slot(origin), self.device(peer))
                copy.start()
                self.second.append(copy)

    def arrived(self):
        for copy in self.near + self.second:
            copy.wait_recv()

    def finish(self):
        for copy in self.first + self.near + self.second:
            copy.wait_send()


def tensor_gather(place, sems, source, slot):
    near = [place.core_peer()] if place.cores == 2 else []
    return Gather(
        sems, source, slot, place.t, [place.y_at(i) for i in range(1, place.ys)], near, lambda i: {"tensor": i}
    )


def row_pieces(rows):
    count = 2 if rows % 32 == 0 else 1
    return [pl.ds(i * (rows // count), rows // count) for i in range(count)]


def dp_gather(place, sems, source, slot):
    return Gather(
        sems, source, slot, place.d, [place.a_at(i) for i in range(1, place.rows)],
        [place.b_at(i) for i in range(1, place.cols)], lambda i: {"dp": i},
    )


def tensor_origins(place):
    return [place.y_at(-i) for i in range(1, place.ys)]


def dp_origins(place):
    return [place.a_at(-i) for i in range(1, place.rows)]


def gather_counts(dp, tensor):
    cores = 2 if tensor % 2 == 0 else 1
    rows = 4 if dp % 4 == 0 else 1
    far_t, near_t, far_d, near_d = tensor // cores - 1, cores - 1, rows - 1, dp // rows - 1
    return far_t + near_t + far_t * near_t, far_d + near_d + far_d * near_d


def vmem_specs(n):
    return [pl.BlockSpec(memory_space=pltpu.VMEM)] * n


def mix_shapes(half, width, hidden_width, filter_parts=3):
    edge4 = half // 4
    return dict(
        z=((3, 2, half + 2 * PAD, width), F32),
        filt_spec=((2, filter_parts, 2 * half, width), F32),
        e_filt_spec=((2, filter_parts, edge4, width), F32),
        spec=((2, 2, 2 * half, width), F32),
        e_spec=((2, 2, edge4, width), F32),
        conv=((2, 2, half, width), F32),
        hidden=((half, 2 * hidden_width), F32),
    )


def front_call(dp, tensor, args, half, hidden_width):
    S = jax.ShapeDtypeStruct
    V = pltpu.VMEM
    _, count, model = args[0].shape
    rows, _, channels = args[5].shape
    units = args[22].shape[1]
    own = count // 2
    shapes = mix_shapes(half, channels, hidden_width)
    norm, gate, mask = ((2, tensor, own, model), BF16), ((2, tensor, own, channels), BF16), ((2, half + PAD, 8), F32)
    outs = [
        S((3, model, channels), BF16), S((tensor, dp, rows, channels), BF16), S((dp, rows, units), BF16),
        S(*norm), S(*norm), S(*gate), S((tensor, 2, own, channels), BF16), S(*mask),
    ] + [S(*v) for v in shapes.values()]
    per_t, per_d = gather_counts(dp, tensor)
    copies = 5 * per_t + 6 * per_d + 2 * (tensor - 1)
    hbm = pl.BlockSpec(memory_space=pl.ANY)
    return pl.pallas_call(
        functools.partial(front, dp, tensor),
        out_shape=outs,
        in_specs=vmem_specs(21) + [hbm] * 4,
        out_specs=[hbm] * len(outs),
        scratch_shapes=[
            V(args[23].shape, BF16), V(args[24].shape, BF16),
            V((3, rows, channels), BF16), V((3, dp, rows, channels), BF16), V((3, model, channels), BF16),
            V((2, own, model), BF16), V(*norm), V(*gate), V(*mask),
        ] + [V(*v) for v in shapes.values()] + [
            V((3, 2, half, channels), F32), V((3 * half, channels), BF16), V((6 * half, channels), BF16),
            V((6 * half, channels), BF16), V((half, channels), F32),
            pltpu.SemaphoreType.DMA((copies,)), pltpu.SemaphoreType.DMA((copies,)), pltpu.SemaphoreType.DMA((32,)),
        ],
        compiler_params=pltpu.CompilerParams(collective_id=0, has_side_effects=True, vmem_limit_bytes=VMEM_LIMIT),
        name="front",
    )(*args)


class Reduce:
    def __init__(self, place, sems, near_out, near_in, far_out, far_in):
        self.place, self.near_in, self.near_out, self.far_in, self.far_out = place, near_in, near_out, far_in, far_out
        peer = {"tensor": place.core_peer()}
        self.near = [sems.copy(near_out.at[i], near_in.at[i], peer) for i in range(place.ys)] if place.cores == 2 else []
        self.far = []
        if far_in is not None:
            self.far = [
                sems.copy(far_out.at[i - 1], far_in.at[i - 1], {"tensor": place.y_at(i)}) for i in range(1, place.ys)
            ]

    def order(self):
        place = self.place
        blocks = []
        for i in [0] + list(range(place.ys - 1, 0, -1)):
            for other in range(place.cores):
                owner = place.y_at(i)
                blocks.append((i, other, owner + (1 - 2 * place.c) if other else owner))
        return blocks

    def combine(self, keep, rows, send=True):
        for i in list(range(1, self.place.ys)) + [0]:
            if self.near:
                self.near[i].wait_recv()

            def work(at, i=i):
                total = keep[i, at, :]
                if self.near:
                    total = total + self.near_in[i, at, :].astype(F32)
                if i:
                    self.far_out[i - 1, at, :] = total.astype(BF16)
                else:
                    keep[0, at, :] = total

            over_rows(rows, 32, work)
            if i and send:
                self.far[i - 1].start()

    def total(self, keep, at):
        out = keep[0, at, :]
        for i in range(self.place.ys - 1):
            out = out + self.far_in[i, at, :].astype(F32)
        return out

    def arrived(self):
        for copy in self.far:
            copy.wait_recv()

    def finish(self):
        for copy in self.near + self.far:
            copy.wait_send()


GELU_SCALE = math.sqrt(2.0 / math.pi)


def gelu_and_slope(x):
    square = x * x
    bent = jnp.tanh(GELU_SCALE * (x + 0.044715 * (x * square)))
    slope = 0.5 * (1.0 + bent) + 0.5 * x * (1.0 - bent * bent) * (GELU_SCALE + (3.0 * 0.044715 * GELU_SCALE) * square)
    return 0.5 * x * (1.0 + bent), slope


def fold8(x):
    return jnp.sum(x.reshape(-1, 8, x.shape[1]), axis=0)


def norm_back(grad, normal, scale, gain):
    k = grad * gain
    return scale * (k - jnp.mean(k, axis=-1, keepdims=True) - normal * jnp.mean(k * normal, axis=-1, keepdims=True))


def put_weight_grad(place, grad, left, right, low):
    rows = low.shape[2]

    @pl.loop(0, 2)
    def _(par):
        flat = lambda ref: ref[par].reshape(-1, ref.shape[-1])
        part = lax.dot_general(flat(left), flat(right), COLUMN_CONTRACT, preferred_element_type=F32)

        @pl.when(par == 0)
        def _():
            grad[...] = part

        @pl.when(par != 0)
        def _():
            grad[...] += part

    for a in range(place.rows):
        for b in range(place.cols):
            start = (a * place.cols + b) * rows
            low[b, a] = grad[start : start + rows, :].astype(BF16)


def middle(
    dp, tensor,
    tokens, cotangent, own_gated, out_full, out_bias, gain, shift, up_bias, down_bias, up_in, cot_in, down_shard,
    d_mixed_out, d_mix_low, mlp_own, mlp_far, g_down, g_up, row_sums, up_sums,
    up_all, cot_full, mixed, normal, scales, norm_full, down_all, slopes, pre, acts, d_pres, keep, near_out, near_in, far_out, far_in,
    keep_mlp, near_out_mlp, near_in_mlp, far_mlp, cot_rows, grad, low_down, low_up, acc, up_acc,
    send, recv, local,
):
    _, count, model = tokens.shape
    own = count // 2
    place = Place(dp, tensor)
    sems, copies = Sems(send, recv), LocalCopies(local)
    barrier = place.greet()
    up_loaded, cot_loaded = copies.start(up_in, up_all), copies.start(cot_in, cot_full)
    parity = parity_matrix(count)
    total = dot(parity, tokens[0]) + row_of(out_bias)
    cot_rows[...] = dot(parity, cotangent[0])
    place.met(barrier)
    downs = [
        dp_gather(place, sems, down_shard.at[at], lambda i, at=at: down_all.at[i, at])
        for at in row_pieces(down_shard.shape[0])
    ]
    for gather in downs:
        gather.start()
    own_down = copies.start(down_shard, down_all.at[place.d])
    for block in range(tensor):
        rows = jnp.concatenate([own_gated[block, 0], own_gated[block, 1]], axis=0)
        total += lax.dot_general(rows, out_full[block], ROW_CONTRACT, preferred_element_type=F32)
    mixed[...] = total
    xhat, scale = layer_norm_parts(total)
    normal[...] = xhat
    scales[...] = jnp.broadcast_to(scale, scales.shape)
    low = (xhat * row_of(gain) + row_of(shift)).astype(BF16)
    for par in range(2):
        norm_full[par, place.t] = low[par * own : (par + 1) * own]
    gathers = [
        tensor_gather(place, sems, norm_full.at[par, place.t], lambda i, par=par: norm_full.at[par, i]) for par in range(2)
    ]
    for gather in gathers:
        gather.start()
    reduce = Reduce(place, sems, near_out, near_in, far_out, far_in)
    up_acc[...] = jnp.zeros_like(up_acc)

    def block_rows(ref, owner):
        return jnp.concatenate([ref[0, owner], ref[1, owner]], axis=0)

    def forward(owner):
        pre[...] = dot(block_rows(norm_full, owner), up_all[...]) + row_of(up_bias)
        for par in range(2):
            def work(at, par=par):
                rows = pl.ds(pl.multiple_of(par * own + at.start, 16), at.size)
                act, slope = gelu_and_slope(pre[rows, :])
                acts[par, owner, at, :] = act.astype(BF16)
                slopes[owner, rows, :] = slope

            over_rows(own, 16, work)

    def backward(step, other, owner):
        pre[...] = dot(block_rows(cot_full, owner), flat_rows(down_all))
        for par in range(2):
            def work(at, par=par):
                rows = pl.ds(pl.multiple_of(par * own + at.start, 16), at.size)
                d_pre = (pre[rows, :] * slopes[owner, rows, :]).astype(BF16)
                d_pres[par, owner, at, :] = d_pre
                up_acc[...] += fold8(d_pre.astype(F32))

            over_rows(own, 16, work)
        part = lax.dot_general(block_rows(d_pres, owner), up_all[...], ROW_CONTRACT, preferred_element_type=F32)
        if other:
            near_out[step] = part.astype(BF16)
            reduce.near[step].start()
        else:
            keep[step] = part

    blocks = reduce.order()
    copies.take(up_loaded)
    copies.take(cot_loaded)
    forwarded = False
    for step, other, owner in blocks:
        if step == 0 and other:
            for gather in gathers:
                for copy in gather.near:
                    copy.wait_recv()
        if step and not forwarded:
            for gather in downs[:-1]:
                gather.forward(dp_origins(place))
            for gather in gathers:
                gather.forward(tensor_origins(place))
            downs[-1].forward(dp_origins(place))
            forwarded = True
        if step and other:
            for gather in gathers:
                gather.second[place.ys - 1 - step].wait_recv()
        forward(owner)
    if not forwarded:
        for gather in (*gathers, *downs):
            gather.forward(tensor_origins(place) if gather in gathers else dp_origins(place))
    for gather in downs:
        gather.arrived()
    copies.take(own_down)
    for block in blocks[::-1]:
        backward(*block)
    reduce.combine(keep, count)
    sums = Reduce(place, sems, near_out_mlp, near_in_mlp, far_mlp, None)
    for step, other, owner in blocks[::-1]:
        part = lax.dot_general(block_rows(acts, owner), flat_rows(down_all), ROW_CONTRACT, preferred_element_type=F32)
        if other:
            near_out_mlp[step] = part.astype(BF16)
            sums.near[step].start()
        else:
            keep_mlp[step] = part
    put_weight_grad(place, grad, cot_full, acts, low_down)
    copies.start(low_down, g_down)
    put_weight_grad(place, grad, norm_full, d_pres, low_up)
    copies.start(low_up, g_up)
    sums.combine(keep_mlp, count, send=False)
    if place.ys > 1:
        copies.start(far_mlp, mlp_far)

    def own_rows(at):
        mlp_own[at, :] = keep_mlp[0, at, :] + mixed[at, :] + row_of(down_bias)

    over_rows(count, 32, own_rows)
    up_sums[...] = jnp.sum(up_acc[...], axis=0, keepdims=True)
    for gather in (*gathers, *downs):
        gather.finish()
    acc[...] = jnp.zeros_like(acc)
    reduce.arrived()

    def back(at):
        grad_rows = reduce.total(keep, at)
        hat = normal[at, :]
        out_grad = cot_rows[at, :]
        d_mixed = out_grad + norm_back(grad_rows, hat, scales[at, 0:1], row_of(gain))
        mixed[at, :] = d_mixed
        d_mix_low[at, :] = d_mixed.astype(BF16)
        acc[0:8, :] += fold8(grad_rows * hat)
        acc[8:16, :] += fold8(grad_rows)
        acc[16:24, :] += fold8(d_mixed)
        acc[24:32, :] += fold8(out_grad)

    over_rows(count, 64, back)
    copies.start(mixed, d_mixed_out)
    for i in range(4):
        row_sums[i : i + 1, :] = jnp.sum(acc[8 * i : 8 * i + 8, :], axis=0, keepdims=True)
    reduce.finish()
    sums.finish()
    copies.finish()


def middle_call(dp, tensor, args):
    S = jax.ShapeDtypeStruct
    _, count, model = args[0].shape
    units = args[9].shape[1]
    own, cores, rows_d = count // 2, 2 if tensor % 2 == 0 else 1, 4 if dp % 4 == 0 else 1
    ys, farther = tensor // cores, max(tensor // cores - 1, 1)
    rows, low_rows = ((count, model), F32), ((ys, count, model), BF16)
    blocks, norms = ((2, tensor, own, units), BF16), ((2, tensor, own, model), BF16)
    low_grad = ((dp // rows_d, rows_d, model // dp, units), BF16)
    far = ((farther, count, model), BF16)
    per_t, per_d = gather_counts(dp, tensor)
    total = 2 * per_t + 2 * per_d + 3 * ys
    hbm, vmem = pl.BlockSpec(memory_space=pl.ANY), pl.BlockSpec(memory_space=pltpu.VMEM)
    return pl.pallas_call(
        functools.partial(middle, dp, tensor),
        out_shape=[
            S(*rows), S((count, model), BF16), S(*rows), S(*far), S(*low_grad), S(*low_grad), S((4, model), F32), S((1, units), F32),
        ],
        in_specs=vmem_specs(len(args) - 3) + [hbm] * 3,
        out_specs=[hbm, vmem, vmem, hbm, hbm, hbm, vmem, vmem],
        scratch_shapes=[
            pltpu.VMEM((model, units), BF16), pltpu.VMEM(*norms),
            pltpu.VMEM(*rows), pltpu.VMEM(*rows), pltpu.VMEM((count, 128), F32), pltpu.VMEM(*norms),
            pltpu.VMEM((dp, model // dp, units), BF16), pltpu.VMEM((tensor, count, units), F32), pltpu.VMEM((count, units), F32),
            pltpu.VMEM(*blocks), pltpu.VMEM(*blocks), pltpu.VMEM((ys, count, model), F32),
            pltpu.VMEM(*low_rows), pltpu.VMEM(*low_rows), pltpu.VMEM(*far), pltpu.VMEM(*far),
            pltpu.VMEM((ys, count, model), F32), pltpu.VMEM(*low_rows), pltpu.VMEM(*low_rows), pltpu.VMEM(*far),
            pltpu.VMEM(*rows), pltpu.VMEM((model, units), F32), pltpu.VMEM(*low_grad), pltpu.VMEM(*low_grad),
            pltpu.VMEM((32, model), F32), pltpu.VMEM((8, units), F32),
            pltpu.SemaphoreType.DMA((total,)), pltpu.SemaphoreType.DMA((total,)), pltpu.SemaphoreType.DMA((8,)),
        ],
        compiler_params=pltpu.CompilerParams(collective_id=1, has_side_effects=True, vmem_limit_bytes=VMEM_LIMIT),
        name="middle",
    )(*args)


class WeightReduce:
    def __init__(self, place, sems, low, near_in, keep, far_out, far_in):
        self.place, self.low, self.near_in, self.keep, self.far_out, self.far_in = place, low, near_in, keep, far_out, far_in
        own = lambda i: lax.rem(place.b + i, place.cols)
        self.near = [
            sems.copy(low.at[own(i)], near_in.at[i - 1], {"dp": place.b_at(i)}) for i in range(1, place.cols)
        ]
        self.far = [sems.copy(far_out.at[i - 1], far_in.at[i - 1], {"dp": place.a_at(i)}) for i in range(1, place.rows)]

    def start(self):
        for copy in self.near:
            copy.start()

    def combine(self, own_blocks=None):
        place = self.place
        for copy in self.near:
            copy.wait_recv()
        for i in list(range(1, place.rows)) + [0]:
            a = lax.rem(place.a + i, place.rows)
            total = (self.low[place.b, a] if own_blocks is None else own_blocks[a]).astype(F32)
            for j in range(place.cols - 1):
                total = total + self.near_in[j, a].astype(F32)
            if i:
                self.far_out[i - 1] = total.astype(BF16)
                self.far[i - 1].start()
            else:
                self.keep[...] = total

    def total(self):
        for copy in self.far:
            copy.wait_recv()
        out = self.keep[...]
        for i in range(self.place.rows - 1):
            out = out + self.far_in[i].astype(F32)
        return out

    def finish(self):
        for copy in self.near + self.far:
            copy.wait_send()


def order_matrix(rows):
    half = rows // 2
    at = lax.broadcasted_iota(jnp.int32, (rows, rows), 0)
    wanted = lax.rem(at, 2) * half + at // 2
    return (lax.broadcasted_iota(jnp.int32, (rows, rows), 1) == wanted).astype(F32).astype(BF16)


MISC, TAPS, SMALL_ROWS = 0, 8, 24


def rear(
    dp, tensor,
    tokens, d_mix_low, row_sums, up_sums, gain, taps, tap_bias, ptable, w1, b1, w2, b2, w3, rates, direct,
    d_mixed_in, mlp_own, mlp_far, g_down, g_up, norm_in, gated_in, w_in_in, out_in, masks_in,
    wave_in, wave_back_in, twist, e_wave, e_back, e_twist,
    z_in, filt_in, e_filt_in, spec_in, e_spec_in, conv_in, hidden_in,
    output, grad_tokens, o_down, o_up, o_in, o_out, o_small, o_first, o_early, o_late,
    wave, wave_back, masks, z, filt_spec, e_filt_spec, spec, e_spec, conv, hidden,
    d_mixed, norm_full, gated, w_in, w_out, d_mix_full, mlp_in, own_down, own_up,
    short, rhs_even, rhs_odd, g, g_spec, e_g_spec, d_short, d_z, acc, normal, scales,
    down_near, down_keep, down_far, down_land, up_near, up_keep, up_far, up_land,
    in_low, in_near, in_keep, in_far, in_land, out_low, out_near, out_keep, out_far, out_land,
    keep, near_out, near_in, far_out, far_in,
    small, small_in, small_own, small_all, first, first_in, whole, whole_in, whole_own, whole_all,
    early_in, early, early_far, late, late_in, late_sum, late_far, wide,
    send, recv, local,
):
    tabs = (wave, wave_back, twist, e_wave, e_back, e_twist)
    half, width = z.shape[2] - 2 * PAD, z.shape[3]
    _, count, model = tokens.shape
    own = count // 2
    d_filt, rhs = conv, rhs_even
    place = Place(dp, tensor)
    sems, copies = Sems(send, recv), LocalCopies(local)
    barrier = place.greet(all_dp=True)
    loads = {}

    def load(name, src, dst):
        loads[name] = copies.start(src, dst)

    def loaded(*names):
        for name in names:
            copies.take(loads[name])

    load("z", z_in, z)
    load("masks", masks_in, masks)
    load("out", out_in.at[place.t], w_out)
    load("conv", conv_in, conv)
    load("wave", wave_in, wave)
    load("filt", filt_in.at[1, 0:2], filt_spec)
    load("e_filt", e_filt_in.at[1, 0:2], e_filt_spec)
    load("wave_back", wave_back_in, wave_back)
    load("gated", gated_in, gated)
    load("norm", norm_in, norm_full)
    load("down", g_down.at[place.b], own_down)
    load("up", g_up.at[place.b], own_up)
    load("w_in", w_in_in, w_in)
    load("spec", spec_in.at[1], spec)
    load("e_spec", e_spec_in.at[1], e_spec)
    load("hidden", hidden_in, hidden)
    load("mixed", d_mixed_in, d_mixed)
    for par in range(2):
        d_mix_full[par, place.t] = d_mix_low[par * own : (par + 1) * own, :]
    place.met(barrier)
    gathers = [
        tensor_gather(place, sems, d_mix_full.at[par, place.t], lambda i, par=par: d_mix_full.at[par, i]) for par in range(2)
    ]
    for gather in gathers:
        gather.start()
    downs = WeightReduce(place, sems, g_down, down_near, down_keep, down_far, down_land)
    ups = WeightReduce(place, sems, g_up, up_near, up_keep, up_far, up_land)
    ins = [
        WeightReduce(place, sems, in_low.at[p], in_near.at[p], in_keep.at[p], in_far.at[p], in_land.at[p]) for p in range(3)
    ]
    outs = WeightReduce(place, sems, out_low, out_near, out_keep, out_far, out_land)
    mlp = [sems.copy(mlp_far.at[i - 1], mlp_in.at[i - 1], {"tensor": place.y_at(i)}) for i in range(1, place.ys)]
    downs.start()
    early_trades = [sems.copy(row_sums, early_in.at[i - 1], {"tensor": place.t_at(i)}) for i in range(1, tensor)]
    for copy in early_trades:
        copy.start()

    xhat, scale = layer_norm_parts(dot(parity_matrix(count), tokens[0]))
    normal[...] = xhat
    scales[...] = jnp.broadcast_to(scale, scales.shape)
    small[...] = jnp.zeros_like(small)
    loaded("z", "masks")
    for which in range(3):
        make_short(short, z, masks, taps, tap_bias, half, which)
    loaded("out", "conv")
    for gather in gathers:
        gather.forward(tensor_origins(place))
    for copy in mlp:
        copy.start()
    for gather in gathers:
        gather.arrived()
    ups.start()
    for par in range(2):
        g[par] = dot(d_mix_full[par].reshape(half, model), w_out[...])

        def gate(at, par=par):
            grad = g[par, at, :]
            d_short[2, par, at, :] = grad * conv[1, par, at, :]
            short[2, par, at, :] = grad * short[2, par, at, :]

        over_rows(half, CHUNK, gate)

    rows = model // dp

    def weight_grad(reduced, low, left, right):
        total = None
        for par in range(2):
            part = lax.dot_general(left(par), right(par), COLUMN_CONTRACT, preferred_element_type=F32)
            total = part if total is None else total + part
        for a in range(place.rows):
            for b in range(place.cols):
                start = (a * place.cols + b) * rows
                low[b, a] = total[start : start + rows, :].astype(BF16)
        reduced.start()

    def in_grad(p):
        weight_grad(ins[p], in_low.at[p], lambda par: norm_full[par].reshape(half, model), lambda par: d_z[p, par])

    hidden_width = w3.shape[0]
    base = 2 * hidden_width

    def short_back(which):
        acc[...] = jnp.zeros_like(acc)
        for par in range(2):
            d_short[which, par, half : half + PAD, :] = jnp.zeros((PAD, width), F32)
        for par in range(2):
            def work(at, marked, par=par):
                size, start = at.size, at.start
                tap = lambda j: taps[j, which : which + 1, :]
                _, here, one, two = short_rows(z, which, par, at, marked, masks, taps, tap_bias)
                grad = d_short[which, par, at, :]
                acc[0:8, :] += fold8(grad)
                acc[8:16, :] += fold8(grad * here)
                acc[16:24, :] += fold8(grad * one)
                acc[24:32, :] += fold8(grad * two)
                rows_on = pl.ds(pl.multiple_of(start, 8), size + PAD)
                same, other = d_short[which, par, rows_on, :], d_short[which, 1 - par, rows_on, :]
                if marked:
                    same, other = same * masks[par, rows_on, 4:5], other * masks[1 - par, rows_on, 3:4]
                same, other = same[1 : size + 1], other[1 : size + 1] if par else other[:size]
                low = (tap(0) * grad + tap(1) * other + tap(2) * same).astype(BF16)
                d_z[which, par, at, :] = low
                acc[32:40, :] += fold8(low.astype(F32))

            over_rows_marked(half, CHUNK, work)
        total = lambda i: jnp.sum(acc[8 * i : 8 * i + 8, :], axis=0, keepdims=True)
        small[pl.ds(base + MISC + which, 1), :] = total(4)
        small[pl.ds(base + MISC + 3 + which, 1), :] = total(0)
        for j in range(3):
            small[pl.ds(base + TAPS + 3 * j + which, 1), :] = total(1 + j)

    def spread_back(o, source, out):
        analyse(tabs, rhs, source, g_spec.at[o], e_g_spec.at[o], masks)
        loaded("filt", "e_filt")
        edges = spectra_product(
            tabs, filt_spec, e_filt_spec, g_spec.at[o], e_g_spec.at[o], rhs_even, rhs_odd, True, True
        )
        if o:
            load("filt", filt_in.at[0, 0:2], filt_spec)
            load("e_filt", e_filt_in.at[0, 0:2], e_filt_spec)
            loaded("wave_back")
        synthesise(tabs, rhs_even, out, 0)
        synthesise(tabs, rhs_odd, out, 1)
        join(out, edges, direct[o : o + 1, :], source, masks, half)

    def filter_back(o, source, forward_in):
        loaded("spec", "e_spec")
        edges = spectra_product(tabs, spec, e_spec, g_spec.at[o], e_g_spec.at[o], rhs_even, rhs_odd, True, True)
        if o:
            load("spec", spec_in.at[0], spec)
            load("e_spec", e_spec_in.at[0], e_spec)
        acc[...] = jnp.zeros_like(acc)
        for par in range(2):
            def product(at, par=par):
                acc[0:8, :] += fold8(source(par, at) * forward_in(par, at))

            over_rows(half, CHUNK, product)
        small[pl.ds(base + MISC + 6 + o, 1), :] = jnp.sum(acc[0:8, :], axis=0, keepdims=True)
        synthesise(tabs, rhs_even, d_filt.at[o], 0)
        synthesise(tabs, rhs_odd, d_filt.at[o], 1)
        for par in range(2):
            edge = edges[par].shape[0] // 2
            d_filt[o, par, 0:edge, :] += (edges[par][:edge] + edges[par][edge:]) * (half / edge)

            def work(at, par=par):
                decay = decay_at(par, CHUNK, at.start, rates[o : o + 1, :])
                d_filt[o, par, at, :] = d_filt[o, par, at, :] * (decay * (1.0 / half))

            over_rows(half, CHUNK, work)

    grad_one = lambda par, at: short[2, par, at, :]
    grad_zero = lambda par, at: g[par, at, :]
    loaded("wave")
    spread_back(1, grad_one, d_short.at[0])
    for copy in early_trades:
        copy.wait()
    early[...] = jnp.zeros_like(early)
    total = row_sums[...]
    for i in range(tensor - 1):
        total = total + early_in[i]
    early[0:4, 0:model] = total
    early[4:5, 0 : up_sums.shape[1]] = up_sums[...]
    early_moves = [sems.copy(early, early_far.at[i - 1], {"dp": place.d_at(i)}) for i in range(1, dp)]
    for copy in early_moves:
        copy.start()
    loaded("gated")
    weight_grad(
        outs, out_low, lambda par: d_mix_full[par].reshape(half, model), lambda par: gated[par].reshape(half, width)
    )
    for par in range(2):
        def gate_again(at, par=par):
            grad = d_short[0, par, at, :]
            d_short[1, par, at, :] = grad * conv[0, par, at, :]
            g[par, at, :] = grad * short[1, par, at, :]

        over_rows(half, CHUNK, gate_again)
    short_back(2)
    loaded("norm")
    in_grad(2)
    loaded("down")
    downs.combine(own_down)
    spread_back(0, grad_zero, d_short.at[0])
    loaded("up")
    ups.combine(own_up)
    short_back(1)
    short_back(0)
    loaded("w_in")
    reduce = Reduce(place, sems, near_out, near_in, far_out, far_in)
    for step, other, owner in reduce.order()[::-1]:
        at = pl.ds(pl.multiple_of(owner * own, 16), own)
        part = None
        for p in range(3):
            rows_p = jnp.concatenate([d_z[p, 0, at, :], d_z[p, 1, at, :]], axis=0)
            term = lax.dot_general(rows_p, w_in[p], ROW_CONTRACT, preferred_element_type=F32)
            part = term if part is None else part + term
        if other:
            near_out[step] = part.astype(BF16)
            reduce.near[step].start()
        else:
            keep[step] = part
    in_grad(1)
    reduce.combine(keep, count)
    in_grad(0)
    outs.combine()
    ins[2].combine()

    filter_back(1, grad_one, lambda par, at: short[1, par, at, :] * conv[0, par, at, :])
    ins[1].combine()
    filter_back(0, grad_zero, lambda par, at: short[0, par, at, :])
    loaded("hidden")
    h1, c1, pre2 = hidden_layers(ptable, w1, b1, w2, b2)
    lane = lax.broadcasted_iota(jnp.int32, pre2.shape, 1)
    d_h2 = [None, None]
    for o in range(2):
        last = w3[:, o, :]
        both = jnp.concatenate([last, last], axis=0)
        grads = [fine_dot(hidden[...], d_filt[o, par], COLUMN_CONTRACT) for par in range(2)]
        small[o * hidden_width : (o + 1) * hidden_width, :] = grads[0][:hidden_width] + grads[1][hidden_width:]
        for par in range(2):
            term = fine_dot(d_filt[o, par], both, ROW_CONTRACT)
            d_h2[par] = term if o == 0 else d_h2[par] + term
    d_pre2 = jnp.where(lane < hidden_width, d_h2[0], d_h2[1]) * sine_cosine(pre2)[1]
    d_pre1 = fine_dot(d_pre2, blocks_of(w2[...], hidden_width), ROW_CONTRACT) * c1
    across = lambda x, at: x[:at, :hidden_width] + x[at:, hidden_width:]
    g_first = across(fine_dot(ptable[...], d_pre1, COLUMN_CONTRACT), ptable.shape[1] // 2)
    g_second = across(fine_dot(h1, d_pre2, COLUMN_CONTRACT), hidden_width)
    room, tall = first.shape[0] - g_first.shape[0], first.shape[0] - 8
    first[...] = jnp.zeros_like(first)
    first[0 : g_first.shape[0], 0:hidden_width] = g_first
    first[g_first.shape[0] :, 0:hidden_width] = g_second[:room]
    first[0 : hidden_width - room, hidden_width:] = g_second[room:]
    for i, grad in enumerate((d_pre1, d_pre2)):
        row = jnp.sum(grad, axis=0, keepdims=True)
        first[tall + i : tall + i + 1, hidden_width:] = row[:, :hidden_width] + row[:, hidden_width:]
    trades = [sems.copy(first, first_in.at[i - 1], {"tensor": place.t_at(i)}) for i in range(1, tensor)]
    for copy in trades:
        copy.start()
    ins[0].combine()

    whole[...] = jnp.zeros_like(whole)
    for copy in trades:
        copy.wait()
    total = first[...]
    for i in range(tensor - 1):
        total = total + first_in[i]
    whole[0 : first.shape[0], :] = total

    def part_of(own_part, d):
        return pl.ds(pl.multiple_of(d * own_part.shape[0], 8), own_part.shape[0])

    groups = ((small, small_in, small_own, small_all), (whole, whole_in, whole_own, whole_all))
    spread = []
    for full, landed, own_part, _ in groups:
        spread.append(
            [
                sems.copy(full.at[part_of(own_part, place.d_at(i)), :], landed.at[i - 1], {"dp": place.d_at(i)})
                for i in range(1, dp)
            ]
        )
        for copy in spread[-1]:
            copy.start()

    loaded("mixed")
    wide[...] = jnp.zeros_like(wide)
    reduce.arrived()
    reduce.finish()

    def back(at):
        grad = reduce.total(keep, at)
        hat = normal[at, :]
        d_input = norm_back(grad, hat, scales[at, 0:1], row_of(gain))
        near_out[0, at, :] = (d_mixed[at, :] + d_input).astype(BF16)
        wide[0:8, :] += fold8(grad * hat)
        wide[8:16, :] += fold8(grad)

    over_rows(count, 64, back)
    mlp_sum = d_mixed
    mlp_loaded = copies.start(mlp_own, mlp_sum)
    late[0:1, :] = jnp.sum(wide[0:8, :], axis=0, keepdims=True)
    late[1:2, :] = jnp.sum(wide[8:16, :], axis=0, keepdims=True)
    row_trades = [sems.copy(late, late_in.at[i - 1], {"tensor": place.t_at(i)}) for i in range(1, tensor)]
    for copy in row_trades:
        copy.start()
    joined = []
    for copies_of, (full, landed, own_part, everyone) in zip(spread, groups, strict=True):
        for copy in copies_of:
            copy.wait_recv()
        total = full[part_of(own_part, place.d), :]
        for i in range(dp - 1):
            total = total + landed[i]
        own_part[...] = total
        everyone[part_of(own_part, place.d), :] = total
        for i in range(1, dp):
            copy = sems.copy(own_part, everyone.at[part_of(own_part, place.d), :], {"dp": place.d_at(i)})
            copy.start()
            joined.append(copy)
    for copy in row_trades:
        copy.wait_recv()
    total = late[...]
    for i in range(tensor - 1):
        total = total + late_in[i]
    late_sum[...] = total
    late_moves = [sems.copy(late_sum, late_far.at[i - 1], {"dp": place.d_at(i)}) for i in range(1, dp)]
    for copy in late_moves:
        copy.start()
    order = order_matrix(count)
    grad_tokens[0] = dot(order, near_out[0]).astype(BF16)
    for copy in mlp:
        copy.wait_recv()
    copies.take(mlp_loaded)
    total = mlp_sum[...]
    for i in range(place.ys - 1):
        total = total + mlp_in[i].astype(F32)
    output[0] = dot(order, total.astype(BF16)).astype(BF16)
    for copy in early_moves:
        copy.wait_recv()
    total = early[...]
    for i in range(dp - 1):
        total = total + early_far[i]
    o_early[...] = total
    o_down[...] = downs.total()
    o_up[...] = ups.total()
    o_out[...] = outs.total()
    for p in (2, 1, 0):
        o_in[p] = ins[p].total()
    for copy in joined:
        copy.wait_recv()
    o_small[...] = small_all[0 : base + SMALL_ROWS, :]
    o_first[...] = whole_all[0 : first.shape[0], :]
    for copy in late_moves:
        copy.wait_recv()
    total = late_sum[...]
    for i in range(dp - 1):
        total = total + late_far[i]
    o_late[...] = total
    for group in (row_trades, *spread, joined, early_moves, late_moves, mlp):
        for copy in group:
            copy.wait_send()
    for group in (*gathers, downs, ups, outs, *ins):
        group.finish()
    copies.finish()


def finish(
    output_in, tokens_in, down, up, weights, out, small, first, early, late,
    output, grad_tokens, o_mix_gain, o_mix_shift, o_in, o_in_bias, o_taps, o_tap_bias, o_w1, o_b1, o_w2, o_b2, o_w3, o_direct,
    o_out, o_out_bias, o_mlp_gain, o_mlp_shift, o_up, o_up_bias, o_down, o_down_bias,
):
    for src, dst in ((output_in, output), (tokens_in, grad_tokens), (down, o_down), (up, o_up), (out, o_out)):
        dst[...] = src[...]
    for p in range(3):
        o_in[:, p, :] = weights[p]
    model, units = o_mix_gain.shape[0], o_up_bias.shape[0]
    for i, ref in enumerate((o_mix_gain, o_mix_shift)):
        ref[...] = late[i : i + 1, :].reshape(model)
    for i, ref in enumerate((o_mlp_gain, o_mlp_shift, o_out_bias, o_down_bias)):
        ref[...] = early[i : i + 1, 0:model].reshape(model)
    o_up_bias[...] = early[4:5, 0:units].reshape(units)
    hidden_width, emb = o_w2.shape[0], o_w1.shape[0]
    base = 2 * hidden_width
    o_in_bias[...] = small[base + MISC : base + MISC + 3, :]
    o_tap_bias[...] = small[base + MISC + 3 : base + MISC + 6, :]
    o_direct[...] = small[base + MISC + 6 : base + MISC + 8, :]
    for j in range(3):
        o_taps[j] = small[base + TAPS + 3 * j : base + TAPS + 3 * j + 3, :]
    for o in range(2):
        o_w3[:, o, :] = small[o * hidden_width : (o + 1) * hidden_width, :]
    tall = first.shape[0] - 8
    room = hidden_width - tall
    o_w1[...] = first[0:emb, 0:hidden_width]
    o_w2[0:room, :] = first[first.shape[0] - room :, 0:hidden_width]
    o_w2[room:, :] = first[0:tall, hidden_width:]
    for i, ref in enumerate((o_b1, o_b2)):
        ref[...] = first[tall + i : tall + i + 1, hidden_width:].reshape(hidden_width)


def finish_call(args, emb):
    f32 = lambda *shape: jax.ShapeDtypeStruct(shape, F32)
    rows_shape = jax.ShapeDtypeStruct(args[0].shape, BF16)
    model, (rows, units), channels, hidden_width = args[0].shape[2], args[2].shape, args[5].shape[1], args[7].shape[1] // 2
    return pl.pallas_call(
        finish,
        out_shape=[
            rows_shape, rows_shape, f32(model), f32(model), f32(rows, 3, channels), f32(3, channels), f32(3, 3, channels),
            f32(3, channels), f32(emb, hidden_width), f32(hidden_width), f32(hidden_width, hidden_width), f32(hidden_width),
            f32(hidden_width, 2, channels), f32(2, channels), f32(rows, channels), f32(model), f32(model), f32(model),
            f32(rows, units), f32(units), f32(rows, units), f32(model),
        ],
        in_specs=vmem_specs(10),
        out_specs=vmem_specs(22),
        compiler_params=pltpu.CompilerParams(vmem_limit_bytes=VMEM_LIMIT),
        name="finish",
    )(*args)


def rear_call(dp, tensor, args, half):
    S = jax.ShapeDtypeStruct
    _, count, model = args[0].shape
    emb, hidden_width = args[8].shape
    channels, units = args[12].shape[2], args[3].shape[1]
    own, cores, rows_d = count // 2, 2 if tensor % 2 == 0 else 1, 4 if dp % 4 == 0 else 1
    cols_d, ys, rows = dp // rows_d, tensor // cores, model // dp
    farther = max(ys - 1, 1)
    base = 2 * hidden_width
    chunk = -(-(base + SMALL_ROWS) // (8 * dp)) * 8
    packed = (-(-emb // 8) * 8 + hidden_width + 8) // 2
    part = -(-packed // (8 * dp)) * 8
    lanes = 2 * hidden_width
    widest = max(model, units)
    V = pltpu.VMEM
    rows_f = ((count, model), F32)
    norm = ((2, tensor, own, model), BF16)
    far = ((farther, count, model), BF16)

    def buffers(lead, last, low):
        first = [V((*lead, cols_d, rows_d, rows, last), BF16)] if low else []
        return first + [
            V((*lead, max(cols_d - 1, 1), rows_d, rows, last), BF16), V((*lead, rows, last), F32),
            V((*lead, max(rows_d - 1, 1), rows, last), BF16), V((*lead, max(rows_d - 1, 1), rows, last), BF16),
        ]

    per_t, _ = gather_counts(dp, tensor)
    copies = 2 * per_t + 6 * (rows_d + cols_d) + 4 * ys + 3 * tensor + 6 * dp
    hbm = pl.BlockSpec(memory_space=pl.ANY)
    wave, wave_back = args[25], args[26]
    f32 = lambda *shape: S(shape, F32)
    return pl.pallas_call(
        functools.partial(rear, dp, tensor),
        out_shape=[
            S((1, count, model), BF16), S((1, count, model), BF16), f32(rows, units), f32(rows, units), f32(3, rows, channels),
            f32(rows, channels), f32(base + SMALL_ROWS, channels), f32(packed, lanes), f32(8, widest), f32(2, model),
        ],
        in_specs=vmem_specs(15) + [hbm] * 12 + vmem_specs(4) + [hbm] * 7,
        out_specs=vmem_specs(10),
        scratch_shapes=[
            V(wave.shape, BF16), V(wave_back.shape, BF16), V((2, half + PAD, 8), F32), V((3, 2, half + 2 * PAD, channels), F32),
            V((2, 2 * half, channels), F32), V((2, half // 4, channels), F32), V((2, 2 * half, channels), F32),
            V((2, half // 4, channels), F32), V((2, 2, half, channels), F32), V((half, 2 * hidden_width), F32),
            V(*rows_f), V(*norm), V((2, tensor, own, channels), BF16), V((3, model, channels), BF16), V((model, channels), BF16),
            V(*norm), V(*far), V((rows_d, rows, units), BF16), V((rows_d, rows, units), BF16),
            V((3, 2, half, channels), F32), V((6 * half, channels), BF16), V((6 * half, channels), BF16),
            V((2, half, channels), F32), V((2, 2, 2 * half, channels), F32), V((2, 2, half // 4, channels), F32),
            V((3, 2, half + PAD, channels), F32), V((3, 2, half, channels), BF16), V((40, channels), F32), V(*rows_f),
            V((count, 128), F32),
        ]
        + buffers((), units, False) + buffers((), units, False) + buffers((3,), channels, True) + buffers((), channels, True)
        + [V((ys, count, model), F32), V((ys, count, model), BF16), V((ys, count, model), BF16), V(*far), V(*far)]
        + [
            V((dp * chunk, channels), F32), V((dp - 1, chunk, channels), F32), V((chunk, channels), F32),
            V((dp * chunk, channels), F32), V((packed, lanes), F32), V((tensor - 1, packed, lanes), F32),
            V((dp * part, lanes), F32), V((dp - 1, part, lanes), F32), V((part, lanes), F32), V((dp * part, lanes), F32),
            V((tensor - 1, 4, model), F32), V((8, widest), F32), V((dp - 1, 8, widest), F32), V((2, model), F32),
            V((tensor - 1, 2, model), F32), V((2, model), F32), V((dp - 1, 2, model), F32), V((16, model), F32),
            pltpu.SemaphoreType.DMA((copies,)), pltpu.SemaphoreType.DMA((copies,)), pltpu.SemaphoreType.DMA((24,)),
        ],
        compiler_params=pltpu.CompilerParams(collective_id=2, has_side_effects=True, vmem_limit_bytes=63 * 2**20),
        name="rear",
    )(*args)


def body(
    tokens,
    segment_ids,
    mix_norm_gain,
    mix_norm_bias,
    in_weight,
    in_bias,
    short_weight,
    short_bias,
    filt_in_weight,
    filt_in_bias,
    filt_mid_weight,
    filt_mid_bias,
    filt_out_weight,
    decay_rates,
    long_bias,
    out_weight,
    out_bias,
    mlp_norm_gain,
    mlp_norm_bias,
    up_weight,
    up_bias,
    down_weight,
    down_bias,
    cotangent,
):
    dp, tensor = lax.axis_size("dp"), lax.axis_size("tensor")
    units = up_weight.shape[1]
    model = tokens.shape[2]
    length, emb, hidden_width = segment_ids.shape[1], filt_in_weight.shape[0], filt_mid_bias.shape[0]
    half = length // 2
    wave, wave_back, *fixed = (jnp.asarray(t) for t in wave_tables(length))
    net = (
        short_weight, short_bias, jnp.asarray(position_table(length, emb)), filt_in_weight, filt_in_bias, filt_mid_weight,
        filt_mid_bias, filt_out_weight, decay_rates, long_bias,
    )
    w_in, out_par, up_par, cot_par, norm_par, gated_par, own_gated, masks, *kept = front_call(
        dp, tensor,
        (tokens, cotangent, segment_ids, mix_norm_gain, mix_norm_bias, in_weight, in_bias) + net
        + (*fixed, out_weight, up_weight, wave, wave_back),
        half, hidden_width,
    )
    out_full = out_par.reshape(tensor, model, -1)
    d_mixed, d_mix_low, mlp_own, mlp_far, g_down, g_up, row_sums, up_sums = middle_call(
        dp, tensor,
        (tokens, cotangent, own_gated, out_full, out_bias, mlp_norm_gain, mlp_norm_bias, up_bias, down_bias,
         up_par.reshape(model, units), cot_par, down_weight),
    )
    results = rear_call(
            dp, tensor,
            (tokens, d_mix_low, row_sums, up_sums, mix_norm_gain) + net
            + (d_mixed, mlp_own, mlp_far, g_down, g_up, norm_par, gated_par, w_in, out_full, masks, wave, wave_back, *fixed, *kept),
            half,
        )
    return tuple(finish_call(results, emb))


def solution(mesh):
    placed = (
        P("dp", "tensor", None),
        P("dp", None),
        P(),
        P(),
        P("dp", None, "tensor"),
        P(None, "tensor"),
        P(None, None, "tensor"),
        P(None, "tensor"),
        P(),
        P(),
        P(),
        P(),
        P(None, None, "tensor"),
        P(None, "tensor"),
        P(None, "tensor"),
        P("dp", "tensor"),
        P(),
        P(),
        P(),
        P("dp", "tensor"),
        P("tensor"),
        P("dp", "tensor"),
        P(),
        P("dp", "tensor", None),
    )
    return jax.shard_map(
        body,
        mesh=mesh,
        in_specs=placed,
        out_specs=(
            P("dp", "tensor", None),
            P("dp", "tensor", None),
            P(),
            P(),
            P("dp", None, "tensor"),
            P(None, "tensor"),
            P(None, None, "tensor"),
            P(None, "tensor"),
            P(),
            P(),
            P(),
            P(),
            P(None, None, "tensor"),
            P(None, "tensor"),
            P("dp", "tensor"),
            P(),
            P(),
            P(),
            P("dp", "tensor"),
            P("tensor"),
            P("dp", "tensor"),
            P(),
        ),
        check_vma=False,
    )
```

```python
import functools
import math

import jax
import jax.numpy as jnp
import numpy as np
from jax import lax
from jax.experimental import pallas as pl
from jax.experimental.pallas import tpu as pltpu
from jax.sharding import PartitionSpec as P

DOCS = 3
EPSILON = 1e-05
ROW_CONTRACT = (((1,), (1,)), ((), ()))
COLUMN_CONTRACT = (((0,), (0,)), ((), ()))
F32, BF16 = jnp.float32, jnp.bfloat16
CHUNK = 64
VMEM_LIMIT = 58 * 2**20


def half_table(count, period):
    turns = ((2 * np.arange(count)[:, None] + 1) * np.arange(count)[None, :]) % (2 * period)
    angle = turns * (math.pi / period)
    return np.cos(angle), -np.sin(angle)


def three_pass(table):
    high = table.astype(np.float32).astype(jnp.bfloat16)
    low = (table.astype(np.float32) - high.astype(np.float32)).astype(jnp.bfloat16)
    return np.concatenate([high, high, low], axis=1)


def wave_tables(length):
    half, edge = length // 2, length // 32
    real, imag = half_table(half, length)
    whole = np.concatenate([real, imag], axis=0)
    e_real, e_imag = half_table(edge, 2 * edge)
    zero = np.zeros_like(e_real)
    both = np.block([[e_real, zero], [zero, e_real], [e_imag, zero], [zero, e_imag]])
    step = (2 * np.arange(half) + 1) * (math.pi / length)
    e_step = np.tile((2 * np.arange(edge) + 1) * (math.pi / (2 * edge)), 2)
    lanes = lambda turn: np.repeat(np.stack([np.cos(turn), -np.sin(turn)])[:, :, None], 128, axis=2).astype(np.float32)
    twist, e_twist = lanes(step), lanes(e_step)
    return (
        three_pass(whole), three_pass(whole.T), twist,
        three_pass(both), three_pass(both.T), e_twist,
    )


def position_table(length, emb_width):
    bands = (emb_width - 1) // 2
    places = np.arange(length, dtype=np.float32)
    angles = (2.0 * math.pi * places / length).astype(np.float32)
    frequency = np.linspace(0.0001, bands - 1, bands, dtype=np.float32)
    phases = (angles[:, None] * frequency[None, :]).astype(np.float64)
    table = np.concatenate([(places / (length - 1))[:, None], np.cos(phases), -np.sin(phases)], axis=1).astype(np.float32)
    room = np.zeros((length, -(-emb_width // 8) * 8 - emb_width), np.float32)
    table = np.concatenate([table, room], axis=1)
    return np.concatenate([table[0::2], table[1::2]], axis=1)


def over_rows(rows, step, work):
    @pl.loop(0, rows // step)
    def _(i):
        work(pl.ds(pl.multiple_of(i * step, step), step))


def over_rows_marked(rows, step, work):
    work(pl.ds(0, step), True)

    @pl.loop(1, rows // step - 1)
    def _(i):
        work(pl.ds(pl.multiple_of(i * step, step), step), False)

    work(pl.ds(rows - step, step), True)


def parts(x):
    high = x.astype(BF16)
    return high, (x - high.astype(F32)).astype(BF16)


def put_parts(rhs, at, base, block, x):
    high, low = parts(x)
    size = x.shape[0]
    start = at.start if isinstance(at, pl.Slice) else at
    for slot, piece in ((0, high), (1, low), (2, high)):
        rhs[pl.ds(pl.multiple_of(start + (base + slot * block), 16), size), :] = piece


def widen(rows, width):
    whole, rest = divmod(width, 128)
    return jnp.concatenate([rows] * whole + ([rows[:, :rest]] if rest else []), axis=1)


def turned(pair_of, twist, at):
    width = pair_of[0].shape[1]
    return mul(*pair_of, widen(twist[0, at, :], width), widen(twist[1, at, :], width))


def mul(ar, ai, br, bi):
    return ar * br - ai * bi, ar * bi + ai * br


def mul_conj(ar, ai, br, bi):
    return ar * br + ai * bi, ar * bi - ai * br


def blend(f, x, conj):
    (fe, fo, ft), (xe, xo) = f, x
    m = mul_conj if conj else mul
    if conj:
        a, b = m(*fe, *xe), m(*fo, *xo)
        c, d = m(*fe, *xo), m(*ft, *xe)
    else:
        a, b = m(*fe, *xe), m(*ft, *xo)
        c, d = m(*fe, *xo), m(*fo, *xe)
    return (a[0] + b[0], a[1] + b[1]), (c[0] + d[0], c[1] + d[1])


def dot(a, b):
    return jnp.dot(a, b, preferred_element_type=F32)


def analyse(tabs, rhs, source, spec, edge_spec, masks):
    wave, _, _, e_wave, _, _ = tabs
    half, edge = wave.shape[1] // 3, e_wave.shape[1] // 6

    @pl.loop(0, 2)
    def _(par):
        def fill(at, marked):
            rows = source(par, at)
            put_parts(rhs, at, 0, half, rows * masks[par, at, 0:1] if marked else rows)

        over_rows_marked(half, CHUNK, fill)
        spec[par] = dot(wave[...], rhs[0 : 3 * half, :])
        first, last = pl.ds(0, edge), pl.ds(half - edge, edge)
        window = jnp.concatenate(
            [source(par, first) * masks[par, first, 1:2], source(par, last) * masks[par, last, 2:3]], axis=0
        )
        high, low = parts(window)
        edge_spec[par] = dot(e_wave[...], jnp.concatenate([high, low, high], axis=0))


def pair(ref, index, at, half):
    start = at.start
    return ref[index, at, :], ref[index, pl.ds(pl.multiple_of(start + half, 8), at.size), :]


def spectra_product(tabs, filt, e_filt, spec, e_spec, rhs_even, rhs_odd, conj, turn):
    _, wave_back, twist, _, e_back, e_twist = tabs
    half, edge2 = wave_back.shape[1] // 6, e_back.shape[1] // 6

    def get(f, tw, at, n):
        fe, fo = pair(f, 0, at, n), pair(f, 1, at, n)
        ft = turned(fo, tw, at) if turn else pair(f, 2, at, n)
        return fe, fo, ft

    def work(at):
        even, odd = blend(get(filt, twist, at, half), (pair(spec, 0, at, half), pair(spec, 1, at, half)), conj)
        for rhs, (real, imag) in ((rhs_even, even), (rhs_odd, odd)):
            put_parts(rhs, at, 0, 2 * half, real)
            put_parts(rhs, at, half, 2 * half, imag)

    over_rows(half, CHUNK // 2, work)
    at = pl.ds(0, edge2)
    even, odd = blend(get(e_filt, e_twist, at, edge2), (pair(e_spec, 0, at, edge2), pair(e_spec, 1, at, edge2)), conj)
    out = []
    for real, imag in (even, odd):
        high, low = parts(jnp.concatenate([real, imag], axis=0))
        out.append(dot(e_back[...], jnp.concatenate([high, low, high], axis=0)))
    return out


def synthesise(tabs, rhs, out, par):
    out[par, 0 : tabs[1].shape[0], :] = dot(tabs[1][...], rhs[...])


def join(out, edges, direct, source, masks, half):
    for par in range(2):
        def work(at, marked, par=par):
            rows = out[par, at, :]
            out[par, at, :] = (rows * masks[par, at, 0:1] if marked else rows) + direct * source(par, at)

        over_rows_marked(half, CHUNK, work)
        edge = edges[par].shape[0] // 2
        first, last = pl.ds(0, edge), pl.ds(half - edge, edge)
        out[par, first, :] += edges[par][:edge] * masks[par, first, 1:2]
        out[par, last, :] += edges[par][edge:] * masks[par, last, 2:3]


INVERSE_PI = 1.0 / math.pi
PI_HIGH, PI_MID = 3.140625, math.pi - 3.140625
SINE = [(-1.0) ** i / math.factorial(2 * i + 1) for i in range(6)]
COSINE = [(-1.0) ** i / math.factorial(2 * i) for i in range(7)]


def reduced(x):
    turns = jnp.floor(x * INVERSE_PI + 0.5)
    sign = 1.0 - 2.0 * (turns - 2.0 * jnp.floor(0.5 * turns))
    return (x - turns * PI_HIGH) - turns * PI_MID, sign


def poly(square, terms):
    total = terms[-1]
    for term in terms[-2::-1]:
        total = total * square + term
    return total


def sine(x):
    left, sign = reduced(x)
    return sign * left * poly(left * left, SINE)


def sine_cosine(x):
    left, sign = reduced(x)
    square = left * left
    return sign * left * poly(square, SINE), sign * poly(square, COSINE)


def fine_dot(a, b, dims=(((1,), (0,)), ((), ()))):
    (ah, al), (bh, bl) = parts(a), parts(b)
    one = lambda x, y: lax.dot_general(x, y, dims, preferred_element_type=F32)
    return one(ah, bh) + (one(al, bh) + one(ah, bl))


def row_of(ref):
    return ref[...].reshape(1, ref.shape[0])


def flat_rows(land):
    n, rows, width = land.shape
    if rows % 16 == 0:
        return land[...].reshape(n * rows, width)
    return jnp.concatenate([land[i].astype(F32) for i in range(n)], axis=0).astype(BF16)


def twice(rows):
    return jnp.concatenate([rows, rows], axis=1)


def blocks_of(matrix, rows):
    height, width = matrix.shape
    padded = matrix if rows == height else jnp.concatenate([matrix, jnp.zeros((rows - height, width), F32)], axis=0)
    none = jnp.zeros_like(padded)
    return jnp.concatenate(
        [jnp.concatenate([padded, none], axis=1), jnp.concatenate([none, padded], axis=1)], axis=0
    )


def of_parity(rows, par):
    lane = lax.broadcasted_iota(jnp.int32, rows.shape, 1)
    return jnp.where((lane >= rows.shape[1] // 2) == (par == 1), rows, 0.0)


def hidden_layers(ptable, w1, b1, w2, b2):
    pre1 = fine_dot(ptable[...], blocks_of(w1[...], ptable.shape[1] // 2)) + twice(row_of(b1))
    h1, c1 = sine_cosine(pre1)
    pre2 = fine_dot(h1, blocks_of(w2[...], w2.shape[0])) + twice(row_of(b2))
    return h1, c1, pre2


def decay_at(par, rows, start, rates):
    m = lax.broadcasted_iota(jnp.int32, (rows, rates.shape[1]), 0) + start
    return jnp.exp((2 * m + par).astype(F32) * -rates)


def make_filter(tabs, rhs, w3, rates, hidden, filt, filt_spec, e_filt_spec, par, o):
    wave, _, _, e_wave, _, _ = tabs
    half, edge = wave.shape[1] // 3, e_wave.shape[1] // 6
    last = w3[:, o, :]
    filt[...] = fine_dot(of_parity(hidden[...], par), jnp.concatenate([last, last], axis=0))

    def fill(at):
        filt[at, :] = filt[at, :] * decay_at(par, CHUNK, at.start, rates[o : o + 1, :])
        put_parts(rhs, at, 0, half, filt[at, :])

    over_rows(half, CHUNK, fill)
    filt_spec[o, par] = dot(wave[...], rhs[0 : 3 * half, :]) * (1.0 / half)
    window = filt[pl.ds(0, edge), :]
    high, low = parts(jnp.concatenate([window, window], axis=0))
    e_filt_spec[o, par] = dot(e_wave[...], jnp.concatenate([high, low, high], axis=0)) * (1.0 / edge)


def turn_filters(tabs, filt_spec, e_filt_spec):
    wave, _, twist, e_wave, _, e_twist = tabs
    half, edge = wave.shape[1] // 3, e_wave.shape[1] // 6
    for o in range(2):
        def turn(at, o=o):
            real, imag = turned(pair(filt_spec.at[o], 1, at, half), twist, at)
            filt_spec[o, 2, at, :] = real
            filt_spec[o, 2, pl.ds(pl.multiple_of(at.start + half, 8), at.size), :] = imag

        over_rows(half, CHUNK, turn)
        n = 2 * edge
        real, imag = turned(pair(e_filt_spec.at[o], 1, pl.ds(0, n), n), e_twist, pl.ds(0, n))
        e_filt_spec[o, 2] = jnp.concatenate([real, imag], axis=0)


PAD = 8


def short_rows(z, which, par, at, marked, masks, taps, tap_bias):
    size, start = at.size, at.start
    here = z[which, par, pl.ds(pl.multiple_of(start + PAD, 8), size), :]
    wide = pl.ds(pl.multiple_of(start, 8), size + PAD)
    same_before = z[which, par, wide, :][PAD - 1 : PAD - 1 + size]
    if par == 0:
        other = z[which, 1, wide, :][PAD - 1 : PAD - 1 + size]
    else:
        other = z[which, 0, pl.ds(pl.multiple_of(start + PAD, 8), size), :]
    one, two = other, same_before
    if marked:
        one, two = masks[par, at, 3:4] * one, masks[par, at, 4:5] * two
    tap = lambda j: taps[j, which : which + 1, :]
    return tap_bias[which : which + 1, :] + tap(0) * here + tap(1) * one + tap(2) * two, here, one, two


def put_zpre(z, normed, weights, in_bias, which, par, half):
    zero = jnp.zeros((PAD, z.shape[3]), F32)
    z[which, par, 0:PAD, :] = zero
    z[which, par, PAD + half : PAD + half + PAD, :] = zero
    z[which, par, PAD : PAD + half, :] = dot(normed, weights) + in_bias[which : which + 1, :]


def make_short(short, z, masks, taps, tap_bias, half, which):
    for par in range(2):
        def work(at, marked, par=par):
            short[which, par, at, :] = short_rows(z, which, par, at, marked, masks, taps, tap_bias)[0]

        over_rows_marked(half, CHUNK, work)


def layer_norm_parts(values):
    center = jnp.mean(values, axis=-1, keepdims=True)
    centred = values - center
    spread = jnp.mean(centred * centred, axis=-1, keepdims=True)
    scale = lax.rsqrt(spread + EPSILON)
    return centred * scale, scale


def parity_matrix(rows):
    half = rows // 2
    at = lax.broadcasted_iota(jnp.int32, (rows, rows), 0)
    wanted = jnp.where(at < half, 2 * at, 2 * (at - half) + 1)
    return (lax.broadcasted_iota(jnp.int32, (rows, rows), 1) == wanted).astype(F32).astype(BF16)


def make_masks(masks, segments, half):
    seg = segments[...].astype(F32)
    length = seg.shape[1]
    place = lax.broadcasted_iota(jnp.int32, (1, length), 1)
    one = lambda ok: jnp.where(ok, 1.0, 0.0)
    rows = [one(seg == 1.0), one(seg == 0.0), one(seg == 2.0)]
    for j in (1, 2):
        rows.append(jnp.where(place >= j, one(pltpu.roll(seg, j, 1) == seg), 0.0))
    marks = jnp.concatenate(rows + [jnp.zeros((3, length), F32)], axis=0).astype(BF16)
    at = lax.broadcasted_iota(jnp.int32, (half, length), 0)
    column = lax.broadcasted_iota(jnp.int32, (half, length), 1)
    for par in range(2):
        choose = jnp.where(column == 2 * at + par, 1.0, 0.0).astype(BF16)
        masks[par, 0:half, :] = lax.dot_general(choose, marks, ROW_CONTRACT, preferred_element_type=F32)
        masks[par, half : half + PAD, :] = jnp.zeros((PAD, 8), F32)


def front(
    dp, tensor,
    tokens, cotangent, segments, gain, shift, in_shard, b_in, taps, tap_bias, ptable, w1, b1, w2, b2, w3, rates, direct,
    twist, e_wave, e_back, e_twist, out_shard, up_shard, wave_in, wave_back_in,
    w_in_out, out_full, up_all, cot_full, norm_out, gated_out, own_gated, masks_out,
    z_out, filt_out, e_filt_out, spec_out, e_spec_out, conv_out, hidden_out,
    wave, wave_back, in_own, in_land, w_in, cot_own, norm_full, gated, masks, z, filt_spec, e_filt_spec, spec, e_spec, conv, hidden,
    short, rhs, rhs_even, rhs_odd, filt, send, recv, local,
):
    tabs = (wave, wave_back, twist, e_wave, e_back, e_twist)
    half = wave.shape[1] // 3
    count = tokens.shape[1]
    own = count // 2
    place = Place(dp, tensor)
    sems, copies = Sems(send, recv), LocalCopies(local)
    barrier = place.greet()
    wave_loaded, back_loaded = copies.start(wave_in, wave), copies.start(wave_back_in, wave_back)
    origins, t_origins = dp_origins(place), tensor_origins(place)

    for which in range(3):
        in_own[which] = in_shard[:, which, :]
    parity = parity_matrix(count)
    normal, _ = layer_norm_parts(dot(parity, tokens[0]))
    low = (normal * row_of(gain) + row_of(shift)).astype(BF16)
    for par in range(2):
        norm_full[par, place.t] = low[par * own : (par + 1) * own]
    place.met(barrier)

    norms = [
        tensor_gather(place, sems, norm_full.at[par, place.t], lambda i, par=par: norm_full.at[par, i]) for par in range(2)
    ]
    ins = [dp_gather(place, sems, in_own.at[p], lambda i, p=p: in_land.at[p, i]) for p in range(3)]
    outs = dp_gather(place, sems, out_shard, lambda i: out_full.at[place.t, i])
    ups = [
        dp_gather(place, sems, up_shard.at[at], lambda i, at=at: up_all.at[i, at]) for at in row_pieces(up_shard.shape[0])
    ]
    cots = [tensor_gather(place, sems, cot_own.at[par], lambda i, par=par: cot_full.at[par, i]) for par in range(2)]
    for gather in (ins[0], *norms, outs):
        gather.start()
    own_ins = [copies.start(in_own.at[p], in_land.at[p, place.d]) for p in range(3)]
    own_out = copies.start(out_shard, out_full.at[place.t, place.d])
    copies.start(up_shard, up_all.at[place.d])

    shuffled = dot(parity, cotangent[0]).astype(BF16)
    for par in range(2):
        cot_own[par] = shuffled[par * own : (par + 1) * own]
        copies.start(cot_own.at[par], cot_full.at[par, place.t])
    make_masks(masks, segments, half)
    copies.start(masks, masks_out)
    hidden[...] = sine(hidden_layers(ptable, w1, b1, w2, b2)[2])
    copies.start(hidden, hidden_out)
    net = (w3, rates, hidden, filt, filt_spec, e_filt_spec)
    copies.take(wave_loaded)
    make_filter(tabs, rhs, *net, 0, 0)
    ins[0].forward(origins)
    ins[1].start()
    outs.forward(origins)
    make_filter(tabs, rhs, *net, 0, 1)
    for gather in norms:
        gather.forward(t_origins)
    make_filter(tabs, rhs, *net, 1, 0)
    ins[1].forward(origins)
    for gather in (ins[2], *ups[:-1]):
        gather.start()
    outs.arrived()
    copies.take(own_out)
    out_rows = tensor_gather(place, sems, out_full.at[place.t], lambda i: out_full.at[i])
    for gather in (out_rows, *cots):
        gather.start()
    make_filter(tabs, rhs, *net, 1, 1)
    turn_filters(tabs, filt_spec, e_filt_spec)
    copies.start(filt_spec, filt_out)
    copies.start(e_filt_spec, e_filt_out)
    for gather in norms:
        gather.arrived()
    copies.start(norm_full, norm_out)

    def project(which):
        ins[which].arrived()
        copies.take(own_ins[which])
        w_in[which] = flat_rows(in_land.at[which])
        for par in range(2):
            put_zpre(z, norm_full[par].reshape(half, -1), w_in[which], b_in, which, par, half)
        make_short(short, z, masks, taps, tap_bias, half, which)

    def convolve(o, source, between):
        analyse(tabs, rhs, source, spec.at[o], e_spec.at[o], masks)
        copies.start(spec.at[o], spec_out.at[o])
        copies.start(e_spec.at[o], e_spec_out.at[o])
        between()
        edges = spectra_product(
            tabs, filt_spec.at[o], e_filt_spec.at[o], spec.at[o], e_spec.at[o], rhs_even, rhs_odd, False, False
        )
        synthesise(tabs, rhs_even, conv.at[o], 0)
        synthesise(tabs, rhs_odd, conv.at[o], 1)
        join(conv.at[o], edges, direct[o : o + 1, :], source, masks, half)
        copies.start(conv.at[o], conv_out.at[o])

    project(0)
    copies.take(back_loaded)
    convolve(0, lambda par, at: short[0, par, at, :], lambda: None)
    ins[2].forward(origins)
    out_rows.forward(t_origins)
    ups[-1].start()
    project(1)
    for gather in ups[:-1]:
        gather.forward(origins)
    convolve(1, lambda par, at: short[1, par, at, :] * conv[0, par, at, :], lambda: None)
    for gather in cots:
        gather.forward(t_origins)
    project(2)
    copies.start(w_in, w_in_out)
    copies.start(z, z_out)
    for par in range(2):
        for block in range(tensor):
            values = short[2, par, block * own : (block + 1) * own, :] * conv[1, par, block * own : (block + 1) * own, :]
            gated[par, block] = values.astype(BF16)
    trades = []
    for i in range(1, tensor):
        to = place.t_at(i)
        for par in range(2):
            trades.append(sems.copy(gated.at[par, to], own_gated.at[place.t, par], {"tensor": to}))
    for copy in trades:
        copy.start()
    ups[-1].forward(origins)
    for par in range(2):
        copies.start(gated.at[par, place.t], own_gated.at[place.t, par])
    copies.start(gated, gated_out)
    for gather in (*cots, *ups, out_rows):
        gather.arrived()
    for copy in trades:
        copy.wait()
    for gather in (*norms, *ins, outs, *ups, *cots, out_rows):
        gather.finish()
    copies.finish()


MESH = pl.DeviceIdType.MESH


class Place:
    def __init__(self, dp, tensor):
        self.dp, self.tensor = dp, tensor
        self.rows = 4 if dp % 4 == 0 else 1
        self.cols = dp // self.rows
        self.cores = 2 if tensor % 2 == 0 else 1
        self.ys = tensor // self.cores
        self.d, self.t = lax.axis_index("dp"), lax.axis_index("tensor")
        self.a, self.b = self.d // self.cols, lax.rem(self.d, self.cols)
        self.y, self.c = self.t // self.cores, lax.rem(self.t, self.cores)

    def a_at(self, i):
        return lax.rem(self.a + i + self.rows, self.rows) * self.cols + self.b

    def b_at(self, i):
        return self.a * self.cols + lax.rem(self.b + i + self.cols, self.cols)

    def y_at(self, i):
        return lax.rem(self.y + i + self.ys, self.ys) * self.cores + self.c

    def core_peer(self):
        return self.y * self.cores + 1 - self.c

    def t_at(self, i):
        return lax.rem(self.t + i + self.tensor, self.tensor)

    def d_at(self, i):
        return lax.rem(self.d + i + self.dp, self.dp)

    def greet(self, dp=True, all_dp=False):
        peers = [{"tensor": self.t_at(i)} for i in range(1, self.tensor)]
        if all_dp:
            peers += [{"dp": self.d_at(i)} for i in range(1, self.dp)]
        elif dp:
            peers += [{"dp": self.a_at(i)} for i in range(1, self.rows)]
            peers += [{"dp": self.b_at(i)} for i in range(1, self.cols)]
        barrier = pltpu.get_barrier_semaphore()
        for peer in peers:
            pl.semaphore_signal(barrier, inc=1, device_id=peer, device_id_type=MESH)
        self.expected = len(peers)
        return barrier

    def met(self, barrier):
        pl.semaphore_wait(barrier, self.expected)


class Sems:
    def __init__(self, send, recv):
        self.send, self.recv, self.used = send, recv, 0

    def copy(self, src, dst, device):
        i = self.used
        self.used += 1
        return pltpu.make_async_remote_copy(
            src_ref=src, dst_ref=dst, send_sem=self.send.at[i], recv_sem=self.recv.at[i],
            device_id=device, device_id_type=MESH,
        )


class LocalCopies:
    def __init__(self, sems):
        self.sems, self.open, self.used = sems, [], 0

    def start(self, src, dst):
        copy = pltpu.make_async_copy(src, dst, self.sems.at[self.used])
        self.used += 1
        copy.start()
        self.open.append(copy)
        return copy

    def take(self, copy):
        copy.wait()
        self.open = [other for other in self.open if other is not copy]

    def finish(self):
        for copy in self.open:
            copy.wait()


class Gather:
    def __init__(self, sems, source, slot, own, far, near, device):
        self.first = [sems.copy(source, slot(own), device(i)) for i in far]
        self.near = [sems.copy(source, slot(own), device(i)) for i in near]
        self.sems, self.slot, self.device, self.near_ids = sems, slot, device, near
        self.second = []

    def start(self):
        for copy in self.first + self.near:
            copy.start()

    def forward(self, origins, which=None):
        for i, origin in enumerate(origins):
            if which is not None and i not in which:
                continue
            self.first[i].wait_recv()
            for peer in self.near_ids:
                copy = self.sems.copy(self.slot(origin), self.slot(origin), self.device(peer))
                copy.start()
                self.second.append(copy)

    def arrived(self):
        for copy in self.near + self.second:
            copy.wait_recv()

    def finish(self):
        for copy in self.first + self.near + self.second:
            copy.wait_send()


def tensor_gather(place, sems, source, slot):
    near = [place.core_peer()] if place.cores == 2 else []
    return Gather(
        sems, source, slot, place.t, [place.y_at(i) for i in range(1, place.ys)], near, lambda i: {"tensor": i}
    )


def row_pieces(rows):
    count = 2 if rows % 32 == 0 else 1
    return [pl.ds(i * (rows // count), rows // count) for i in range(count)]


def dp_gather(place, sems, source, slot):
    return Gather(
        sems, source, slot, place.d, [place.a_at(i) for i in range(1, place.rows)],
        [place.b_at(i) for i in range(1, place.cols)], lambda i: {"dp": i},
    )


def tensor_origins(place):
    return [place.y_at(-i) for i in range(1, place.ys)]


def dp_origins(place):
    return [place.a_at(-i) for i in range(1, place.rows)]


def gather_counts(dp, tensor):
    cores = 2 if tensor % 2 == 0 else 1
    rows = 4 if dp % 4 == 0 else 1
    far_t, near_t, far_d, near_d = tensor // cores - 1, cores - 1, rows - 1, dp // rows - 1
    return far_t + near_t + far_t * near_t, far_d + near_d + far_d * near_d


def vmem_specs(n):
    return [pl.BlockSpec(memory_space=pltpu.VMEM)] * n


def mix_shapes(half, width, hidden_width, filter_parts=3):
    edge4 = half // 4
    return dict(
        z=((3, 2, half + 2 * PAD, width), F32),
        filt_spec=((2, filter_parts, 2 * half, width), F32),
        e_filt_spec=((2, filter_parts, edge4, width), F32),
        spec=((2, 2, 2 * half, width), F32),
        e_spec=((2, 2, edge4, width), F32),
        conv=((2, 2, half, width), F32),
        hidden=((half, 2 * hidden_width), F32),
    )


def front_call(dp, tensor, args, half, hidden_width):
    S = jax.ShapeDtypeStruct
    V = pltpu.VMEM
    _, count, model = args[0].shape
    rows, _, channels = args[5].shape
    units = args[22].shape[1]
    own = count // 2
    shapes = mix_shapes(half, channels, hidden_width)
    norm, gate, mask = ((2, tensor, own, model), BF16), ((2, tensor, own, channels), BF16), ((2, half + PAD, 8), F32)
    outs = [
        S((3, model, channels), BF16), S((tensor, dp, rows, channels), BF16), S((dp, rows, units), BF16),
        S(*norm), S(*norm), S(*gate), S((tensor, 2, own, channels), BF16), S(*mask),
    ] + [S(*v) for v in shapes.values()]
    per_t, per_d = gather_counts(dp, tensor)
    copies = 5 * per_t + 6 * per_d + 2 * (tensor - 1)
    hbm = pl.BlockSpec(memory_space=pl.ANY)
    return pl.pallas_call(
        functools.partial(front, dp, tensor),
        out_shape=outs,
        in_specs=vmem_specs(21) + [hbm] * 4,
        out_specs=[hbm] * len(outs),
        scratch_shapes=[
            V(args[23].shape, BF16), V(args[24].shape, BF16),
            V((3, rows, channels), BF16), V((3, dp, rows, channels), BF16), V((3, model, channels), BF16),
            V((2, own, model), BF16), V(*norm), V(*gate), V(*mask),
        ] + [V(*v) for v in shapes.values()] + [
            V((3, 2, half, channels), F32), V((3 * half, channels), BF16), V((6 * half, channels), BF16),
            V((6 * half, channels), BF16), V((half, channels), F32),
            pltpu.SemaphoreType.DMA((copies,)), pltpu.SemaphoreType.DMA((copies,)), pltpu.SemaphoreType.DMA((32,)),
        ],
        compiler_params=pltpu.CompilerParams(collective_id=0, has_side_effects=True, vmem_limit_bytes=VMEM_LIMIT),
        name="front",
    )(*args)


def far_moves(place, sems, far_out, far_in):
    return [sems.copy(far_out.at[i - 1], far_in.at[i - 1], {"dp": place.a_at(i)}) for i in range(1, place.rows)]


def far_total(moves, keep, far_in):
    out = keep[...]
    for i, copy in enumerate(moves):
        copy.wait_recv()
        out = out + far_in[i].astype(F32)
    return out


class WeightReduce:
    def __init__(self, place, sems, low, near_in, keep, far_out, far_in):
        self.place, self.low, self.near_in, self.keep, self.far_out, self.far_in = place, low, near_in, keep, far_out, far_in
        own = lambda i: lax.rem(place.b + i, place.cols)
        self.near = [
            sems.copy(low.at[own(i)], near_in.at[i - 1], {"dp": place.b_at(i)}) for i in range(1, place.cols)
        ]
        self.far = [] if far_in is None else far_moves(place, sems, far_out, far_in)

    def start(self):
        for copy in self.near:
            copy.start()

    def combine(self):
        place = self.place
        for copy in self.near:
            copy.wait_recv()
        for i in list(range(1, place.rows)) + [0]:
            a = lax.rem(place.a + i, place.rows)
            total = self.low[place.b, a].astype(F32)
            for j in range(place.cols - 1):
                total = total + self.near_in[j, a].astype(F32)
            if i:
                self.far_out[i - 1] = total.astype(BF16)
                if self.far:
                    self.far[i - 1].start()
            else:
                self.keep[...] = total

    def total(self):
        return far_total(self.far, self.keep, self.far_in)

    def finish(self):
        for copy in self.near + self.far:
            copy.wait_send()


class Reduce:
    def __init__(self, place, sems, near_out, near_in, far_out, far_in):
        self.place, self.near_in, self.near_out, self.far_in, self.far_out = place, near_in, near_out, far_in, far_out
        peer = {"tensor": place.core_peer()}
        self.near = [sems.copy(near_out.at[i], near_in.at[i], peer) for i in range(place.ys)] if place.cores == 2 else []
        self.far = []
        if far_in is not None:
            self.far = [
                sems.copy(far_out.at[i - 1], far_in.at[i - 1], {"tensor": place.y_at(i)}) for i in range(1, place.ys)
            ]

    def order(self):
        place = self.place
        blocks = []
        for i in [0] + list(range(place.ys - 1, 0, -1)):
            for other in range(place.cores):
                owner = place.y_at(i)
                blocks.append((i, other, owner + (1 - 2 * place.c) if other else owner))
        return blocks

    def combine(self, keep, rows, send=True):
        for i in list(range(1, self.place.ys)) + [0]:
            if self.near:
                self.near[i].wait_recv()

            def work(at, i=i):
                total = keep[i, at, :]
                if self.near:
                    total = total + self.near_in[i, at, :].astype(F32)
                if i:
                    self.far_out[i - 1, at, :] = total.astype(BF16)
                else:
                    keep[0, at, :] = total

            over_rows(rows, 32, work)
            if i and send:
                self.far[i - 1].start()

    def total(self, keep, at):
        out = keep[0, at, :]
        for i in range(self.place.ys - 1):
            out = out + self.far_in[i, at, :].astype(F32)
        return out

    def arrived(self):
        for copy in self.far:
            copy.wait_recv()

    def finish(self):
        for copy in self.near + self.far:
            copy.wait_send()


GELU_SCALE = math.sqrt(2.0 / math.pi)


def gelu_and_slope(x):
    square = x * x
    bent = jnp.tanh(GELU_SCALE * (x + 0.044715 * (x * square)))
    slope = 0.5 * (1.0 + bent) + 0.5 * x * (1.0 - bent * bent) * (GELU_SCALE + (3.0 * 0.044715 * GELU_SCALE) * square)
    return 0.5 * x * (1.0 + bent), slope


def fold8(x):
    return jnp.sum(x.reshape(-1, 8, x.shape[1]), axis=0)


def norm_back(grad, normal, scale, gain):
    k = grad * gain
    return scale * (k - jnp.mean(k, axis=-1, keepdims=True) - normal * jnp.mean(k * normal, axis=-1, keepdims=True))


def put_weight_grad(place, grad, left, right, low):
    rows = low.shape[2]

    @pl.loop(0, 2)
    def _(par):
        flat = lambda ref: ref[par].reshape(-1, ref.shape[-1])
        part = lax.dot_general(flat(left), flat(right), COLUMN_CONTRACT, preferred_element_type=F32)

        @pl.when(par == 0)
        def _():
            grad[...] = part

        @pl.when(par != 0)
        def _():
            grad[...] += part

    for a in range(place.rows):
        for b in range(place.cols):
            start = (a * place.cols + b) * rows
            low[b, a] = grad[start : start + rows, :].astype(BF16)


def middle(
    dp, tensor,
    tokens, cotangent, own_gated, out_full, out_bias, gain, shift, up_bias, down_bias, up_in, cot_in, down_shard,
    d_mixed_out, d_mix_low, mlp_own, mlp_far, down_far, down_keep, g_up, row_sums, up_sums,
    up_all, cot_full, mixed, normal, scales, norm_full, down_all, slopes, pre, acts, d_pres, keep, near_out, near_in, far_out, far_in,
    keep_mlp, near_out_mlp, near_in_mlp, far_mlp, cot_rows, grad, low_down, low_up, down_near, down_far_v, acc, up_acc,
    send, recv, local,
):
    _, count, model = tokens.shape
    own = count // 2
    place = Place(dp, tensor)
    sems, copies = Sems(send, recv), LocalCopies(local)
    barrier = place.greet()
    up_loaded, cot_loaded = copies.start(up_in, up_all), copies.start(cot_in, cot_full)
    parity = parity_matrix(count)
    total = dot(parity, tokens[0]) + row_of(out_bias)
    cot_rows[...] = dot(parity, cotangent[0])
    place.met(barrier)
    downs = [
        dp_gather(place, sems, down_shard.at[at], lambda i, at=at: down_all.at[i, at])
        for at in row_pieces(down_shard.shape[0])
    ]
    for gather in downs:
        gather.start()
    own_down = copies.start(down_shard, down_all.at[place.d])
    for block in range(tensor):
        rows = jnp.concatenate([own_gated[block, 0], own_gated[block, 1]], axis=0)
        total += lax.dot_general(rows, out_full[block], ROW_CONTRACT, preferred_element_type=F32)
    mixed[...] = total
    xhat, scale = layer_norm_parts(total)
    normal[...] = xhat
    scales[...] = jnp.broadcast_to(scale, scales.shape)
    low = (xhat * row_of(gain) + row_of(shift)).astype(BF16)
    for par in range(2):
        norm_full[par, place.t] = low[par * own : (par + 1) * own]
    gathers = [
        tensor_gather(place, sems, norm_full.at[par, place.t], lambda i, par=par: norm_full.at[par, i]) for par in range(2)
    ]
    for gather in gathers:
        gather.start()
    reduce = Reduce(place, sems, near_out, near_in, far_out, far_in)
    up_acc[...] = jnp.zeros_like(up_acc)

    def block_rows(ref, owner):
        return jnp.concatenate([ref[0, owner], ref[1, owner]], axis=0)

    def forward(owner):
        pre[...] = dot(block_rows(norm_full, owner), up_all[...]) + row_of(up_bias)
        for par in range(2):
            def work(at, par=par):
                rows = pl.ds(pl.multiple_of(par * own + at.start, 16), at.size)
                act, slope = gelu_and_slope(pre[rows, :])
                acts[par, owner, at, :] = act.astype(BF16)
                slopes[owner, rows, :] = slope

            over_rows(own, 16, work)

    def backward(step, other, owner):
        pre[...] = dot(block_rows(cot_full, owner), flat_rows(down_all))
        for par in range(2):
            def work(at, par=par):
                rows = pl.ds(pl.multiple_of(par * own + at.start, 16), at.size)
                d_pre = (pre[rows, :] * slopes[owner, rows, :]).astype(BF16)
                d_pres[par, owner, at, :] = d_pre
                up_acc[...] += fold8(d_pre.astype(F32))

            over_rows(own, 16, work)
        part = lax.dot_general(block_rows(d_pres, owner), up_all[...], ROW_CONTRACT, preferred_element_type=F32)
        if other:
            near_out[step] = part.astype(BF16)
            reduce.near[step].start()
        else:
            keep[step] = part

    blocks = reduce.order()
    copies.take(up_loaded)
    copies.take(cot_loaded)
    forwarded = False
    for step, other, owner in blocks:
        if step == 0 and other:
            for gather in gathers:
                for copy in gather.near:
                    copy.wait_recv()
        if step and not forwarded:
            for gather in downs[:-1]:
                gather.forward(dp_origins(place))
            for gather in gathers:
                gather.forward(tensor_origins(place))
            downs[-1].forward(dp_origins(place))
            forwarded = True
        if step and other:
            for gather in gathers:
                gather.second[place.ys - 1 - step].wait_recv()
        forward(owner)
    if not forwarded:
        for gather in (*gathers, *downs):
            gather.forward(tensor_origins(place) if gather in gathers else dp_origins(place))
    grad_down = WeightReduce(place, sems, low_down, down_near, down_keep, down_far_v, None)
    put_weight_grad(place, grad, cot_full, acts, low_down)
    grad_down.start()
    for gather in downs:
        gather.arrived()
    copies.take(own_down)
    for block in blocks[::-1]:
        backward(*block)
    reduce.combine(keep, count)
    put_weight_grad(place, grad, norm_full, d_pres, low_up)
    copies.start(low_up, g_up)
    sums = Reduce(place, sems, near_out_mlp, near_in_mlp, far_mlp, None)
    for step, other, owner in blocks[::-1]:
        part = lax.dot_general(block_rows(acts, owner), flat_rows(down_all), ROW_CONTRACT, preferred_element_type=F32)
        if other:
            near_out_mlp[step] = part.astype(BF16)
            sums.near[step].start()
        else:
            keep_mlp[step] = part
    sums.combine(keep_mlp, count, send=False)
    if place.ys > 1:
        copies.start(far_mlp, mlp_far)

    def own_rows(at):
        mlp_own[at, :] = keep_mlp[0, at, :] + mixed[at, :] + row_of(down_bias)

    over_rows(count, 32, own_rows)
    up_sums[...] = jnp.sum(up_acc[...], axis=0, keepdims=True)
    for gather in (*gathers, *downs):
        gather.finish()
    acc[...] = jnp.zeros_like(acc)
    reduce.arrived()

    def back(at):
        grad_rows = reduce.total(keep, at)
        hat = normal[at, :]
        out_grad = cot_rows[at, :]
        d_mixed = out_grad + norm_back(grad_rows, hat, scales[at, 0:1], row_of(gain))
        mixed[at, :] = d_mixed
        d_mix_low[at, :] = d_mixed.astype(BF16)
        acc[0:8, :] += fold8(grad_rows * hat)
        acc[8:16, :] += fold8(grad_rows)
        acc[16:24, :] += fold8(d_mixed)
        acc[24:32, :] += fold8(out_grad)

    over_rows(count, 64, back)
    copies.start(mixed, d_mixed_out)
    grad_down.combine()
    if place.rows > 1:
        copies.start(down_far_v, down_far)
    for i in range(4):
        row_sums[i : i + 1, :] = jnp.sum(acc[8 * i : 8 * i + 8, :], axis=0, keepdims=True)
    for group in (reduce, sums, grad_down):
        group.finish()
    copies.finish()


def middle_call(dp, tensor, args):
    S = jax.ShapeDtypeStruct
    _, count, model = args[0].shape
    units = args[9].shape[1]
    own, cores, rows_d = count // 2, 2 if tensor % 2 == 0 else 1, 4 if dp % 4 == 0 else 1
    ys, farther = tensor // cores, max(tensor // cores - 1, 1)
    rows, low_rows = ((count, model), F32), ((ys, count, model), BF16)
    blocks, norms = ((2, tensor, own, units), BF16), ((2, tensor, own, model), BF16)
    low_grad = ((dp // rows_d, rows_d, model // dp, units), BF16)
    far = ((farther, count, model), BF16)
    far_grad = ((max(rows_d - 1, 1), model // dp, units), BF16)
    near_grad = ((max(dp // rows_d - 1, 1), rows_d, model // dp, units), BF16)
    kept = ((model // dp, units), F32)
    per_t, per_d = gather_counts(dp, tensor)
    total = 2 * per_t + 2 * per_d + 3 * ys + dp // rows_d
    hbm, vmem = pl.BlockSpec(memory_space=pl.ANY), pl.BlockSpec(memory_space=pltpu.VMEM)
    return pl.pallas_call(
        functools.partial(middle, dp, tensor),
        out_shape=[
            S(*rows), S((count, model), BF16), S(*rows), S(*far), S(*far_grad), S(*kept), S(*low_grad), S((4, model), F32), S((1, units), F32),
        ],
        in_specs=vmem_specs(len(args) - 3) + [hbm] * 3,
        out_specs=[hbm, vmem, vmem, hbm, hbm, vmem, hbm, vmem, vmem],
        scratch_shapes=[
            pltpu.VMEM((model, units), BF16), pltpu.VMEM(*norms),
            pltpu.VMEM(*rows), pltpu.VMEM(*rows), pltpu.VMEM((count, 128), F32), pltpu.VMEM(*norms),
            pltpu.VMEM((dp, model // dp, units), BF16), pltpu.VMEM((tensor, count, units), F32), pltpu.VMEM((count, units), F32),
            pltpu.VMEM(*blocks), pltpu.VMEM(*blocks), pltpu.VMEM((ys, count, model), F32),
            pltpu.VMEM(*low_rows), pltpu.VMEM(*low_rows), pltpu.VMEM(*far), pltpu.VMEM(*far),
            pltpu.VMEM((ys, count, model), F32), pltpu.VMEM(*low_rows), pltpu.VMEM(*low_rows), pltpu.VMEM(*far),
            pltpu.VMEM(*rows), pltpu.VMEM((model, units), F32), pltpu.VMEM(*low_grad), pltpu.VMEM(*low_grad),
            pltpu.VMEM(*near_grad), pltpu.VMEM(*far_grad),
            pltpu.VMEM((32, model), F32), pltpu.VMEM((8, units), F32),
            pltpu.SemaphoreType.DMA((total,)), pltpu.SemaphoreType.DMA((total,)), pltpu.SemaphoreType.DMA((8,)),
        ],
        compiler_params=pltpu.CompilerParams(collective_id=1, has_side_effects=True, vmem_limit_bytes=VMEM_LIMIT),
        name="middle",
    )(*args)


def order_matrix(rows):
    half = rows // 2
    at = lax.broadcasted_iota(jnp.int32, (rows, rows), 0)
    wanted = lax.rem(at, 2) * half + at // 2
    return (lax.broadcasted_iota(jnp.int32, (rows, rows), 1) == wanted).astype(F32).astype(BF16)


MISC, TAPS, SMALL_ROWS = 0, 8, 24


def rear(
    dp, tensor,
    tokens, d_mix_low, row_sums, up_sums, gain, taps, tap_bias, ptable, w1, b1, w2, b2, w3, rates, direct,
    d_mixed_in, mlp_own, mlp_far, down_far, down_keep_in, g_up, norm_in, gated_in, w_in_in, out_in, masks_in,
    wave_in, wave_back_in, twist, e_wave, e_back, e_twist,
    z_in, filt_in, e_filt_in, spec_in, e_spec_in, conv_in, hidden_in,
    output, grad_tokens, o_down, o_up, o_in, o_out, o_small, o_first, o_early, o_late,
    wave, wave_back, masks, z, filt_spec, e_filt_spec, spec, e_spec, conv, hidden,
    d_mixed, norm_full, gated, w_in, w_out, d_mix_full, mlp_in, low_up,
    short, rhs_even, rhs_odd, g, g_spec, e_g_spec, d_short, d_z, acc, normal, scales,
    down_keep, down_land, up_near, up_keep, up_far, up_land,
    in_low, in_near, in_keep, in_far, in_land, out_low, out_near, out_keep, out_far, out_land,
    keep, near_out, near_in, far_out, far_in,
    small, small_in, small_own, small_all, first, first_in, whole, whole_in, whole_own, whole_all,
    early_in, early, early_far, late, late_in, late_sum, late_far, wide,
    send, recv, local,
):
    tabs = (wave, wave_back, twist, e_wave, e_back, e_twist)
    half, width = z.shape[2] - 2 * PAD, z.shape[3]
    _, count, model = tokens.shape
    own = count // 2
    d_filt, rhs = conv, rhs_even
    place = Place(dp, tensor)
    sems, copies = Sems(send, recv), LocalCopies(local)
    barrier = place.greet(all_dp=True)
    loads = {}

    def load(name, src, dst):
        loads[name] = copies.start(src, dst)

    def loaded(*names):
        for name in names:
            copies.take(loads[name])

    load("up", g_up, low_up)
    load("z", z_in, z)
    load("masks", masks_in, masks)
    load("out", out_in.at[place.t], w_out)
    load("conv", conv_in, conv)
    load("wave", wave_in, wave)
    load("filt", filt_in.at[1, 0:2], filt_spec)
    load("e_filt", e_filt_in.at[1, 0:2], e_filt_spec)
    load("wave_back", wave_back_in, wave_back)
    load("gated", gated_in, gated)
    load("norm", norm_in, norm_full)
    load("w_in", w_in_in, w_in)
    load("spec", spec_in.at[1], spec)
    load("e_spec", e_spec_in.at[1], e_spec)
    load("hidden", hidden_in, hidden)
    load("mixed", d_mixed_in, d_mixed)
    load("down", down_keep_in, down_keep)
    for par in range(2):
        d_mix_full[par, place.t] = d_mix_low[par * own : (par + 1) * own, :]
    place.met(barrier)
    gathers = [
        tensor_gather(place, sems, d_mix_full.at[par, place.t], lambda i, par=par: d_mix_full.at[par, i]) for par in range(2)
    ]
    for gather in gathers:
        gather.start()
    downs = far_moves(place, sems, down_far, down_land)
    ups = WeightReduce(place, sems, low_up, up_near, up_keep, up_far, up_land)
    ins = [
        WeightReduce(place, sems, in_low.at[p], in_near.at[p], in_keep.at[p], in_far.at[p], in_land.at[p]) for p in range(3)
    ]
    outs = WeightReduce(place, sems, out_low, out_near, out_keep, out_far, out_land)
    mlp = [sems.copy(mlp_far.at[i - 1], mlp_in.at[i - 1], {"tensor": place.y_at(i)}) for i in range(1, place.ys)]
    for copy in downs:
        copy.start()
    loaded("up")
    ups.start()
    early_trades = [sems.copy(row_sums, early_in.at[i - 1], {"tensor": place.t_at(i)}) for i in range(1, tensor)]
    for copy in early_trades:
        copy.start()

    xhat, scale = layer_norm_parts(dot(parity_matrix(count), tokens[0]))
    normal[...] = xhat
    scales[...] = jnp.broadcast_to(scale, scales.shape)
    small[...] = jnp.zeros_like(small)
    loaded("z", "masks")
    for which in range(3):
        make_short(short, z, masks, taps, tap_bias, half, which)
    loaded("out", "conv")
    for gather in gathers:
        gather.forward(tensor_origins(place))
    for copy in mlp:
        copy.start()
    for gather in gathers:
        gather.arrived()
    for par in range(2):
        g[par] = dot(d_mix_full[par].reshape(half, model), w_out[...])

        def gate(at, par=par):
            grad = g[par, at, :]
            d_short[2, par, at, :] = grad * conv[1, par, at, :]
            short[2, par, at, :] = grad * short[2, par, at, :]

        over_rows(half, CHUNK, gate)

    rows = model // dp

    def weight_grad(reduced, low, left, right):
        total = None
        for par in range(2):
            part = lax.dot_general(left(par), right(par), COLUMN_CONTRACT, preferred_element_type=F32)
            total = part if total is None else total + part
        for a in range(place.rows):
            for b in range(place.cols):
                start = (a * place.cols + b) * rows
                low[b, a] = total[start : start + rows, :].astype(BF16)
        reduced.start()

    def in_grad(p):
        weight_grad(ins[p], in_low.at[p], lambda par: norm_full[par].reshape(half, model), lambda par: d_z[p, par])

    hidden_width = w3.shape[0]
    base = 2 * hidden_width

    def short_back(which):
        acc[...] = jnp.zeros_like(acc)
        for par in range(2):
            d_short[which, par, half : half + PAD, :] = jnp.zeros((PAD, width), F32)
        for par in range(2):
            def work(at, marked, par=par):
                size, start = at.size, at.start
                tap = lambda j: taps[j, which : which + 1, :]
                _, here, one, two = short_rows(z, which, par, at, marked, masks, taps, tap_bias)
                grad = d_short[which, par, at, :]
                acc[0:8, :] += fold8(grad)
                acc[8:16, :] += fold8(grad * here)
                acc[16:24, :] += fold8(grad * one)
                acc[24:32, :] += fold8(grad * two)
                rows_on = pl.ds(pl.multiple_of(start, 8), size + PAD)
                same, other = d_short[which, par, rows_on, :], d_short[which, 1 - par, rows_on, :]
                if marked:
                    same, other = same * masks[par, rows_on, 4:5], other * masks[1 - par, rows_on, 3:4]
                same, other = same[1 : size + 1], other[1 : size + 1] if par else other[:size]
                low = (tap(0) * grad + tap(1) * other + tap(2) * same).astype(BF16)
                d_z[which, par, at, :] = low
                acc[32:40, :] += fold8(low.astype(F32))

            over_rows_marked(half, CHUNK, work)
        total = lambda i: jnp.sum(acc[8 * i : 8 * i + 8, :], axis=0, keepdims=True)
        small[pl.ds(base + MISC + which, 1), :] = total(4)
        small[pl.ds(base + MISC + 3 + which, 1), :] = total(0)
        for j in range(3):
            small[pl.ds(base + TAPS + 3 * j + which, 1), :] = total(1 + j)

    def spread_back(o, source, out):
        analyse(tabs, rhs, source, g_spec.at[o], e_g_spec.at[o], masks)
        loaded("filt", "e_filt")
        edges = spectra_product(
            tabs, filt_spec, e_filt_spec, g_spec.at[o], e_g_spec.at[o], rhs_even, rhs_odd, True, True
        )
        if o:
            load("filt", filt_in.at[0, 0:2], filt_spec)
            load("e_filt", e_filt_in.at[0, 0:2], e_filt_spec)
            loaded("wave_back")
        synthesise(tabs, rhs_even, out, 0)
        synthesise(tabs, rhs_odd, out, 1)
        join(out, edges, direct[o : o + 1, :], source, masks, half)

    def filter_back(o, source, forward_in):
        loaded("spec", "e_spec")
        edges = spectra_product(tabs, spec, e_spec, g_spec.at[o], e_g_spec.at[o], rhs_even, rhs_odd, True, True)
        if o:
            load("spec", spec_in.at[0], spec)
            load("e_spec", e_spec_in.at[0], e_spec)
        acc[...] = jnp.zeros_like(acc)
        for par in range(2):
            def product(at, par=par):
                acc[0:8, :] += fold8(source(par, at) * forward_in(par, at))

            over_rows(half, CHUNK, product)
        small[pl.ds(base + MISC + 6 + o, 1), :] = jnp.sum(acc[0:8, :], axis=0, keepdims=True)
        synthesise(tabs, rhs_even, d_filt.at[o], 0)
        synthesise(tabs, rhs_odd, d_filt.at[o], 1)
        for par in range(2):
            edge = edges[par].shape[0] // 2
            d_filt[o, par, 0:edge, :] += (edges[par][:edge] + edges[par][edge:]) * (half / edge)

            def work(at, par=par):
                decay = decay_at(par, CHUNK, at.start, rates[o : o + 1, :])
                d_filt[o, par, at, :] = d_filt[o, par, at, :] * (decay * (1.0 / half))

            over_rows(half, CHUNK, work)

    grad_one = lambda par, at: short[2, par, at, :]
    grad_zero = lambda par, at: g[par, at, :]
    loaded("wave")
    spread_back(1, grad_one, d_short.at[0])
    for copy in early_trades:
        copy.wait()
    early[...] = jnp.zeros_like(early)
    total = row_sums[...]
    for i in range(tensor - 1):
        total = total + early_in[i]
    early[0:4, 0:model] = total
    early[4:5, 0 : up_sums.shape[1]] = up_sums[...]
    early_moves = [sems.copy(early, early_far.at[i - 1], {"dp": place.d_at(i)}) for i in range(1, dp)]
    for copy in early_moves:
        copy.start()
    loaded("gated")
    weight_grad(
        outs, out_low, lambda par: d_mix_full[par].reshape(half, model), lambda par: gated[par].reshape(half, width)
    )
    ups.combine()
    for par in range(2):
        def gate_again(at, par=par):
            grad = d_short[0, par, at, :]
            d_short[1, par, at, :] = grad * conv[0, par, at, :]
            g[par, at, :] = grad * short[1, par, at, :]

        over_rows(half, CHUNK, gate_again)
    short_back(2)
    loaded("norm")
    in_grad(2)
    spread_back(0, grad_zero, d_short.at[0])
    short_back(1)
    short_back(0)
    loaded("w_in")
    reduce = Reduce(place, sems, near_out, near_in, far_out, far_in)
    for step, other, owner in reduce.order()[::-1]:
        at = pl.ds(pl.multiple_of(owner * own, 16), own)
        part = None
        for p in range(3):
            rows_p = jnp.concatenate([d_z[p, 0, at, :], d_z[p, 1, at, :]], axis=0)
            term = lax.dot_general(rows_p, w_in[p], ROW_CONTRACT, preferred_element_type=F32)
            part = term if part is None else part + term
        if other:
            near_out[step] = part.astype(BF16)
            reduce.near[step].start()
        else:
            keep[step] = part
    in_grad(1)
    reduce.combine(keep, count)
    in_grad(0)
    outs.combine()
    ins[2].combine()

    filter_back(1, grad_one, lambda par, at: short[1, par, at, :] * conv[0, par, at, :])
    ins[1].combine()
    filter_back(0, grad_zero, lambda par, at: short[0, par, at, :])
    loaded("hidden")
    h1, c1, pre2 = hidden_layers(ptable, w1, b1, w2, b2)
    lane = lax.broadcasted_iota(jnp.int32, pre2.shape, 1)
    d_h2 = [None, None]
    for o in range(2):
        last = w3[:, o, :]
        both = jnp.concatenate([last, last], axis=0)
        grads = [fine_dot(hidden[...], d_filt[o, par], COLUMN_CONTRACT) for par in range(2)]
        small[o * hidden_width : (o + 1) * hidden_width, :] = grads[0][:hidden_width] + grads[1][hidden_width:]
        for par in range(2):
            term = fine_dot(d_filt[o, par], both, ROW_CONTRACT)
            d_h2[par] = term if o == 0 else d_h2[par] + term
    d_pre2 = jnp.where(lane < hidden_width, d_h2[0], d_h2[1]) * sine_cosine(pre2)[1]
    d_pre1 = fine_dot(d_pre2, blocks_of(w2[...], hidden_width), ROW_CONTRACT) * c1
    across = lambda x, at: x[:at, :hidden_width] + x[at:, hidden_width:]
    g_first = across(fine_dot(ptable[...], d_pre1, COLUMN_CONTRACT), ptable.shape[1] // 2)
    g_second = across(fine_dot(h1, d_pre2, COLUMN_CONTRACT), hidden_width)
    room, tall = first.shape[0] - g_first.shape[0], first.shape[0] - 8
    first[...] = jnp.zeros_like(first)
    first[0 : g_first.shape[0], 0:hidden_width] = g_first
    first[g_first.shape[0] :, 0:hidden_width] = g_second[:room]
    first[0 : hidden_width - room, hidden_width:] = g_second[room:]
    for i, grad in enumerate((d_pre1, d_pre2)):
        row = jnp.sum(grad, axis=0, keepdims=True)
        first[tall + i : tall + i + 1, hidden_width:] = row[:, :hidden_width] + row[:, hidden_width:]
    trades = [sems.copy(first, first_in.at[i - 1], {"tensor": place.t_at(i)}) for i in range(1, tensor)]
    for copy in trades:
        copy.start()
    ins[0].combine()

    whole[...] = jnp.zeros_like(whole)
    for copy in trades:
        copy.wait()
    total = first[...]
    for i in range(tensor - 1):
        total = total + first_in[i]
    whole[0 : first.shape[0], :] = total

    def part_of(own_part, d):
        return pl.ds(pl.multiple_of(d * own_part.shape[0], 8), own_part.shape[0])

    groups = ((small, small_in, small_own, small_all), (whole, whole_in, whole_own, whole_all))
    spread = []
    for full, landed, own_part, _ in groups:
        spread.append(
            [
                sems.copy(full.at[part_of(own_part, place.d_at(i)), :], landed.at[i - 1], {"dp": place.d_at(i)})
                for i in range(1, dp)
            ]
        )
        for copy in spread[-1]:
            copy.start()

    loaded("mixed")
    wide[...] = jnp.zeros_like(wide)
    reduce.arrived()
    reduce.finish()

    def back(at):
        grad = reduce.total(keep, at)
        hat = normal[at, :]
        d_input = norm_back(grad, hat, scales[at, 0:1], row_of(gain))
        near_out[0, at, :] = (d_mixed[at, :] + d_input).astype(BF16)
        wide[0:8, :] += fold8(grad * hat)
        wide[8:16, :] += fold8(grad)

    over_rows(count, 64, back)
    mlp_sum = d_mixed
    mlp_loaded = copies.start(mlp_own, mlp_sum)
    late[0:1, :] = jnp.sum(wide[0:8, :], axis=0, keepdims=True)
    late[1:2, :] = jnp.sum(wide[8:16, :], axis=0, keepdims=True)
    row_trades = [sems.copy(late, late_in.at[i - 1], {"tensor": place.t_at(i)}) for i in range(1, tensor)]
    for copy in row_trades:
        copy.start()
    joined = []
    for copies_of, (full, landed, own_part, everyone) in zip(spread, groups, strict=True):
        for copy in copies_of:
            copy.wait_recv()
        total = full[part_of(own_part, place.d), :]
        for i in range(dp - 1):
            total = total + landed[i]
        own_part[...] = total
        everyone[part_of(own_part, place.d), :] = total
        for i in range(1, dp):
            copy = sems.copy(own_part, everyone.at[part_of(own_part, place.d), :], {"dp": place.d_at(i)})
            copy.start()
            joined.append(copy)
    for copy in row_trades:
        copy.wait_recv()
    total = late[...]
    for i in range(tensor - 1):
        total = total + late_in[i]
    late_sum[...] = total
    late_moves = [sems.copy(late_sum, late_far.at[i - 1], {"dp": place.d_at(i)}) for i in range(1, dp)]
    for copy in late_moves:
        copy.start()
    order = order_matrix(count)
    grad_tokens[0] = dot(order, near_out[0]).astype(BF16)
    for copy in mlp:
        copy.wait_recv()
    copies.take(mlp_loaded)
    total = mlp_sum[...]
    for i in range(place.ys - 1):
        total = total + mlp_in[i].astype(F32)
    output[0] = dot(order, total.astype(BF16)).astype(BF16)
    for copy in early_moves:
        copy.wait_recv()
    total = early[...]
    for i in range(dp - 1):
        total = total + early_far[i]
    o_early[...] = total
    loaded("down")
    o_down[...] = far_total(downs, down_keep, down_land)
    o_up[...] = ups.total()
    o_out[...] = outs.total()
    for p in (2, 1, 0):
        o_in[p] = ins[p].total()
    for copy in joined:
        copy.wait_recv()
    o_small[...] = small_all[0 : base + SMALL_ROWS, :]
    o_first[...] = whole_all[0 : first.shape[0], :]
    for copy in late_moves:
        copy.wait_recv()
    total = late_sum[...]
    for i in range(dp - 1):
        total = total + late_far[i]
    o_late[...] = total
    for group in (row_trades, *spread, joined, early_moves, late_moves, mlp, downs):
        for copy in group:
            copy.wait_send()
    for group in (*gathers, ups, outs, *ins):
        group.finish()
    copies.finish()


def finish(
    output_in, tokens_in, down, up, weights, out, small, first, early, late,
    output, grad_tokens, o_mix_gain, o_mix_shift, o_in, o_in_bias, o_taps, o_tap_bias, o_w1, o_b1, o_w2, o_b2, o_w3, o_direct,
    o_out, o_out_bias, o_mlp_gain, o_mlp_shift, o_up, o_up_bias, o_down, o_down_bias,
):
    for src, dst in ((output_in, output), (tokens_in, grad_tokens), (down, o_down), (up, o_up), (out, o_out)):
        dst[...] = src[...]
    for p in range(3):
        o_in[:, p, :] = weights[p]
    model, units = o_mix_gain.shape[0], o_up_bias.shape[0]
    for i, ref in enumerate((o_mix_gain, o_mix_shift)):
        ref[...] = late[i : i + 1, :].reshape(model)
    for i, ref in enumerate((o_mlp_gain, o_mlp_shift, o_out_bias, o_down_bias)):
        ref[...] = early[i : i + 1, 0:model].reshape(model)
    o_up_bias[...] = early[4:5, 0:units].reshape(units)
    hidden_width, emb = o_w2.shape[0], o_w1.shape[0]
    base = 2 * hidden_width
    o_in_bias[...] = small[base + MISC : base + MISC + 3, :]
    o_tap_bias[...] = small[base + MISC + 3 : base + MISC + 6, :]
    o_direct[...] = small[base + MISC + 6 : base + MISC + 8, :]
    for j in range(3):
        o_taps[j] = small[base + TAPS + 3 * j : base + TAPS + 3 * j + 3, :]
    for o in range(2):
        o_w3[:, o, :] = small[o * hidden_width : (o + 1) * hidden_width, :]
    tall = first.shape[0] - 8
    room = hidden_width - tall
    o_w1[...] = first[0:emb, 0:hidden_width]
    o_w2[0:room, :] = first[first.shape[0] - room :, 0:hidden_width]
    o_w2[room:, :] = first[0:tall, hidden_width:]
    for i, ref in enumerate((o_b1, o_b2)):
        ref[...] = first[tall + i : tall + i + 1, hidden_width:].reshape(hidden_width)


def finish_call(args, emb):
    f32 = lambda *shape: jax.ShapeDtypeStruct(shape, F32)
    rows_shape = jax.ShapeDtypeStruct(args[0].shape, BF16)
    model, (rows, units), channels, hidden_width = args[0].shape[2], args[2].shape, args[5].shape[1], args[7].shape[1] // 2
    return pl.pallas_call(
        finish,
        out_shape=[
            rows_shape, rows_shape, f32(model), f32(model), f32(rows, 3, channels), f32(3, channels), f32(3, 3, channels),
            f32(3, channels), f32(emb, hidden_width), f32(hidden_width), f32(hidden_width, hidden_width), f32(hidden_width),
            f32(hidden_width, 2, channels), f32(2, channels), f32(rows, channels), f32(model), f32(model), f32(model),
            f32(rows, units), f32(units), f32(rows, units), f32(model),
        ],
        in_specs=vmem_specs(10),
        out_specs=vmem_specs(22),
        compiler_params=pltpu.CompilerParams(vmem_limit_bytes=VMEM_LIMIT),
        name="finish",
    )(*args)


def rear_call(dp, tensor, args, half):
    S = jax.ShapeDtypeStruct
    _, count, model = args[0].shape
    emb, hidden_width = args[8].shape
    channels, units = args[12].shape[2], args[3].shape[1]
    own, cores, rows_d = count // 2, 2 if tensor % 2 == 0 else 1, 4 if dp % 4 == 0 else 1
    cols_d, ys, rows = dp // rows_d, tensor // cores, model // dp
    farther = max(ys - 1, 1)
    base = 2 * hidden_width
    chunk = -(-(base + SMALL_ROWS) // (8 * dp)) * 8
    packed = (-(-emb // 8) * 8 + hidden_width + 8) // 2
    part = -(-packed // (8 * dp)) * 8
    lanes = 2 * hidden_width
    widest = max(model, units)
    V = pltpu.VMEM
    rows_f = ((count, model), F32)
    norm = ((2, tensor, own, model), BF16)
    far = ((farther, count, model), BF16)

    def buffers(lead, last):
        return [
            V((*lead, cols_d, rows_d, rows, last), BF16), V((*lead, max(cols_d - 1, 1), rows_d, rows, last), BF16), V((*lead, rows, last), F32),
            V((*lead, max(rows_d - 1, 1), rows, last), BF16), V((*lead, max(rows_d - 1, 1), rows, last), BF16),
        ]

    per_t, _ = gather_counts(dp, tensor)
    copies = 2 * per_t + 6 * (rows_d + cols_d) + 4 * ys + 3 * tensor + 6 * dp
    hbm = pl.BlockSpec(memory_space=pl.ANY)
    wave, wave_back = args[26], args[27]
    f32 = lambda *shape: S(shape, F32)
    return pl.pallas_call(
        functools.partial(rear, dp, tensor),
        out_shape=[
            S((1, count, model), BF16), S((1, count, model), BF16), f32(rows, units), f32(rows, units), f32(3, rows, channels),
            f32(rows, channels), f32(base + SMALL_ROWS, channels), f32(packed, lanes), f32(8, widest), f32(2, model),
        ],
        in_specs=vmem_specs(15) + [hbm] * 13 + vmem_specs(4) + [hbm] * 7,
        out_specs=vmem_specs(10),
        scratch_shapes=[
            V(wave.shape, BF16), V(wave_back.shape, BF16), V((2, half + PAD, 8), F32), V((3, 2, half + 2 * PAD, channels), F32),
            V((2, 2 * half, channels), F32), V((2, half // 4, channels), F32), V((2, 2 * half, channels), F32),
            V((2, half // 4, channels), F32), V((2, 2, half, channels), F32), V((half, 2 * hidden_width), F32),
            V(*rows_f), V(*norm), V((2, tensor, own, channels), BF16), V((3, model, channels), BF16), V((model, channels), BF16),
            V(*norm), V(*far), V((cols_d, rows_d, rows, units), BF16),
            V((3, 2, half, channels), F32), V((6 * half, channels), BF16), V((6 * half, channels), BF16),
            V((2, half, channels), F32), V((2, 2, 2 * half, channels), F32), V((2, 2, half // 4, channels), F32),
            V((3, 2, half + PAD, channels), F32), V((3, 2, half, channels), BF16), V((40, channels), F32), V(*rows_f),
            V((count, 128), F32),
        ]
        + [V((rows, units), F32), V((max(rows_d - 1, 1), rows, units), BF16)] + buffers((), units)[1:]
        + buffers((3,), channels) + buffers((), channels)
        + [V((ys, count, model), F32), V((ys, count, model), BF16), V((ys, count, model), BF16), V(*far), V(*far)]
        + [
            V((dp * chunk, channels), F32), V((dp - 1, chunk, channels), F32), V((chunk, channels), F32),
            V((dp * chunk, channels), F32), V((packed, lanes), F32), V((tensor - 1, packed, lanes), F32),
            V((dp * part, lanes), F32), V((dp - 1, part, lanes), F32), V((part, lanes), F32), V((dp * part, lanes), F32),
            V((tensor - 1, 4, model), F32), V((8, widest), F32), V((dp - 1, 8, widest), F32), V((2, model), F32),
            V((tensor - 1, 2, model), F32), V((2, model), F32), V((dp - 1, 2, model), F32), V((16, model), F32),
            pltpu.SemaphoreType.DMA((copies,)), pltpu.SemaphoreType.DMA((copies,)), pltpu.SemaphoreType.DMA((28,)),
        ],
        compiler_params=pltpu.CompilerParams(collective_id=2, has_side_effects=True, vmem_limit_bytes=63 * 2**20),
        name="rear",
    )(*args)


def body(
    tokens,
    segment_ids,
    mix_norm_gain,
    mix_norm_bias,
    in_weight,
    in_bias,
    short_weight,
    short_bias,
    filt_in_weight,
    filt_in_bias,
    filt_mid_weight,
    filt_mid_bias,
    filt_out_weight,
    decay_rates,
    long_bias,
    out_weight,
    out_bias,
    mlp_norm_gain,
    mlp_norm_bias,
    up_weight,
    up_bias,
    down_weight,
    down_bias,
    cotangent,
):
    dp, tensor = lax.axis_size("dp"), lax.axis_size("tensor")
    units = up_weight.shape[1]
    model = tokens.shape[2]
    length, emb, hidden_width = segment_ids.shape[1], filt_in_weight.shape[0], filt_mid_bias.shape[0]
    half = length // 2
    wave, wave_back, *fixed = (jnp.asarray(t) for t in wave_tables(length))
    net = (
        short_weight, short_bias, jnp.asarray(position_table(length, emb)), filt_in_weight, filt_in_bias, filt_mid_weight,
        filt_mid_bias, filt_out_weight, decay_rates, long_bias,
    )
    w_in, out_par, up_par, cot_par, norm_par, gated_par, own_gated, masks, *kept = front_call(
        dp, tensor,
        (tokens, cotangent, segment_ids, mix_norm_gain, mix_norm_bias, in_weight, in_bias) + net
        + (*fixed, out_weight, up_weight, wave, wave_back),
        half, hidden_width,
    )
    out_full = out_par.reshape(tensor, model, -1)
    d_mixed, d_mix_low, mlp_own, mlp_far, *low_grads, row_sums, up_sums = middle_call(
        dp, tensor,
        (tokens, cotangent, own_gated, out_full, out_bias, mlp_norm_gain, mlp_norm_bias, up_bias, down_bias,
         up_par.reshape(model, units), cot_par, down_weight),
    )
    results = rear_call(
            dp, tensor,
            (tokens, d_mix_low, row_sums, up_sums, mix_norm_gain) + net
            + (d_mixed, mlp_own, mlp_far, *low_grads, norm_par, gated_par, w_in, out_full, masks, wave, wave_back, *fixed, *kept),
            half,
        )
    return tuple(finish_call(results, emb))


def solution(mesh):
    placed = (
        P("dp", "tensor", None),
        P("dp", None),
        P(),
        P(),
        P("dp", None, "tensor"),
        P(None, "tensor"),
        P(None, None, "tensor"),
        P(None, "tensor"),
        P(),
        P(),
        P(),
        P(),
        P(None, None, "tensor"),
        P(None, "tensor"),
        P(None, "tensor"),
        P("dp", "tensor"),
        P(),
        P(),
        P(),
        P("dp", "tensor"),
        P("tensor"),
        P("dp", "tensor"),
        P(),
        P("dp", "tensor", None),
    )
    return jax.shard_map(
        body,
        mesh=mesh,
        in_specs=placed,
        out_specs=(
            P("dp", "tensor", None),
            P("dp", "tensor", None),
            P(),
            P(),
            P("dp", None, "tensor"),
            P(None, "tensor"),
            P(None, None, "tensor"),
            P(None, "tensor"),
            P(),
            P(),
            P(),
            P(),
            P(None, None, "tensor"),
            P(None, "tensor"),
            P("dp", "tensor"),
            P(),
            P(),
            P(),
            P("dp", "tensor"),
            P("tensor"),
            P("dp", "tensor"),
            P(),
        ),
        check_vma=False,
    )
```

```python
import functools
import math

import jax
import jax.numpy as jnp
import numpy as np
from jax import lax
from jax.experimental import pallas as pl
from jax.experimental.pallas import tpu as pltpu
from jax.sharding import PartitionSpec as P

DOCS = 3
EPSILON = 1e-05
ROW_CONTRACT = (((1,), (1,)), ((), ()))
COLUMN_CONTRACT = (((0,), (0,)), ((), ()))
F32, BF16 = jnp.float32, jnp.bfloat16
CHUNK = 128
VMEM_LIMIT = 58 * 2**20


def half_table(count, period):
    turns = ((2 * np.arange(count)[:, None] + 1) * np.arange(count)[None, :]) % (2 * period)
    angle = turns * (math.pi / period)
    return np.cos(angle), -np.sin(angle)


def three_pass(table):
    high = table.astype(np.float32).astype(jnp.bfloat16)
    low = (table.astype(np.float32) - high.astype(np.float32)).astype(jnp.bfloat16)
    return np.concatenate([high, high, low], axis=1)


def wave_tables(length):
    half, edge = length // 2, length // 32
    real, imag = half_table(half, length)
    whole = np.concatenate([real, imag], axis=0)
    e_real, e_imag = half_table(edge, 2 * edge)
    zero = np.zeros_like(e_real)
    both = np.block([[e_real, zero], [zero, e_real], [e_imag, zero], [zero, e_imag]])
    step = (2 * np.arange(half) + 1) * (math.pi / length)
    e_step = np.tile((2 * np.arange(edge) + 1) * (math.pi / (2 * edge)), 2)
    lanes = lambda turn: np.repeat(np.stack([np.cos(turn), -np.sin(turn)])[:, :, None], 128, axis=2).astype(np.float32)
    twist, e_twist = lanes(step), lanes(e_step)
    return (
        three_pass(whole), three_pass(whole.T), twist,
        three_pass(both), three_pass(both.T), e_twist,
    )


def position_table(length, emb_width):
    bands = (emb_width - 1) // 2
    places = np.arange(length, dtype=np.float32)
    angles = (2.0 * math.pi * places / length).astype(np.float32)
    frequency = np.linspace(0.0001, bands - 1, bands, dtype=np.float32)
    phases = (angles[:, None] * frequency[None, :]).astype(np.float64)
    table = np.concatenate([(places / (length - 1))[:, None], np.cos(phases), -np.sin(phases)], axis=1).astype(np.float32)
    room = np.zeros((length, -(-emb_width // 8) * 8 - emb_width), np.float32)
    table = np.concatenate([table, room], axis=1)
    return np.concatenate([table[0::2], table[1::2]], axis=1)


def over_rows(rows, step, work):
    @pl.loop(0, rows // step)
    def _(i):
        work(pl.ds(pl.multiple_of(i * step, step), step))


def over_rows_marked(rows, step, work):
    work(pl.ds(0, step), True)

    @pl.loop(1, rows // step - 1)
    def _(i):
        work(pl.ds(pl.multiple_of(i * step, step), step), False)

    work(pl.ds(rows - step, step), True)


def parts(x):
    high = x.astype(BF16)
    return high, (x - high.astype(F32)).astype(BF16)


def put_parts(rhs, at, base, block, x):
    high, low = parts(x)
    size = x.shape[0]
    start = at.start if isinstance(at, pl.Slice) else at
    for slot, piece in ((0, high), (1, low), (2, high)):
        rhs[pl.ds(pl.multiple_of(start + (base + slot * block), 16), size), :] = piece


def widen(rows, width):
    whole, rest = divmod(width, 128)
    return jnp.concatenate([rows] * whole + ([rows[:, :rest]] if rest else []), axis=1)


def turned(pair_of, twist, at):
    width = pair_of[0].shape[1]
    return mul(*pair_of, widen(twist[0, at, :], width), widen(twist[1, at, :], width))


def mul(ar, ai, br, bi):
    return ar * br - ai * bi, ar * bi + ai * br


def mul_conj(ar, ai, br, bi):
    return ar * br + ai * bi, ar * bi - ai * br


def blend(f, x, conj):
    (fe, fo, ft), (xe, xo) = f, x
    m = mul_conj if conj else mul
    if conj:
        a, b = m(*fe, *xe), m(*fo, *xo)
        c, d = m(*fe, *xo), m(*ft, *xe)
    else:
        a, b = m(*fe, *xe), m(*ft, *xo)
        c, d = m(*fe, *xo), m(*fo, *xe)
    return (a[0] + b[0], a[1] + b[1]), (c[0] + d[0], c[1] + d[1])


def dot(a, b):
    return jnp.dot(a, b, preferred_element_type=F32)


def analyse(tabs, rhs, source, spec, edge_spec, masks):
    wave, _, _, e_wave, _, _ = tabs
    half, edge = wave.shape[1] // 3, e_wave.shape[1] // 6

    @pl.loop(0, 2)
    def _(par):
        def fill(at, marked):
            rows = source(par, at)
            put_parts(rhs, at, 0, half, rows * masks[par, at, 0:1] if marked else rows)

        over_rows_marked(half, CHUNK, fill)
        spec[par] = dot(wave[...], rhs[0 : 3 * half, :])
        first, last = pl.ds(0, edge), pl.ds(half - edge, edge)
        window = jnp.concatenate(
            [source(par, first) * masks[par, first, 1:2], source(par, last) * masks[par, last, 2:3]], axis=0
        )
        high, low = parts(window)
        edge_spec[par] = dot(e_wave[...], jnp.concatenate([high, low, high], axis=0))


def pair(ref, index, at, half):
    start = at.start
    return ref[index, at, :], ref[index, pl.ds(pl.multiple_of(start + half, 8), at.size), :]


def spectra_product(tabs, filt, e_filt, spec, e_spec, rhs_even, rhs_odd, conj, turn):
    _, wave_back, twist, _, e_back, e_twist = tabs
    half, edge2 = wave_back.shape[1] // 6, e_back.shape[1] // 6

    def get(f, tw, at, n):
        fe, fo = pair(f, 0, at, n), pair(f, 1, at, n)
        ft = turned(fo, tw, at) if turn else pair(f, 2, at, n)
        return fe, fo, ft

    def work(at):
        even, odd = blend(get(filt, twist, at, half), (pair(spec, 0, at, half), pair(spec, 1, at, half)), conj)
        for rhs, (real, imag) in ((rhs_even, even), (rhs_odd, odd)):
            put_parts(rhs, at, 0, 2 * half, real)
            put_parts(rhs, at, half, 2 * half, imag)

    over_rows(half, CHUNK // 2, work)
    at = pl.ds(0, edge2)
    even, odd = blend(get(e_filt, e_twist, at, edge2), (pair(e_spec, 0, at, edge2), pair(e_spec, 1, at, edge2)), conj)
    out = []
    for real, imag in (even, odd):
        high, low = parts(jnp.concatenate([real, imag], axis=0))
        out.append(dot(e_back[...], jnp.concatenate([high, low, high], axis=0)))
    return out


def synthesise(tabs, rhs, out, par):
    out[par, 0 : tabs[1].shape[0], :] = dot(tabs[1][...], rhs[...])


def join(out, edges, direct, source, masks, half):
    for par in range(2):
        def work(at, marked, par=par):
            rows = out[par, at, :]
            out[par, at, :] = (rows * masks[par, at, 0:1] if marked else rows) + direct * source(par, at)

        over_rows_marked(half, CHUNK, work)
        edge = edges[par].shape[0] // 2
        first, last = pl.ds(0, edge), pl.ds(half - edge, edge)
        out[par, first, :] += edges[par][:edge] * masks[par, first, 1:2]
        out[par, last, :] += edges[par][edge:] * masks[par, last, 2:3]


INVERSE_PI = 1.0 / math.pi
PI_HIGH, PI_MID = 3.140625, math.pi - 3.140625
SINE = [(-1.0) ** i / math.factorial(2 * i + 1) for i in range(6)]
COSINE = [(-1.0) ** i / math.factorial(2 * i) for i in range(7)]


def reduced(x):
    turns = jnp.floor(x * INVERSE_PI + 0.5)
    sign = 1.0 - 2.0 * (turns - 2.0 * jnp.floor(0.5 * turns))
    return (x - turns * PI_HIGH) - turns * PI_MID, sign


def poly(square, terms):
    total = terms[-1]
    for term in terms[-2::-1]:
        total = total * square + term
    return total


def sine(x):
    left, sign = reduced(x)
    return sign * left * poly(left * left, SINE)


def sine_cosine(x):
    left, sign = reduced(x)
    square = left * left
    return sign * left * poly(square, SINE), sign * poly(square, COSINE)


def fine_dot(a, b, dims=(((1,), (0,)), ((), ()))):
    (ah, al), (bh, bl) = parts(a), parts(b)
    one = lambda x, y: lax.dot_general(x, y, dims, preferred_element_type=F32)
    return one(ah, bh) + (one(al, bh) + one(ah, bl))


def row_of(ref):
    return ref[...].reshape(1, ref.shape[0])


def flat_rows(land):
    n, rows, width = land.shape
    if rows % 16 == 0:
        return land[...].reshape(n * rows, width)
    return jnp.concatenate([land[i].astype(F32) for i in range(n)], axis=0).astype(BF16)


def twice(rows):
    return jnp.concatenate([rows, rows], axis=1)


def blocks_of(matrix, rows):
    height, width = matrix.shape
    padded = matrix if rows == height else jnp.concatenate([matrix, jnp.zeros((rows - height, width), F32)], axis=0)
    none = jnp.zeros_like(padded)
    return jnp.concatenate(
        [jnp.concatenate([padded, none], axis=1), jnp.concatenate([none, padded], axis=1)], axis=0
    )


def of_parity(rows, par):
    lane = lax.broadcasted_iota(jnp.int32, rows.shape, 1)
    return jnp.where((lane >= rows.shape[1] // 2) == (par == 1), rows, 0.0)


def hidden_layers(ptable, w1, b1, w2, b2):
    pre1 = fine_dot(ptable[...], blocks_of(w1[...], ptable.shape[1] // 2)) + twice(row_of(b1))
    h1, c1 = sine_cosine(pre1)
    pre2 = fine_dot(h1, blocks_of(w2[...], w2.shape[0])) + twice(row_of(b2))
    return h1, c1, pre2


def decay_at(par, rows, start, rates):
    m = lax.broadcasted_iota(jnp.int32, (rows, rates.shape[1]), 0) + start
    return jnp.exp((2 * m + par).astype(F32) * -rates)


def make_filter(tabs, rhs, w3, rates, hidden, filt, filt_spec, e_filt_spec, par, o):
    wave, _, _, e_wave, _, _ = tabs
    half, edge = wave.shape[1] // 3, e_wave.shape[1] // 6
    last = w3[:, o, :]
    filt[...] = fine_dot(of_parity(hidden[...], par), jnp.concatenate([last, last], axis=0))

    def fill(at):
        filt[at, :] = filt[at, :] * decay_at(par, CHUNK, at.start, rates[o : o + 1, :])
        put_parts(rhs, at, 0, half, filt[at, :])

    over_rows(half, CHUNK, fill)
    filt_spec[o, par] = dot(wave[...], rhs[0 : 3 * half, :]) * (1.0 / half)
    window = filt[pl.ds(0, edge), :]
    high, low = parts(jnp.concatenate([window, window], axis=0))
    e_filt_spec[o, par] = dot(e_wave[...], jnp.concatenate([high, low, high], axis=0)) * (1.0 / edge)


def turn_filters(tabs, filt_spec, e_filt_spec):
    wave, _, twist, e_wave, _, e_twist = tabs
    half, edge = wave.shape[1] // 3, e_wave.shape[1] // 6
    for o in range(2):
        def turn(at, o=o):
            real, imag = turned(pair(filt_spec.at[o], 1, at, half), twist, at)
            filt_spec[o, 2, at, :] = real
            filt_spec[o, 2, pl.ds(pl.multiple_of(at.start + half, 8), at.size), :] = imag

        over_rows(half, CHUNK, turn)
        n = 2 * edge
        real, imag = turned(pair(e_filt_spec.at[o], 1, pl.ds(0, n), n), e_twist, pl.ds(0, n))
        e_filt_spec[o, 2] = jnp.concatenate([real, imag], axis=0)


PAD = 8


def short_rows(z, which, par, at, marked, masks, taps, tap_bias):
    size, start = at.size, at.start
    here = z[which, par, pl.ds(pl.multiple_of(start + PAD, 8), size), :]
    wide = pl.ds(pl.multiple_of(start, 8), size + PAD)
    same_before = z[which, par, wide, :][PAD - 1 : PAD - 1 + size]
    if par == 0:
        other = z[which, 1, wide, :][PAD - 1 : PAD - 1 + size]
    else:
        other = z[which, 0, pl.ds(pl.multiple_of(start + PAD, 8), size), :]
    one, two = other, same_before
    if marked:
        one, two = masks[par, at, 3:4] * one, masks[par, at, 4:5] * two
    tap = lambda j: taps[j, which : which + 1, :]
    return tap_bias[which : which + 1, :] + tap(0) * here + tap(1) * one + tap(2) * two, here, one, two


def put_zpre(z, normed, weights, in_bias, which, par, half):
    zero = jnp.zeros((PAD, z.shape[3]), F32)
    z[which, par, 0:PAD, :] = zero
    z[which, par, PAD + half : PAD + half + PAD, :] = zero
    z[which, par, PAD : PAD + half, :] = dot(normed, weights) + in_bias[which : which + 1, :]


def make_short(short, z, masks, taps, tap_bias, half, which):
    for par in range(2):
        def work(at, marked, par=par):
            short[which, par, at, :] = short_rows(z, which, par, at, marked, masks, taps, tap_bias)[0]

        over_rows_marked(half, CHUNK, work)


def layer_norm_parts(values):
    center = jnp.mean(values, axis=-1, keepdims=True)
    centred = values - center
    spread = jnp.mean(centred * centred, axis=-1, keepdims=True)
    scale = lax.rsqrt(spread + EPSILON)
    return centred * scale, scale


def parity_matrix(rows):
    half = rows // 2
    at = lax.broadcasted_iota(jnp.int32, (rows, rows), 0)
    wanted = jnp.where(at < half, 2 * at, 2 * (at - half) + 1)
    return (lax.broadcasted_iota(jnp.int32, (rows, rows), 1) == wanted).astype(F32).astype(BF16)


def make_masks(masks, segments, half):
    seg = segments[...].astype(F32)
    length = seg.shape[1]
    place = lax.broadcasted_iota(jnp.int32, (1, length), 1)
    one = lambda ok: jnp.where(ok, 1.0, 0.0)
    rows = [one(seg == 1.0), one(seg == 0.0), one(seg == 2.0)]
    for j in (1, 2):
        rows.append(jnp.where(place >= j, one(pltpu.roll(seg, j, 1) == seg), 0.0))
    marks = jnp.concatenate(rows + [jnp.zeros((3, length), F32)], axis=0).astype(BF16)
    at = lax.broadcasted_iota(jnp.int32, (half, length), 0)
    column = lax.broadcasted_iota(jnp.int32, (half, length), 1)
    for par in range(2):
        choose = jnp.where(column == 2 * at + par, 1.0, 0.0).astype(BF16)
        masks[par, 0:half, :] = lax.dot_general(choose, marks, ROW_CONTRACT, preferred_element_type=F32)
        masks[par, half : half + PAD, :] = jnp.zeros((PAD, 8), F32)


def front(
    dp, tensor,
    tokens, cotangent, segments, gain, shift, in_shard, b_in, taps, tap_bias, ptable, w1, b1, w2, b2, w3, rates, direct,
    twist, e_wave, e_back, e_twist, out_shard, up_shard, wave_in, wave_back_in,
    w_in_out, out_full, up_all, cot_full, norm_out, gated_out, own_gated, masks_out,
    z_out, filt_out, e_filt_out, spec_out, e_spec_out, conv_out, hidden_out,
    wave, wave_back, in_own, in_land, w_in, cot_own, norm_full, gated, masks, z, filt_spec, e_filt_spec, spec, e_spec, conv, hidden,
    short, rhs, rhs_even, rhs_odd, filt, send, recv, local,
):
    tabs = (wave, wave_back, twist, e_wave, e_back, e_twist)
    half = wave.shape[1] // 3
    count = tokens.shape[1]
    own = count // 2
    place = Place(dp, tensor)
    sems, copies = Sems(send, recv), LocalCopies(local)
    barrier = place.greet()
    wave_loaded, back_loaded = copies.start(wave_in, wave), copies.start(wave_back_in, wave_back)
    origins, t_origins = dp_origins(place), tensor_origins(place)

    for which in range(3):
        in_own[which] = in_shard[:, which, :]
    parity = parity_matrix(count)
    normal, _ = layer_norm_parts(dot(parity, tokens[0]))
    low = (normal * row_of(gain) + row_of(shift)).astype(BF16)
    for par in range(2):
        norm_full[par, place.t] = low[par * own : (par + 1) * own]
    place.met(barrier)

    norms = [
        tensor_gather(place, sems, norm_full.at[par, place.t], lambda i, par=par: norm_full.at[par, i]) for par in range(2)
    ]
    ins = [dp_gather(place, sems, in_own.at[p], lambda i, p=p: in_land.at[p, i]) for p in range(3)]
    outs = dp_gather(place, sems, out_shard, lambda i: out_full.at[place.t, i])
    ups = [
        dp_gather(place, sems, up_shard.at[at], lambda i, at=at: up_all.at[i, at]) for at in row_pieces(up_shard.shape[0])
    ]
    cots = [tensor_gather(place, sems, cot_own.at[par], lambda i, par=par: cot_full.at[par, i]) for par in range(2)]
    for gather in (ins[0], *norms, outs):
        gather.start()
    own_ins = [copies.start(in_own.at[p], in_land.at[p, place.d]) for p in range(3)]
    own_out = copies.start(out_shard, out_full.at[place.t, place.d])
    copies.start(up_shard, up_all.at[place.d])

    shuffled = dot(parity, cotangent[0]).astype(BF16)
    for par in range(2):
        cot_own[par] = shuffled[par * own : (par + 1) * own]
        copies.start(cot_own.at[par], cot_full.at[par, place.t])
    make_masks(masks, segments, half)
    copies.start(masks, masks_out)
    hidden[...] = sine(hidden_layers(ptable, w1, b1, w2, b2)[2])
    copies.start(hidden, hidden_out)
    net = (w3, rates, hidden, filt, filt_spec, e_filt_spec)
    copies.take(wave_loaded)
    make_filter(tabs, rhs, *net, 0, 0)
    ins[0].forward(origins)
    ins[1].start()
    outs.forward(origins)
    make_filter(tabs, rhs, *net, 0, 1)
    for gather in norms:
        gather.forward(t_origins)
    make_filter(tabs, rhs, *net, 1, 0)
    ins[1].forward(origins)
    for gather in (ins[2], *ups[:-1]):
        gather.start()
    outs.arrived()
    copies.take(own_out)
    out_rows = tensor_gather(place, sems, out_full.at[place.t], lambda i: out_full.at[i])
    for gather in (out_rows, *cots):
        gather.start()
    make_filter(tabs, rhs, *net, 1, 1)
    turn_filters(tabs, filt_spec, e_filt_spec)
    copies.start(filt_spec, filt_out)
    copies.start(e_filt_spec, e_filt_out)
    for gather in norms:
        gather.arrived()
    copies.start(norm_full, norm_out)

    def project(which):
        ins[which].arrived()
        copies.take(own_ins[which])
        w_in[which] = flat_rows(in_land.at[which])
        for par in range(2):
            put_zpre(z, norm_full[par].reshape(half, -1), w_in[which], b_in, which, par, half)
        make_short(short, z, masks, taps, tap_bias, half, which)

    def convolve(o, source, between):
        analyse(tabs, rhs, source, spec.at[o], e_spec.at[o], masks)
        copies.start(spec.at[o], spec_out.at[o])
        copies.start(e_spec.at[o], e_spec_out.at[o])
        between()
        edges = spectra_product(
            tabs, filt_spec.at[o], e_filt_spec.at[o], spec.at[o], e_spec.at[o], rhs_even, rhs_odd, False, False
        )
        synthesise(tabs, rhs_even, conv.at[o], 0)
        synthesise(tabs, rhs_odd, conv.at[o], 1)
        join(conv.at[o], edges, direct[o : o + 1, :], source, masks, half)
        copies.start(conv.at[o], conv_out.at[o])

    project(0)
    copies.take(back_loaded)
    convolve(0, lambda par, at: short[0, par, at, :], lambda: None)
    ins[2].forward(origins)
    out_rows.forward(t_origins)
    ups[-1].start()
    project(1)
    for gather in ups[:-1]:
        gather.forward(origins)
    convolve(1, lambda par, at: short[1, par, at, :] * conv[0, par, at, :], lambda: None)
    for gather in cots:
        gather.forward(t_origins)
    project(2)
    copies.start(w_in, w_in_out)
    copies.start(z, z_out)
    for par in range(2):
        for block in range(tensor):
            values = short[2, par, block * own : (block + 1) * own, :] * conv[1, par, block * own : (block + 1) * own, :]
            gated[par, block] = values.astype(BF16)
    trades = []
    for i in range(1, tensor):
        to = place.t_at(i)
        for par in range(2):
            trades.append(sems.copy(gated.at[par, to], own_gated.at[place.t, par], {"tensor": to}))
    for copy in trades:
        copy.start()
    ups[-1].forward(origins)
    for par in range(2):
        copies.start(gated.at[par, place.t], own_gated.at[place.t, par])
    copies.start(gated, gated_out)
    for gather in (*cots, *ups, out_rows):
        gather.arrived()
    for copy in trades:
        copy.wait()
    for gather in (*norms, *ins, outs, *ups, *cots, out_rows):
        gather.finish()
    copies.finish()


MESH = pl.DeviceIdType.MESH


class Place:
    def __init__(self, dp, tensor):
        self.dp, self.tensor = dp, tensor
        self.rows = 4 if dp % 4 == 0 else 1
        self.cols = dp // self.rows
        self.cores = 2 if tensor % 2 == 0 else 1
        self.ys = tensor // self.cores
        self.d, self.t = lax.axis_index("dp"), lax.axis_index("tensor")
        self.a, self.b = self.d // self.cols, lax.rem(self.d, self.cols)
        self.y, self.c = self.t // self.cores, lax.rem(self.t, self.cores)

    def a_at(self, i):
        return lax.rem(self.a + i + self.rows, self.rows) * self.cols + self.b

    def b_at(self, i):
        return self.a * self.cols + lax.rem(self.b + i + self.cols, self.cols)

    def y_at(self, i):
        return lax.rem(self.y + i + self.ys, self.ys) * self.cores + self.c

    def core_peer(self):
        return self.y * self.cores + 1 - self.c

    def t_at(self, i):
        return lax.rem(self.t + i + self.tensor, self.tensor)

    def d_at(self, i):
        return lax.rem(self.d + i + self.dp, self.dp)

    def greet(self, dp=True, all_dp=False):
        peers = [{"tensor": self.t_at(i)} for i in range(1, self.tensor)]
        if all_dp:
            peers += [{"dp": self.d_at(i)} for i in range(1, self.dp)]
        elif dp:
            peers += [{"dp": self.a_at(i)} for i in range(1, self.rows)]
            peers += [{"dp": self.b_at(i)} for i in range(1, self.cols)]
        barrier = pltpu.get_barrier_semaphore()
        for peer in peers:
            pl.semaphore_signal(barrier, inc=1, device_id=peer, device_id_type=MESH)
        self.expected = len(peers)
        return barrier

    def met(self, barrier):
        pl.semaphore_wait(barrier, self.expected)


class Sems:
    def __init__(self, send, recv):
        self.send, self.recv, self.used = send, recv, 0

    def copy(self, src, dst, device):
        i = self.used
        self.used += 1
        return pltpu.make_async_remote_copy(
            src_ref=src, dst_ref=dst, send_sem=self.send.at[i], recv_sem=self.recv.at[i],
            device_id=device, device_id_type=MESH,
        )


class LocalCopies:
    def __init__(self, sems):
        self.sems, self.open, self.used = sems, [], 0

    def start(self, src, dst):
        copy = pltpu.make_async_copy(src, dst, self.sems.at[self.used])
        self.used += 1
        copy.start()
        self.open.append(copy)
        return copy

    def take(self, copy):
        copy.wait()
        self.open = [other for other in self.open if other is not copy]

    def finish(self):
        for copy in self.open:
            copy.wait()


class Gather:
    def __init__(self, sems, source, slot, own, far, near, device):
        self.first = [sems.copy(source, slot(own), device(i)) for i in far]
        self.near = [sems.copy(source, slot(own), device(i)) for i in near]
        self.sems, self.slot, self.device, self.near_ids = sems, slot, device, near
        self.second = []

    def start(self):
        for copy in self.first + self.near:
            copy.start()

    def forward(self, origins, which=None):
        for i, origin in enumerate(origins):
            if which is not None and i not in which:
                continue
            self.first[i].wait_recv()
            for peer in self.near_ids:
                copy = self.sems.copy(self.slot(origin), self.slot(origin), self.device(peer))
                copy.start()
                self.second.append(copy)

    def arrived(self):
        for copy in self.near + self.second:
            copy.wait_recv()

    def finish(self):
        for copy in self.first + self.near + self.second:
            copy.wait_send()


def tensor_gather(place, sems, source, slot):
    near = [place.core_peer()] if place.cores == 2 else []
    return Gather(
        sems, source, slot, place.t, [place.y_at(i) for i in range(1, place.ys)], near, lambda i: {"tensor": i}
    )


def row_pieces(rows):
    count = 2 if rows % 32 == 0 else 1
    return [pl.ds(i * (rows // count), rows // count) for i in range(count)]


def dp_gather(place, sems, source, slot):
    return Gather(
        sems, source, slot, place.d, [place.a_at(i) for i in range(1, place.rows)],
        [place.b_at(i) for i in range(1, place.cols)], lambda i: {"dp": i},
    )


def tensor_origins(place):
    return [place.y_at(-i) for i in range(1, place.ys)]


def dp_origins(place):
    return [place.a_at(-i) for i in range(1, place.rows)]


def gather_counts(dp, tensor):
    cores = 2 if tensor % 2 == 0 else 1
    rows = 4 if dp % 4 == 0 else 1
    far_t, near_t, far_d, near_d = tensor // cores - 1, cores - 1, rows - 1, dp // rows - 1
    return far_t + near_t + far_t * near_t, far_d + near_d + far_d * near_d


def vmem_specs(n):
    return [pl.BlockSpec(memory_space=pltpu.VMEM)] * n


def mix_shapes(half, width, hidden_width, filter_parts=3):
    edge4 = half // 4
    return dict(
        z=((3, 2, half + 2 * PAD, width), F32),
        filt_spec=((2, filter_parts, 2 * half, width), F32),
        e_filt_spec=((2, filter_parts, edge4, width), F32),
        spec=((2, 2, 2 * half, width), F32),
        e_spec=((2, 2, edge4, width), F32),
        conv=((2, 2, half, width), F32),
        hidden=((half, 2 * hidden_width), F32),
    )


def front_call(dp, tensor, args, half, hidden_width):
    S = jax.ShapeDtypeStruct
    V = pltpu.VMEM
    _, count, model = args[0].shape
    rows, _, channels = args[5].shape
    units = args[22].shape[1]
    own = count // 2
    shapes = mix_shapes(half, channels, hidden_width)
    norm, gate, mask = ((2, tensor, own, model), BF16), ((2, tensor, own, channels), BF16), ((2, half + PAD, 8), F32)
    outs = [
        S((3, model, channels), BF16), S((tensor, dp, rows, channels), BF16), S((dp, rows, units), BF16),
        S(*norm), S(*norm), S(*gate), S((tensor, 2, own, channels), BF16), S(*mask),
    ] + [S(*v) for v in shapes.values()]
    per_t, per_d = gather_counts(dp, tensor)
    copies = 5 * per_t + 6 * per_d + 2 * (tensor - 1)
    hbm = pl.BlockSpec(memory_space=pl.ANY)
    return pl.pallas_call(
        functools.partial(front, dp, tensor),
        out_shape=outs,
        in_specs=vmem_specs(21) + [hbm] * 4,
        out_specs=[hbm] * len(outs),
        scratch_shapes=[
            V(args[23].shape, BF16), V(args[24].shape, BF16),
            V((3, rows, channels), BF16), V((3, dp, rows, channels), BF16), V((3, model, channels), BF16),
            V((2, own, model), BF16), V(*norm), V(*gate), V(*mask),
        ] + [V(*v) for v in shapes.values()] + [
            V((3, 2, half, channels), F32), V((3 * half, channels), BF16), V((6 * half, channels), BF16),
            V((6 * half, channels), BF16), V((half, channels), F32),
            pltpu.SemaphoreType.DMA((copies,)), pltpu.SemaphoreType.DMA((copies,)), pltpu.SemaphoreType.DMA((32,)),
        ],
        compiler_params=pltpu.CompilerParams(collective_id=0, has_side_effects=True, vmem_limit_bytes=VMEM_LIMIT),
        name="front",
    )(*args)


def far_moves(place, sems, far_out, far_in):
    return [sems.copy(far_out.at[i - 1], far_in.at[i - 1], {"dp": place.a_at(i)}) for i in range(1, place.rows)]


def far_total(moves, keep, far_in):
    out = keep[...]
    for i, copy in enumerate(moves):
        copy.wait_recv()
        out = out + far_in[i].astype(F32)
    return out


class WeightReduce:
    def __init__(self, place, sems, low, near_in, keep, far_out, far_in):
        self.place, self.low, self.near_in, self.keep, self.far_out, self.far_in = place, low, near_in, keep, far_out, far_in
        own = lambda i: lax.rem(place.b + i, place.cols)
        self.near = [
            sems.copy(low.at[own(i)], near_in.at[i - 1], {"dp": place.b_at(i)}) for i in range(1, place.cols)
        ]
        self.far = [] if far_in is None else far_moves(place, sems, far_out, far_in)

    def start(self):
        for copy in self.near:
            copy.start()

    def combine(self):
        place = self.place
        for copy in self.near:
            copy.wait_recv()
        for i in list(range(1, place.rows)) + [0]:
            a = lax.rem(place.a + i, place.rows)
            total = self.low[place.b, a].astype(F32)
            for j in range(place.cols - 1):
                total = total + self.near_in[j, a].astype(F32)
            if i:
                self.far_out[i - 1] = total.astype(BF16)
                if self.far:
                    self.far[i - 1].start()
            else:
                self.keep[...] = total

    def total(self):
        return far_total(self.far, self.keep, self.far_in)

    def finish(self):
        for copy in self.near + self.far:
            copy.wait_send()


class Reduce:
    def __init__(self, place, sems, near_out, near_in, far_out, far_in):
        self.place, self.near_in, self.near_out, self.far_in, self.far_out = place, near_in, near_out, far_in, far_out
        peer = {"tensor": place.core_peer()}
        self.near = [sems.copy(near_out.at[i], near_in.at[i], peer) for i in range(place.ys)] if place.cores == 2 else []
        self.far = []
        if far_in is not None:
            self.far = [
                sems.copy(far_out.at[i - 1], far_in.at[i - 1], {"tensor": place.y_at(i)}) for i in range(1, place.ys)
            ]

    def order(self):
        place = self.place
        blocks = []
        for i in [0] + list(range(place.ys - 1, 0, -1)):
            for other in range(place.cores):
                owner = place.y_at(i)
                blocks.append((i, other, owner + (1 - 2 * place.c) if other else owner))
        return blocks

    def combine(self, keep, rows, send=True):
        for i in list(range(1, self.place.ys)) + [0]:
            if self.near:
                self.near[i].wait_recv()

            def work(at, i=i):
                total = keep[i, at, :]
                if self.near:
                    total = total + self.near_in[i, at, :].astype(F32)
                if i:
                    self.far_out[i - 1, at, :] = total.astype(BF16)
                else:
                    keep[0, at, :] = total

            over_rows(rows, 32, work)
            if i and send:
                self.far[i - 1].start()

    def total(self, keep, at):
        out = keep[0, at, :]
        for i in range(self.place.ys - 1):
            out = out + self.far_in[i, at, :].astype(F32)
        return out

    def arrived(self):
        for copy in self.far:
            copy.wait_recv()

    def finish(self):
        for copy in self.near + self.far:
            copy.wait_send()


GELU_SCALE = math.sqrt(2.0 / math.pi)


def gelu_and_slope(x):
    square = x * x
    bent = jnp.tanh(GELU_SCALE * (x + 0.044715 * (x * square)))
    slope = 0.5 * (1.0 + bent) + 0.5 * x * (1.0 - bent * bent) * (GELU_SCALE + (3.0 * 0.044715 * GELU_SCALE) * square)
    return 0.5 * x * (1.0 + bent), slope


def fold8(x):
    return jnp.sum(x.reshape(-1, 8, x.shape[1]), axis=0)


def norm_back(grad, normal, scale, gain):
    k = grad * gain
    return scale * (k - jnp.mean(k, axis=-1, keepdims=True) - normal * jnp.mean(k * normal, axis=-1, keepdims=True))


def put_weight_grad(place, grad, left, right, low):
    rows = low.shape[2]

    @pl.loop(0, 2)
    def _(par):
        flat = lambda ref: ref[par].reshape(-1, ref.shape[-1])
        part = lax.dot_general(flat(left), flat(right), COLUMN_CONTRACT, preferred_element_type=F32)

        @pl.when(par == 0)
        def _():
            grad[...] = part

        @pl.when(par != 0)
        def _():
            grad[...] += part

    for a in range(place.rows):
        for b in range(place.cols):
            start = (a * place.cols + b) * rows
            low[b, a] = grad[start : start + rows, :].astype(BF16)


def middle(
    dp, tensor,
    tokens, cotangent, own_gated, out_full, out_bias, gain, shift, up_bias, down_bias, up_in, cot_in, down_shard,
    d_mixed_out, d_mix_low, mlp_own, mlp_far, down_far, down_keep, g_up, row_sums, up_sums,
    up_all, cot_full, mixed, normal, scales, norm_full, down_all, slopes, pre, acts, d_pres, keep, near_out, near_in, far_out, far_in,
    keep_mlp, near_out_mlp, near_in_mlp, far_mlp, cot_rows, grad, low_down, low_up, down_near, down_far_v, acc, up_acc,
    send, recv, local,
):
    _, count, model = tokens.shape
    own = count // 2
    place = Place(dp, tensor)
    sems, copies = Sems(send, recv), LocalCopies(local)
    barrier = place.greet()
    up_loaded, cot_loaded = copies.start(up_in, up_all), copies.start(cot_in, cot_full)
    parity = parity_matrix(count)
    total = dot(parity, tokens[0]) + row_of(out_bias)
    cot_rows[...] = dot(parity, cotangent[0])
    place.met(barrier)
    downs = [
        dp_gather(place, sems, down_shard.at[at], lambda i, at=at: down_all.at[i, at])
        for at in row_pieces(down_shard.shape[0])
    ]
    for gather in downs:
        gather.start()
    own_down = copies.start(down_shard, down_all.at[place.d])
    for block in range(tensor):
        rows = jnp.concatenate([own_gated[block, 0], own_gated[block, 1]], axis=0)
        total += lax.dot_general(rows, out_full[block], ROW_CONTRACT, preferred_element_type=F32)
    mixed[...] = total
    xhat, scale = layer_norm_parts(total)
    normal[...] = xhat
    scales[...] = jnp.broadcast_to(scale, scales.shape)
    low = (xhat * row_of(gain) + row_of(shift)).astype(BF16)
    for par in range(2):
        norm_full[par, place.t] = low[par * own : (par + 1) * own]
    gathers = [
        tensor_gather(place, sems, norm_full.at[par, place.t], lambda i, par=par: norm_full.at[par, i]) for par in range(2)
    ]
    for gather in gathers:
        gather.start()
    reduce = Reduce(place, sems, near_out, near_in, far_out, far_in)
    up_acc[...] = jnp.zeros_like(up_acc)

    def block_rows(ref, owner):
        return jnp.concatenate([ref[0, owner], ref[1, owner]], axis=0)

    def forward(owner):
        pre[...] = dot(block_rows(norm_full, owner), up_all[...]) + row_of(up_bias)
        for par in range(2):
            def work(at, par=par):
                rows = pl.ds(pl.multiple_of(par * own + at.start, 16), at.size)
                act, slope = gelu_and_slope(pre[rows, :])
                acts[par, owner, at, :] = act.astype(BF16)
                slopes[owner, rows, :] = slope

            over_rows(own, 16, work)

    def backward(step, other, owner):
        pre[...] = dot(block_rows(cot_full, owner), flat_rows(down_all))
        for par in range(2):
            def work(at, par=par):
                rows = pl.ds(pl.multiple_of(par * own + at.start, 16), at.size)
                d_pre = (pre[rows, :] * slopes[owner, rows, :]).astype(BF16)
                d_pres[par, owner, at, :] = d_pre
                up_acc[...] += fold8(d_pre.astype(F32))

            over_rows(own, 16, work)
        part = lax.dot_general(block_rows(d_pres, owner), up_all[...], ROW_CONTRACT, preferred_element_type=F32)
        if other:
            near_out[step] = part.astype(BF16)
            reduce.near[step].start()
        else:
            keep[step] = part

    blocks = reduce.order()
    copies.take(up_loaded)
    copies.take(cot_loaded)
    forwarded = False
    for step, other, owner in blocks:
        if step == 0 and other:
            for gather in gathers:
                for copy in gather.near:
                    copy.wait_recv()
        if step and not forwarded:
            for gather in downs[:-1]:
                gather.forward(dp_origins(place))
            for gather in gathers:
                gather.forward(tensor_origins(place))
            downs[-1].forward(dp_origins(place))
            forwarded = True
        if step and other:
            for gather in gathers:
                gather.second[place.ys - 1 - step].wait_recv()
        forward(owner)
    if not forwarded:
        for gather in (*gathers, *downs):
            gather.forward(tensor_origins(place) if gather in gathers else dp_origins(place))
    grad_down = WeightReduce(place, sems, low_down, down_near, down_keep, down_far_v, None)
    put_weight_grad(place, grad, cot_full, acts, low_down)
    grad_down.start()
    for gather in downs:
        gather.arrived()
    copies.take(own_down)
    for block in blocks[::-1]:
        backward(*block)
    reduce.combine(keep, count)
    put_weight_grad(place, grad, norm_full, d_pres, low_up)
    copies.start(low_up, g_up)
    sums = Reduce(place, sems, near_out_mlp, near_in_mlp, far_mlp, None)
    for step, other, owner in blocks[::-1]:
        part = lax.dot_general(block_rows(acts, owner), flat_rows(down_all), ROW_CONTRACT, preferred_element_type=F32)
        if other:
            near_out_mlp[step] = part.astype(BF16)
            sums.near[step].start()
        else:
            keep_mlp[step] = part
    sums.combine(keep_mlp, count, send=False)
    if place.ys > 1:
        copies.start(far_mlp, mlp_far)

    def own_rows(at):
        mlp_own[at, :] = keep_mlp[0, at, :] + mixed[at, :] + row_of(down_bias)

    over_rows(count, 32, own_rows)
    up_sums[...] = jnp.sum(up_acc[...], axis=0, keepdims=True)
    for gather in (*gathers, *downs):
        gather.finish()
    acc[...] = jnp.zeros_like(acc)
    reduce.arrived()

    def back(at):
        grad_rows = reduce.total(keep, at)
        hat = normal[at, :]
        out_grad = cot_rows[at, :]
        d_mixed = out_grad + norm_back(grad_rows, hat, scales[at, 0:1], row_of(gain))
        mixed[at, :] = d_mixed
        d_mix_low[at, :] = d_mixed.astype(BF16)
        acc[0:8, :] += fold8(grad_rows * hat)
        acc[8:16, :] += fold8(grad_rows)
        acc[16:24, :] += fold8(d_mixed)
        acc[24:32, :] += fold8(out_grad)

    over_rows(count, 64, back)
    copies.start(mixed, d_mixed_out)
    grad_down.combine()
    if place.rows > 1:
        copies.start(down_far_v, down_far)
    for i in range(4):
        row_sums[i : i + 1, :] = jnp.sum(acc[8 * i : 8 * i + 8, :], axis=0, keepdims=True)
    for group in (reduce, sums, grad_down):
        group.finish()
    copies.finish()


def middle_call(dp, tensor, args):
    S = jax.ShapeDtypeStruct
    _, count, model = args[0].shape
    units = args[9].shape[1]
    own, cores, rows_d = count // 2, 2 if tensor % 2 == 0 else 1, 4 if dp % 4 == 0 else 1
    ys, farther = tensor // cores, max(tensor // cores - 1, 1)
    rows, low_rows = ((count, model), F32), ((ys, count, model), BF16)
    blocks, norms = ((2, tensor, own, units), BF16), ((2, tensor, own, model), BF16)
    low_grad = ((dp // rows_d, rows_d, model // dp, units), BF16)
    far = ((farther, count, model), BF16)
    far_grad = ((max(rows_d - 1, 1), model // dp, units), BF16)
    near_grad = ((max(dp // rows_d - 1, 1), rows_d, model // dp, units), BF16)
    kept = ((model // dp, units), F32)
    per_t, per_d = gather_counts(dp, tensor)
    total = 2 * per_t + 2 * per_d + 3 * ys + dp // rows_d
    hbm, vmem = pl.BlockSpec(memory_space=pl.ANY), pl.BlockSpec(memory_space=pltpu.VMEM)
    return pl.pallas_call(
        functools.partial(middle, dp, tensor),
        out_shape=[
            S(*rows), S((count, model), BF16), S(*rows), S(*far), S(*far_grad), S(*kept), S(*low_grad), S((4, model), F32), S((1, units), F32),
        ],
        in_specs=vmem_specs(len(args) - 3) + [hbm] * 3,
        out_specs=[hbm, vmem, vmem, hbm, hbm, vmem, hbm, vmem, vmem],
        scratch_shapes=[
            pltpu.VMEM((model, units), BF16), pltpu.VMEM(*norms),
            pltpu.VMEM(*rows), pltpu.VMEM(*rows), pltpu.VMEM((count, 128), F32), pltpu.VMEM(*norms),
            pltpu.VMEM((dp, model // dp, units), BF16), pltpu.VMEM((tensor, count, units), F32), pltpu.VMEM((count, units), F32),
            pltpu.VMEM(*blocks), pltpu.VMEM(*blocks), pltpu.VMEM((ys, count, model), F32),
            pltpu.VMEM(*low_rows), pltpu.VMEM(*low_rows), pltpu.VMEM(*far), pltpu.VMEM(*far),
            pltpu.VMEM((ys, count, model), F32), pltpu.VMEM(*low_rows), pltpu.VMEM(*low_rows), pltpu.VMEM(*far),
            pltpu.VMEM(*rows), pltpu.VMEM((model, units), F32), pltpu.VMEM(*low_grad), pltpu.VMEM(*low_grad),
            pltpu.VMEM(*near_grad), pltpu.VMEM(*far_grad),
            pltpu.VMEM((32, model), F32), pltpu.VMEM((8, units), F32),
            pltpu.SemaphoreType.DMA((total,)), pltpu.SemaphoreType.DMA((total,)), pltpu.SemaphoreType.DMA((8,)),
        ],
        compiler_params=pltpu.CompilerParams(collective_id=1, has_side_effects=True, vmem_limit_bytes=VMEM_LIMIT),
        name="middle",
    )(*args)


def order_matrix(rows):
    half = rows // 2
    at = lax.broadcasted_iota(jnp.int32, (rows, rows), 0)
    wanted = lax.rem(at, 2) * half + at // 2
    return (lax.broadcasted_iota(jnp.int32, (rows, rows), 1) == wanted).astype(F32).astype(BF16)


MISC, TAPS, SMALL_ROWS = 0, 8, 24


def rear(
    dp, tensor,
    tokens, d_mix_low, row_sums, up_sums, gain, taps, tap_bias, ptable, w1, b1, w2, b2, w3, rates, direct,
    d_mixed_in, mlp_own, mlp_far, down_far, down_keep_in, g_up, norm_in, gated_in, w_in_in, out_in, masks_in,
    wave_in, wave_back_in, twist, e_wave, e_back, e_twist,
    z_in, filt_in, e_filt_in, spec_in, e_spec_in, conv_in, hidden_in,
    output, grad_tokens, o_down, o_up, o_in, o_out, o_small, o_first, o_early, o_late,
    wave, wave_back, masks, z, filt_spec, e_filt_spec, spec, e_spec, conv, hidden,
    d_mixed, norm_full, gated, w_in, w_out, d_mix_full, mlp_in, low_up,
    short, rhs_even, rhs_odd, g, g_spec, e_g_spec, d_short, d_z, acc, normal, scales,
    down_keep, down_land, up_near, up_keep, up_far, up_land,
    in_low, in_near, in_keep, in_far, in_land, out_low, out_near, out_keep, out_far, out_land,
    keep, near_out, near_in, far_out, far_in,
    small, small_in, small_own, small_all, first, first_in, whole, whole_in, whole_own, whole_all,
    early_in, early, early_far, late, late_in, late_sum, late_far, wide,
    send, recv, local,
):
    tabs = (wave, wave_back, twist, e_wave, e_back, e_twist)
    half, width = z.shape[2] - 2 * PAD, z.shape[3]
    _, count, model = tokens.shape
    own = count // 2
    d_filt, rhs = conv, rhs_even
    place = Place(dp, tensor)
    sems, copies = Sems(send, recv), LocalCopies(local)
    barrier = place.greet(all_dp=True)
    loads = {}

    def load(name, src, dst):
        loads[name] = copies.start(src, dst)

    def loaded(*names):
        for name in names:
            copies.take(loads[name])

    load("up", g_up, low_up)
    load("z", z_in, z)
    load("masks", masks_in, masks)
    load("out", out_in.at[place.t], w_out)
    load("conv", conv_in, conv)
    load("wave", wave_in, wave)
    load("filt", filt_in.at[1, 0:2], filt_spec)
    load("e_filt", e_filt_in.at[1, 0:2], e_filt_spec)
    load("wave_back", wave_back_in, wave_back)
    load("gated", gated_in, gated)
    load("norm", norm_in, norm_full)
    load("w_in", w_in_in, w_in)
    load("spec", spec_in.at[1], spec)
    load("e_spec", e_spec_in.at[1], e_spec)
    load("hidden", hidden_in, hidden)
    load("mixed", d_mixed_in, d_mixed)
    load("down", down_keep_in, down_keep)
    for par in range(2):
        d_mix_full[par, place.t] = d_mix_low[par * own : (par + 1) * own, :]
    place.met(barrier)
    gathers = [
        tensor_gather(place, sems, d_mix_full.at[par, place.t], lambda i, par=par: d_mix_full.at[par, i]) for par in range(2)
    ]
    for gather in gathers:
        gather.start()
    downs = far_moves(place, sems, down_far, down_land)
    ups = WeightReduce(place, sems, low_up, up_near, up_keep, up_far, up_land)
    ins = [
        WeightReduce(place, sems, in_low.at[p], in_near.at[p], in_keep.at[p], in_far.at[p], in_land.at[p]) for p in range(3)
    ]
    outs = WeightReduce(place, sems, out_low, out_near, out_keep, out_far, out_land)
    mlp = [sems.copy(mlp_far.at[i - 1], mlp_in.at[i - 1], {"tensor": place.y_at(i)}) for i in range(1, place.ys)]
    for copy in downs:
        copy.start()
    loaded("up")
    ups.start()
    early_trades = [sems.copy(row_sums, early_in.at[i - 1], {"tensor": place.t_at(i)}) for i in range(1, tensor)]
    for copy in early_trades:
        copy.start()

    xhat, scale = layer_norm_parts(dot(parity_matrix(count), tokens[0]))
    normal[...] = xhat
    scales[...] = jnp.broadcast_to(scale, scales.shape)
    small[...] = jnp.zeros_like(small)
    loaded("z", "masks")
    for which in range(3):
        make_short(short, z, masks, taps, tap_bias, half, which)
    loaded("out", "conv")
    for gather in gathers:
        gather.forward(tensor_origins(place))
    for copy in mlp:
        copy.start()
    for gather in gathers:
        gather.arrived()
    for par in range(2):
        g[par] = dot(d_mix_full[par].reshape(half, model), w_out[...])

        def gate(at, par=par):
            grad = g[par, at, :]
            d_short[2, par, at, :] = grad * conv[1, par, at, :]
            short[2, par, at, :] = grad * short[2, par, at, :]

        over_rows(half, CHUNK, gate)

    rows = model // dp

    def weight_grad(reduced, low, left, right):
        total = None
        for par in range(2):
            part = lax.dot_general(left(par), right(par), COLUMN_CONTRACT, preferred_element_type=F32)
            total = part if total is None else total + part
        for a in range(place.rows):
            for b in range(place.cols):
                start = (a * place.cols + b) * rows
                low[b, a] = total[start : start + rows, :].astype(BF16)
        reduced.start()

    def in_grad(p):
        weight_grad(ins[p], in_low.at[p], lambda par: norm_full[par].reshape(half, model), lambda par: d_z[p, par])

    hidden_width = w3.shape[0]
    base = 2 * hidden_width

    def short_back(which):
        acc[...] = jnp.zeros_like(acc)
        for par in range(2):
            d_short[which, par, half : half + PAD, :] = jnp.zeros((PAD, width), F32)
        for par in range(2):
            def work(at, marked, par=par):
                size, start = at.size, at.start
                tap = lambda j: taps[j, which : which + 1, :]
                _, here, one, two = short_rows(z, which, par, at, marked, masks, taps, tap_bias)
                grad = d_short[which, par, at, :]
                acc[0:8, :] += fold8(grad)
                acc[8:16, :] += fold8(grad * here)
                acc[16:24, :] += fold8(grad * one)
                acc[24:32, :] += fold8(grad * two)
                rows_on = pl.ds(pl.multiple_of(start, 8), size + PAD)
                same, other = d_short[which, par, rows_on, :], d_short[which, 1 - par, rows_on, :]
                if marked:
                    same, other = same * masks[par, rows_on, 4:5], other * masks[1 - par, rows_on, 3:4]
                same, other = same[1 : size + 1], other[1 : size + 1] if par else other[:size]
                low = (tap(0) * grad + tap(1) * other + tap(2) * same).astype(BF16)
                d_z[which, par, at, :] = low
                acc[32:40, :] += fold8(low.astype(F32))

            over_rows_marked(half, CHUNK, work)
        total = lambda i: jnp.sum(acc[8 * i : 8 * i + 8, :], axis=0, keepdims=True)
        small[pl.ds(base + MISC + which, 1), :] = total(4)
        small[pl.ds(base + MISC + 3 + which, 1), :] = total(0)
        for j in range(3):
            small[pl.ds(base + TAPS + 3 * j + which, 1), :] = total(1 + j)

    def spread_back(o, source, out):
        analyse(tabs, rhs, source, g_spec.at[o], e_g_spec.at[o], masks)
        loaded("filt", "e_filt")
        edges = spectra_product(
            tabs, filt_spec, e_filt_spec, g_spec.at[o], e_g_spec.at[o], rhs_even, rhs_odd, True, True
        )
        if o:
            load("filt", filt_in.at[0, 0:2], filt_spec)
            load("e_filt", e_filt_in.at[0, 0:2], e_filt_spec)
            loaded("wave_back")
        synthesise(tabs, rhs_even, out, 0)
        synthesise(tabs, rhs_odd, out, 1)
        join(out, edges, direct[o : o + 1, :], source, masks, half)

    def filter_back(o, source, forward_in):
        loaded("spec", "e_spec")
        edges = spectra_product(tabs, spec, e_spec, g_spec.at[o], e_g_spec.at[o], rhs_even, rhs_odd, True, True)
        if o:
            load("spec", spec_in.at[0], spec)
            load("e_spec", e_spec_in.at[0], e_spec)
        acc[...] = jnp.zeros_like(acc)
        for par in range(2):
            def product(at, par=par):
                acc[0:8, :] += fold8(source(par, at) * forward_in(par, at))

            over_rows(half, CHUNK, product)
        small[pl.ds(base + MISC + 6 + o, 1), :] = jnp.sum(acc[0:8, :], axis=0, keepdims=True)
        synthesise(tabs, rhs_even, d_filt.at[o], 0)
        synthesise(tabs, rhs_odd, d_filt.at[o], 1)
        for par in range(2):
            edge = edges[par].shape[0] // 2
            d_filt[o, par, 0:edge, :] += (edges[par][:edge] + edges[par][edge:]) * (half / edge)

            def work(at, par=par):
                decay = decay_at(par, CHUNK, at.start, rates[o : o + 1, :])
                d_filt[o, par, at, :] = d_filt[o, par, at, :] * (decay * (1.0 / half))

            over_rows(half, CHUNK, work)

    grad_one = lambda par, at: short[2, par, at, :]
    grad_zero = lambda par, at: g[par, at, :]
    loaded("wave")
    spread_back(1, grad_one, d_short.at[0])
    for copy in early_trades:
        copy.wait()
    early[...] = jnp.zeros_like(early)
    total = row_sums[...]
    for i in range(tensor - 1):
        total = total + early_in[i]
    early[0:4, 0:model] = total
    early[4:5, 0 : up_sums.shape[1]] = up_sums[...]
    early_moves = [sems.copy(early, early_far.at[i - 1], {"dp": place.d_at(i)}) for i in range(1, dp)]
    for copy in early_moves:
        copy.start()
    loaded("gated")
    weight_grad(
        outs, out_low, lambda par: d_mix_full[par].reshape(half, model), lambda par: gated[par].reshape(half, width)
    )
    ups.combine()
    for par in range(2):
        def gate_again(at, par=par):
            grad = d_short[0, par, at, :]
            d_short[1, par, at, :] = grad * conv[0, par, at, :]
            g[par, at, :] = grad * short[1, par, at, :]

        over_rows(half, CHUNK, gate_again)
    short_back(2)
    loaded("norm")
    in_grad(2)
    spread_back(0, grad_zero, d_short.at[0])
    short_back(1)
    short_back(0)
    loaded("w_in")
    reduce = Reduce(place, sems, near_out, near_in, far_out, far_in)
    for step, other, owner in reduce.order()[::-1]:
        at = pl.ds(pl.multiple_of(owner * own, 16), own)
        part = None
        for p in range(3):
            rows_p = jnp.concatenate([d_z[p, 0, at, :], d_z[p, 1, at, :]], axis=0)
            term = lax.dot_general(rows_p, w_in[p], ROW_CONTRACT, preferred_element_type=F32)
            part = term if part is None else part + term
        if other:
            near_out[step] = part.astype(BF16)
            reduce.near[step].start()
        else:
            keep[step] = part
    in_grad(1)
    reduce.combine(keep, count)
    in_grad(0)
    outs.combine()
    ins[2].combine()

    filter_back(1, grad_one, lambda par, at: short[1, par, at, :] * conv[0, par, at, :])
    ins[1].combine()
    filter_back(0, grad_zero, lambda par, at: short[0, par, at, :])
    loaded("hidden")
    h1, c1, pre2 = hidden_layers(ptable, w1, b1, w2, b2)
    lane = lax.broadcasted_iota(jnp.int32, pre2.shape, 1)
    d_h2 = [None, None]
    for o in range(2):
        last = w3[:, o, :]
        both = jnp.concatenate([last, last], axis=0)
        grads = [fine_dot(hidden[...], d_filt[o, par], COLUMN_CONTRACT) for par in range(2)]
        small[o * hidden_width : (o + 1) * hidden_width, :] = grads[0][:hidden_width] + grads[1][hidden_width:]
        for par in range(2):
            term = fine_dot(d_filt[o, par], both, ROW_CONTRACT)
            d_h2[par] = term if o == 0 else d_h2[par] + term
    d_pre2 = jnp.where(lane < hidden_width, d_h2[0], d_h2[1]) * sine_cosine(pre2)[1]
    d_pre1 = fine_dot(d_pre2, blocks_of(w2[...], hidden_width), ROW_CONTRACT) * c1
    across = lambda x, at: x[:at, :hidden_width] + x[at:, hidden_width:]
    g_first = across(fine_dot(ptable[...], d_pre1, COLUMN_CONTRACT), ptable.shape[1] // 2)
    g_second = across(fine_dot(h1, d_pre2, COLUMN_CONTRACT), hidden_width)
    room, tall = first.shape[0] - g_first.shape[0], first.shape[0] - 8
    first[...] = jnp.zeros_like(first)
    first[0 : g_first.shape[0], 0:hidden_width] = g_first
    first[g_first.shape[0] :, 0:hidden_width] = g_second[:room]
    first[0 : hidden_width - room, hidden_width:] = g_second[room:]
    for i, grad in enumerate((d_pre1, d_pre2)):
        row = jnp.sum(grad, axis=0, keepdims=True)
        first[tall + i : tall + i + 1, hidden_width:] = row[:, :hidden_width] + row[:, hidden_width:]
    trades = [sems.copy(first, first_in.at[i - 1], {"tensor": place.t_at(i)}) for i in range(1, tensor)]
    for copy in trades:
        copy.start()
    ins[0].combine()

    whole[...] = jnp.zeros_like(whole)
    for copy in trades:
        copy.wait()
    total = first[...]
    for i in range(tensor - 1):
        total = total + first_in[i]
    whole[0 : first.shape[0], :] = total

    def part_of(own_part, d):
        return pl.ds(pl.multiple_of(d * own_part.shape[0], 8), own_part.shape[0])

    groups = ((small, small_in, small_own, small_all), (whole, whole_in, whole_own, whole_all))
    spread = []
    for full, landed, own_part, _ in groups:
        spread.append(
            [
                sems.copy(full.at[part_of(own_part, place.d_at(i)), :], landed.at[i - 1], {"dp": place.d_at(i)})
                for i in range(1, dp)
            ]
        )
        for copy in spread[-1]:
            copy.start()

    loaded("mixed")
    wide[...] = jnp.zeros_like(wide)
    reduce.arrived()
    reduce.finish()

    def back(at):
        grad = reduce.total(keep, at)
        hat = normal[at, :]
        d_input = norm_back(grad, hat, scales[at, 0:1], row_of(gain))
        near_out[0, at, :] = (d_mixed[at, :] + d_input).astype(BF16)
        wide[0:8, :] += fold8(grad * hat)
        wide[8:16, :] += fold8(grad)

    over_rows(count, 64, back)
    mlp_sum = d_mixed
    mlp_loaded = copies.start(mlp_own, mlp_sum)
    late[0:1, :] = jnp.sum(wide[0:8, :], axis=0, keepdims=True)
    late[1:2, :] = jnp.sum(wide[8:16, :], axis=0, keepdims=True)
    row_trades = [sems.copy(late, late_in.at[i - 1], {"tensor": place.t_at(i)}) for i in range(1, tensor)]
    for copy in row_trades:
        copy.start()
    joined = []
    for copies_of, (full, landed, own_part, everyone) in zip(spread, groups, strict=True):
        for copy in copies_of:
            copy.wait_recv()
        total = full[part_of(own_part, place.d), :]
        for i in range(dp - 1):
            total = total + landed[i]
        own_part[...] = total
        everyone[part_of(own_part, place.d), :] = total
        for i in range(1, dp):
            copy = sems.copy(own_part, everyone.at[part_of(own_part, place.d), :], {"dp": place.d_at(i)})
            copy.start()
            joined.append(copy)
    for copy in row_trades:
        copy.wait_recv()
    total = late[...]
    for i in range(tensor - 1):
        total = total + late_in[i]
    late_sum[...] = total
    late_moves = [sems.copy(late_sum, late_far.at[i - 1], {"dp": place.d_at(i)}) for i in range(1, dp)]
    for copy in late_moves:
        copy.start()
    order = order_matrix(count)
    grad_tokens[0] = dot(order, near_out[0]).astype(BF16)
    for copy in mlp:
        copy.wait_recv()
    copies.take(mlp_loaded)
    total = mlp_sum[...]
    for i in range(place.ys - 1):
        total = total + mlp_in[i].astype(F32)
    output[0] = dot(order, total.astype(BF16)).astype(BF16)
    for copy in early_moves:
        copy.wait_recv()
    total = early[...]
    for i in range(dp - 1):
        total = total + early_far[i]
    o_early[...] = total
    loaded("down")
    o_down[...] = far_total(downs, down_keep, down_land)
    o_up[...] = ups.total()
    o_out[...] = outs.total()
    for p in (2, 1, 0):
        o_in[p] = ins[p].total()
    for copy in joined:
        copy.wait_recv()
    o_small[...] = small_all[0 : base + SMALL_ROWS, :]
    o_first[...] = whole_all[0 : first.shape[0], :]
    for copy in late_moves:
        copy.wait_recv()
    total = late_sum[...]
    for i in range(dp - 1):
        total = total + late_far[i]
    o_late[...] = total
    for group in (row_trades, *spread, joined, early_moves, late_moves, mlp, downs):
        for copy in group:
            copy.wait_send()
    for group in (*gathers, ups, outs, *ins):
        group.finish()
    copies.finish()


def finish(
    output_in, tokens_in, down, up, weights, out, small, first, early, late,
    output, grad_tokens, o_mix_gain, o_mix_shift, o_in, o_in_bias, o_taps, o_tap_bias, o_w1, o_b1, o_w2, o_b2, o_w3, o_direct,
    o_out, o_out_bias, o_mlp_gain, o_mlp_shift, o_up, o_up_bias, o_down, o_down_bias,
):
    for src, dst in ((output_in, output), (tokens_in, grad_tokens), (down, o_down), (up, o_up), (out, o_out)):
        dst[...] = src[...]
    for p in range(3):
        o_in[:, p, :] = weights[p]
    model, units = o_mix_gain.shape[0], o_up_bias.shape[0]
    for i, ref in enumerate((o_mix_gain, o_mix_shift)):
        ref[...] = late[i : i + 1, :].reshape(model)
    for i, ref in enumerate((o_mlp_gain, o_mlp_shift, o_out_bias, o_down_bias)):
        ref[...] = early[i : i + 1, 0:model].reshape(model)
    o_up_bias[...] = early[4:5, 0:units].reshape(units)
    hidden_width, emb = o_w2.shape[0], o_w1.shape[0]
    base = 2 * hidden_width
    o_in_bias[...] = small[base + MISC : base + MISC + 3, :]
    o_tap_bias[...] = small[base + MISC + 3 : base + MISC + 6, :]
    o_direct[...] = small[base + MISC + 6 : base + MISC + 8, :]
    for j in range(3):
        o_taps[j] = small[base + TAPS + 3 * j : base + TAPS + 3 * j + 3, :]
    for o in range(2):
        o_w3[:, o, :] = small[o * hidden_width : (o + 1) * hidden_width, :]
    tall = first.shape[0] - 8
    room = hidden_width - tall
    o_w1[...] = first[0:emb, 0:hidden_width]
    o_w2[0:room, :] = first[first.shape[0] - room :, 0:hidden_width]
    o_w2[room:, :] = first[0:tall, hidden_width:]
    for i, ref in enumerate((o_b1, o_b2)):
        ref[...] = first[tall + i : tall + i + 1, hidden_width:].reshape(hidden_width)


def finish_call(args, emb):
    f32 = lambda *shape: jax.ShapeDtypeStruct(shape, F32)
    rows_shape = jax.ShapeDtypeStruct(args[0].shape, BF16)
    model, (rows, units), channels, hidden_width = args[0].shape[2], args[2].shape, args[5].shape[1], args[7].shape[1] // 2
    return pl.pallas_call(
        finish,
        out_shape=[
            rows_shape, rows_shape, f32(model), f32(model), f32(rows, 3, channels), f32(3, channels), f32(3, 3, channels),
            f32(3, channels), f32(emb, hidden_width), f32(hidden_width), f32(hidden_width, hidden_width), f32(hidden_width),
            f32(hidden_width, 2, channels), f32(2, channels), f32(rows, channels), f32(model), f32(model), f32(model),
            f32(rows, units), f32(units), f32(rows, units), f32(model),
        ],
        in_specs=vmem_specs(10),
        out_specs=vmem_specs(22),
        compiler_params=pltpu.CompilerParams(vmem_limit_bytes=VMEM_LIMIT),
        name="finish",
    )(*args)


def rear_call(dp, tensor, args, half):
    S = jax.ShapeDtypeStruct
    _, count, model = args[0].shape
    emb, hidden_width = args[8].shape
    channels, units = args[12].shape[2], args[3].shape[1]
    own, cores, rows_d = count // 2, 2 if tensor % 2 == 0 else 1, 4 if dp % 4 == 0 else 1
    cols_d, ys, rows = dp // rows_d, tensor // cores, model // dp
    farther = max(ys - 1, 1)
    base = 2 * hidden_width
    chunk = -(-(base + SMALL_ROWS) // (8 * dp)) * 8
    packed = (-(-emb // 8) * 8 + hidden_width + 8) // 2
    part = -(-packed // (8 * dp)) * 8
    lanes = 2 * hidden_width
    widest = max(model, units)
    V = pltpu.VMEM
    rows_f = ((count, model), F32)
    norm = ((2, tensor, own, model), BF16)
    far = ((farther, count, model), BF16)

    def buffers(lead, last):
        return [
            V((*lead, cols_d, rows_d, rows, last), BF16), V((*lead, max(cols_d - 1, 1), rows_d, rows, last), BF16), V((*lead, rows, last), F32),
            V((*lead, max(rows_d - 1, 1), rows, last), BF16), V((*lead, max(rows_d - 1, 1), rows, last), BF16),
        ]

    per_t, _ = gather_counts(dp, tensor)
    copies = 2 * per_t + 6 * (rows_d + cols_d) + 4 * ys + 3 * tensor + 6 * dp
    hbm = pl.BlockSpec(memory_space=pl.ANY)
    wave, wave_back = args[26], args[27]
    f32 = lambda *shape: S(shape, F32)
    return pl.pallas_call(
        functools.partial(rear, dp, tensor),
        out_shape=[
            S((1, count, model), BF16), S((1, count, model), BF16), f32(rows, units), f32(rows, units), f32(3, rows, channels),
            f32(rows, channels), f32(base + SMALL_ROWS, channels), f32(packed, lanes), f32(8, widest), f32(2, model),
        ],
        in_specs=vmem_specs(15) + [hbm] * 13 + vmem_specs(4) + [hbm] * 7,
        out_specs=vmem_specs(10),
        scratch_shapes=[
            V(wave.shape, BF16), V(wave_back.shape, BF16), V((2, half + PAD, 8), F32), V((3, 2, half + 2 * PAD, channels), F32),
            V((2, 2 * half, channels), F32), V((2, half // 4, channels), F32), V((2, 2 * half, channels), F32),
            V((2, half // 4, channels), F32), V((2, 2, half, channels), F32), V((half, 2 * hidden_width), F32),
            V(*rows_f), V(*norm), V((2, tensor, own, channels), BF16), V((3, model, channels), BF16), V((model, channels), BF16),
            V(*norm), V(*far), V((cols_d, rows_d, rows, units), BF16),
            V((3, 2, half, channels), F32), V((6 * half, channels), BF16), V((6 * half, channels), BF16),
            V((2, half, channels), F32), V((2, 2, 2 * half, channels), F32), V((2, 2, half // 4, channels), F32),
            V((3, 2, half + PAD, channels), F32), V((3, 2, half, channels), BF16), V((40, channels), F32), V(*rows_f),
            V((count, 128), F32),
        ]
        + [V((rows, units), F32), V((max(rows_d - 1, 1), rows, units), BF16)] + buffers((), units)[1:]
        + buffers((3,), channels) + buffers((), channels)
        + [V((ys, count, model), F32), V((ys, count, model), BF16), V((ys, count, model), BF16), V(*far), V(*far)]
        + [
            V((dp * chunk, channels), F32), V((dp - 1, chunk, channels), F32), V((chunk, channels), F32),
            V((dp * chunk, channels), F32), V((packed, lanes), F32), V((tensor - 1, packed, lanes), F32),
            V((dp * part, lanes), F32), V((dp - 1, part, lanes), F32), V((part, lanes), F32), V((dp * part, lanes), F32),
            V((tensor - 1, 4, model), F32), V((8, widest), F32), V((dp - 1, 8, widest), F32), V((2, model), F32),
            V((tensor - 1, 2, model), F32), V((2, model), F32), V((dp - 1, 2, model), F32), V((16, model), F32),
            pltpu.SemaphoreType.DMA((copies,)), pltpu.SemaphoreType.DMA((copies,)), pltpu.SemaphoreType.DMA((28,)),
        ],
        compiler_params=pltpu.CompilerParams(collective_id=2, has_side_effects=True, vmem_limit_bytes=63 * 2**20),
        name="rear",
    )(*args)


def body(
    tokens,
    segment_ids,
    mix_norm_gain,
    mix_norm_bias,
    in_weight,
    in_bias,
    short_weight,
    short_bias,
    filt_in_weight,
    filt_in_bias,
    filt_mid_weight,
    filt_mid_bias,
    filt_out_weight,
    decay_rates,
    long_bias,
    out_weight,
    out_bias,
    mlp_norm_gain,
    mlp_norm_bias,
    up_weight,
    up_bias,
    down_weight,
    down_bias,
    cotangent,
):
    dp, tensor = lax.axis_size("dp"), lax.axis_size("tensor")
    units = up_weight.shape[1]
    model = tokens.shape[2]
    length, emb, hidden_width = segment_ids.shape[1], filt_in_weight.shape[0], filt_mid_bias.shape[0]
    half = length // 2
    wave, wave_back, *fixed = (jnp.asarray(t) for t in wave_tables(length))
    net = (
        short_weight, short_bias, jnp.asarray(position_table(length, emb)), filt_in_weight, filt_in_bias, filt_mid_weight,
        filt_mid_bias, filt_out_weight, decay_rates, long_bias,
    )
    w_in, out_par, up_par, cot_par, norm_par, gated_par, own_gated, masks, *kept = front_call(
        dp, tensor,
        (tokens, cotangent, segment_ids, mix_norm_gain, mix_norm_bias, in_weight, in_bias) + net
        + (*fixed, out_weight, up_weight, wave, wave_back),
        half, hidden_width,
    )
    out_full = out_par.reshape(tensor, model, -1)
    d_mixed, d_mix_low, mlp_own, mlp_far, *low_grads, row_sums, up_sums = middle_call(
        dp, tensor,
        (tokens, cotangent, own_gated, out_full, out_bias, mlp_norm_gain, mlp_norm_bias, up_bias, down_bias,
         up_par.reshape(model, units), cot_par, down_weight),
    )
    results = rear_call(
            dp, tensor,
            (tokens, d_mix_low, row_sums, up_sums, mix_norm_gain) + net
            + (d_mixed, mlp_own, mlp_far, *low_grads, norm_par, gated_par, w_in, out_full, masks, wave, wave_back, *fixed, *kept),
            half,
        )
    return tuple(finish_call(results, emb))


def solution(mesh):
    placed = (
        P("dp", "tensor", None),
        P("dp", None),
        P(),
        P(),
        P("dp", None, "tensor"),
        P(None, "tensor"),
        P(None, None, "tensor"),
        P(None, "tensor"),
        P(),
        P(),
        P(),
        P(),
        P(None, None, "tensor"),
        P(None, "tensor"),
        P(None, "tensor"),
        P("dp", "tensor"),
        P(),
        P(),
        P(),
        P("dp", "tensor"),
        P("tensor"),
        P("dp", "tensor"),
        P(),
        P("dp", "tensor", None),
    )
    return jax.shard_map(
        body,
        mesh=mesh,
        in_specs=placed,
        out_specs=(
            P("dp", "tensor", None),
            P("dp", "tensor", None),
            P(),
            P(),
            P("dp", None, "tensor"),
            P(None, "tensor"),
            P(None, None, "tensor"),
            P(None, "tensor"),
            P(),
            P(),
            P(),
            P(),
            P(None, None, "tensor"),
            P(None, "tensor"),
            P("dp", "tensor"),
            P(),
            P(),
            P(),
            P("dp", "tensor"),
            P("tensor"),
            P("dp", "tensor"),
            P(),
        ),
        check_vma=False,
    )
```
